128 devices in a mesh: context: 16 (over y, x), tensor: 8 (over z, core).
Axes of the slice: x: 4, y: 4, z: 4, core: 2. Of those that a mesh axis runs over, the one named last changes fastest.
Arguments:
- seq_inputs: bfloat16 [2, 8192, 8192], P(None, 'context', 'tensor'), may hold values from -6 to 6
- b_proj: bfloat16 [2, 8192, 2048], P(None, 'context', 'tensor'), may hold values from -1.796875 to 1.796875
- c_proj: bfloat16 [2, 8192, 2048], P(None, 'context', 'tensor'), may hold values from -1.796875 to 1.796875
- dt_raw: float32 [2, 128, 8192], P(None, 'tensor', 'context'), may hold values from -3 to 3
- dt_bias: float32 [128], P('tensor'), may hold values from -4 to -2
- a_log: float32 [128], P('tensor'), may hold values from -11 to 0
- d_skip: float32 [128], P('tensor'), may hold values from 0.5 to 1.5
- out_grad: bfloat16 [2, 8192, 8192], P(None, 'context', 'tensor'), may hold values from -6 to 6
- log_ratio: float32 [2, 8192], P(None, ('context', 'tensor')), may hold values from -0.15 to 0.15
- lengths: int32 [2], replicated, may hold values from 4096 to 8192, as said below
Outputs:
- grad_inputs: bfloat16 [2, 8192, 8192], P(None, 'context', 'tensor')
- grad_b: bfloat16 [2, 8192, 2048], P(None, 'context', 'tensor')
- grad_c: bfloat16 [2, 8192, 2048], P(None, 'context', 'tensor')
- grad_dt: float32 [2, 128, 8192], P(None, 'tensor', 'context')
- grad_a_log: float32 [128], P('tensor')
- grad_dt_bias: float32 [128], P('tensor')
- grad_skip: float32 [128], P('tensor')
The draws below stay inside these ranges and needn't reach their ends.
Inputs may be any that keep to these rules, and one draw needn't show every extreme that they name: One of the two lengths is 8192, the other at least 4096.
All inputs are finite; a program needn't handle non-finite values.
Results may differ from the reference program's by a relative error of at most 0.0075.
Values sent between devices are 32-bit elements; how exact they have to be, the bound alone decides.
No kernel may reach another device: no remote copies, remote signals or barrier semaphores. Data moves between devices by JAX's collectives and lax.ppermute only.
A program may use at most 256 MiB of HBM per device.

```python
import jax
import jax.numpy as jnp
from jax import lax

H = 128
HP = 64
NS = 256
G = 8
L = 8192
QB = 256


def draw_lengths(key, part):
    key = jax.random.fold_in(key, 11)
    pick_key, span_key = jax.random.split(key)
    full_pick = jax.random.randint(pick_key, (), 0, 2)
    other_len = jax.random.randint(span_key, (), L // 2, L + 1)
    return jnp.where(jnp.arange(2) == full_pick, L, other_len).astype(jnp.int32)


def draw_log_ratio(key, part):
    key = jax.random.fold_in(key, 23)
    ramp_scale = 0.5 + jnp.arange(L, dtype=jnp.float32) / L
    noise_vals = jnp.clip(jax.random.normal(key, (2, L), jnp.float32), -5.0, 5.0)
    return (0.02 * ramp_scale * noise_vals).astype(jnp.float32)


def block_levels(key, extent, cuts, least, top_value):
    def one(axis_at, shards_of):
        heights = jax.random.uniform(jax.random.fold_in(jax.random.fold_in(key, 6), axis_at), (shards_of,), jnp.float32, least / len(cuts), top_value / len(cuts))
        return jnp.repeat(jnp.exp(heights), extent[axis_at] // shards_of).reshape((-1,) + (1,) * (len(extent) - axis_at - 1))

    factor_of = one(*cuts[0])
    for cut in cuts[1:]:
        factor_of = factor_of * one(*cut)
    return factor_of


def bell_draw(key, dims, scale, reach, cuts=(), kind=jnp.bfloat16):
    loudness = block_levels(key, dims, cuts, -0.22, 0.18) if cuts else 1.0
    drawn = jax.random.normal(key, dims, jnp.float32) * scale * loudness
    return jnp.minimum(jnp.maximum(drawn, -reach), reach).astype(kind)


def setup_inputs(seed: int = 0) -> dict:
    streams_of = jax.random.split(jax.random.key(seed), 11)
    seq_inputs = bell_draw(streams_of[0], (2, L, H * HP), 1.0, 6.0, ((1, 16), (2, 8)))
    b_proj = bell_draw(streams_of[1], (2, L, G * NS), 0.3, 1.796875, ((1, 16), (2, 8)))
    c_proj = bell_draw(streams_of[2], (2, L, G * NS), 0.3, 1.796875, ((1, 16), (2, 8)))
    dt_raw = bell_draw(streams_of[3], (2, H, L), 0.5, 3.0, ((1, 8), (2, 16)), jnp.float32)
    dt_bias = jnp.clip(-4.0 + 2.0 * jax.random.uniform(streams_of[4], (H,), jnp.float32) ** block_levels(streams_of[4], (H,), ((0, 8),), -0.2, 0.2), -4.0, -2.0)
    a_log = jnp.clip(-11.0 + 11.0 * jax.random.uniform(streams_of[5], (H,), jnp.float32) ** block_levels(streams_of[5], (H,), ((0, 8),), -0.2, 0.2), -11.0, 0.0)
    d_skip = jnp.clip(0.5 + 1.0 * jax.random.uniform(streams_of[6], (H,), jnp.float32) ** block_levels(streams_of[6], (H,), ((0, 8),), -0.2, 0.2), 0.5, 1.5)
    out_grad = bell_draw(streams_of[7], (2, L, H * HP), 1.0, 6.0, ((1, 16), (2, 8)))
    log_ratio = draw_log_ratio(jax.random.fold_in(streams_of[10], 71), 0)
    lengths = draw_lengths(jax.random.fold_in(streams_of[10], 71), 0)
    return {"seq_inputs": seq_inputs, "b_proj": b_proj, "c_proj": c_proj, "dt_raw": dt_raw, "dt_bias": dt_bias, "a_log": a_log, "d_skip": d_skip, "out_grad": out_grad, "log_ratio": log_ratio, "lengths": lengths}


BETA = 0.5
HIGH = lax.Precision.HIGHEST

def to_heads(values, num_groups):
    seq_count, tok_rows, head_count = values.shape
    shaped = values.reshape(seq_count, tok_rows, num_groups, head_count // num_groups)
    return jnp.transpose(shaped, (0, 2, 3, 1))

def from_heads(values):
    return jnp.transpose(values, (0, 3, 1, 2))[..., None]

def block_step(decay_rates, skip_gain, carry_state, inputs):
    x_block, b_block, c_block, step_block = inputs
    seq_count, tok_rows, row_width = x_block.shape
    num_groups = b_block.shape[-1] // NS
    per_group = decay_rates.shape[0] // num_groups
    x_five = x_block.reshape(seq_count, tok_rows, num_groups, per_group, HP)
    b_four = b_block.reshape(seq_count, tok_rows, num_groups, NS)
    c_four = c_block.reshape(seq_count, tok_rows, num_groups, NS)
    running = jnp.cumsum(to_heads(step_block * decay_rates, num_groups), axis=-1)
    step_heads = to_heads(step_block, num_groups)
    causal = jnp.arange(tok_rows)[:, None] >= jnp.arange(tok_rows)[None, :]
    spread = jnp.where(causal, running[..., :, None] - running[..., None, :], -jnp.inf)
    c_half = c_four.astype(jnp.bfloat16).astype(jnp.float32)
    b_half = b_four.astype(jnp.bfloat16).astype(jnp.float32)
    gram_block = jnp.einsum('sqgn,skgn->sgqk', c_half, b_half, precision=HIGH)
    weights = (gram_block[:, :, None] * jnp.exp(spread) * step_heads[..., None, :]).astype(jnp.bfloat16)
    x_half = x_five.astype(jnp.bfloat16).astype(jnp.float32)
    intra_out = jnp.einsum('sgjqk,skgjp->sqgjp', weights.astype(jnp.float32), x_half, precision=HIGH)
    carried = jnp.einsum('sqgn,sgjpn->sqgjp', c_four, carry_state, precision=HIGH) * from_heads(jnp.exp(running))
    outputs = intra_out + carried + skip_gain.reshape(num_groups, per_group, 1) * x_five
    tail_decay = jnp.exp(running[..., -1:] - running) * step_heads
    fresh_state = jnp.einsum('sqgjp,sqgn->sgjpn', x_five * from_heads(tail_decay), b_four, precision=HIGH)
    carry_state = jnp.exp(running[..., -1])[..., None, None] * carry_state + fresh_state
    return (carry_state, outputs.reshape(seq_count, tok_rows, row_width))

def scan_blocks(x_in, b_in, c_in, step_raw, bias_in, log_rate, skip_in, init_state):
    step_size = jax.nn.softplus(step_raw + bias_in)
    decay_rates = -jnp.exp(log_rate)
    seq_count, tok_rows, row_width = x_in.shape
    num_blocks = tok_rows // QB

    def to_blocks(array_in):
        return jnp.swapaxes(array_in.reshape((seq_count, num_blocks, QB) + array_in.shape[2:]), 0, 1)

    def block_fn(carry_state, inputs):
        return block_step(decay_rates, skip_in, carry_state, inputs)
    final_state, outputs = lax.scan(jax.checkpoint(block_fn), init_state, (to_blocks(x_in), to_blocks(b_in), to_blocks(c_in), to_blocks(step_size)))
    return (jnp.swapaxes(outputs, 0, 1).reshape(seq_count, tok_rows, row_width), final_state)

def reference(seq_inputs, b_proj, c_proj, dt_raw, dt_bias, a_log, d_skip, out_grad, log_ratio, lengths):
    positions = jnp.arange(L, dtype=jnp.int32)
    live_mask = (positions[None, :] < lengths[:, None]).astype(jnp.float32)
    totals = lax.optimization_barrier(jnp.sum(live_mask * log_ratio, axis=1))
    seq_signs = jnp.where(jnp.arange(2, dtype=jnp.int32) == 0, -1.0, 1.0).astype(jnp.float32)
    margin = -jnp.sum(seq_signs * totals)
    seq_gate = seq_signs * BETA * jax.nn.sigmoid(-BETA * margin)
    per_group = H // G

    def group_grads(pieces):
        x_part, b_part, c_part, step_part, bias_part, rate_part, skip_part, grad_part = pieces
        cotangent = seq_gate[:, None, None] * live_mask[:, :, None] * grad_part.astype(jnp.float32)
        init_state = jnp.zeros((2, 1, per_group, HP, NS), jnp.float32)

        def forward(x_in, b_in, c_in, step_raw, bias_in, log_rate, skip_in):
            return scan_blocks(x_in, b_in, c_in, step_raw, bias_in, log_rate, skip_in, init_state)[0]
        _, pull_fn = jax.vjp(forward, x_part.astype(jnp.float32), b_part.astype(jnp.float32), c_part.astype(jnp.float32), step_part, bias_part, rate_part, skip_part)
        return pull_fn(cotangent)

    def by_group(array_in, piece_width):
        return jnp.moveaxis(array_in.reshape(array_in.shape[:-1] + (G, piece_width)), -2, 0)
    pieces = (by_group(seq_inputs, per_group * HP), by_group(b_proj, NS), by_group(c_proj, NS), by_group(jnp.swapaxes(dt_raw, 1, 2), per_group), dt_bias.reshape(G, per_group), a_log.reshape(G, per_group), d_skip.reshape(G, per_group), by_group(out_grad, per_group * HP))
    g_inputs, g_bproj, g_cproj, g_steps, g_bias, g_rate, g_skip = lax.map(group_grads, pieces)

    def join_group(array_in):
        moved = jnp.moveaxis(array_in, 0, -2)
        return moved.reshape(moved.shape[:-2] + (moved.shape[-2] * moved.shape[-1],))
    return (join_group(g_inputs).astype(jnp.bfloat16), join_group(g_bproj).astype(jnp.bfloat16), join_group(g_cproj).astype(jnp.bfloat16), jnp.swapaxes(join_group(g_steps), 1, 2), g_rate.reshape(H), g_bias.reshape(H), g_skip.reshape(H))
```

```python
import functools

import jax
import jax.numpy as jnp
from jax import lax
from jax.experimental import pallas as pl
from jax.experimental.pallas import tpu as pltpu
from jax.sharding import PartitionSpec as P

HP = 64
NS = 256
QB = 256
HALF = 128
BETA = 0.5
VMEM = 56 * 1024 * 1024
F32 = jnp.float32
BF16 = jnp.bfloat16
HIGH = lax.Precision.HIGHEST


def dot(lhs, rhs, dims, precision=None):
    return lax.dot_general(
        lhs, rhs, (dims, ((), ())), precision=precision, preferred_element_type=F32
    )


NN = ((1,), (0,))
NT = ((1,), (1,))
TN = ((0,), (0,))


def split3(value):
    top = value.astype(BF16)
    rest = value - top.astype(F32)
    mid = rest.astype(BF16)
    return top, mid, (rest - mid.astype(F32)).astype(BF16)


def spread_matrix(heads):
    row = lax.broadcasted_iota(jnp.int32, (3 * heads, heads * HP), 0)
    lane = lax.broadcasted_iota(jnp.int32, (3 * heads, heads * HP), 1)
    return (lax.rem(row, heads) == lax.div(lane, HP)).astype(BF16)


def spread(values, ones_rows):
    return dot(jnp.concatenate(split3(values), axis=0), ones_rows, TN)


def head_sums(product, ones_rows, heads):
    top = product.astype(BF16)
    low = (product - top.astype(F32)).astype(BF16)
    ones = ones_rows[:heads]
    return dot(ones, top, NT) + dot(ones, low, NT)


def softplus(value):
    return jnp.maximum(value, 0.0) + jnp.log1p(jnp.exp(-jnp.abs(value)))


def upper_ones():
    row = lax.broadcasted_iota(jnp.int32, (QB, QB), 0)
    col = lax.broadcasted_iota(jnp.int32, (QB, QB), 1)
    return (row <= col).astype(F32)


def running_sum(values, ones_upper):
    return dot(values, ones_upper, NN, HIGH)


def live_rows(base, length, count):
    row = lax.broadcasted_iota(jnp.int32, (count, 1), 0)
    return base + row < length


def states_kernel(info, x_ref, g_ref, b_ref, c_ref, dt_ref, bias_ref, alog_ref,
                  out_ref, first_ref, last_ref):
    heads = dt_ref.shape[1]
    seq = pl.program_id(0)
    ones_rows = spread_matrix(heads)
    ones_upper = upper_ones()
    step = softplus(dt_ref[0] + bias_ref[...])
    logs = step * -jnp.exp(alog_ref[...])
    fresh, pulls, ends = [], [], []
    for blk in range(2):
        rows = slice(blk * QB, (blk + 1) * QB)
        cum = running_sum(logs[:, rows], ones_upper)
        cum_last = cum[:, QB - 1 : QB]
        tail = spread(jnp.exp(cum_last - cum) * step[:, rows], ones_rows)
        grow = spread(jnp.exp(cum), ones_rows)
        ends.append(grow[QB - 1 : QB])
        x_tail = (x_ref[0, rows].astype(F32) * tail).astype(BF16)
        fresh.append(dot(b_ref[0, rows], x_tail, TN))
        live = live_rows(info[0] + blk * QB, info[1 + seq], QB)
        g_grow = jnp.where(live, g_ref[0, rows].astype(F32) * grow, 0.0).astype(BF16)
        pulls.append(dot(c_ref[0, rows], g_grow, TN))
    first_ref[0] = fresh[0]
    last_ref[0] = pulls[1]
    pieces, lanes = out_ref.shape[0], out_ref.shape[-1]
    out_ref[:, 0, 0] = (ends[1] * fresh[0] + fresh[1]).reshape(pieces, -1, lanes)
    out_ref[:, 1, 0] = (pulls[0] + ends[0] * pulls[1]).reshape(pieces, -1, lanes)


def chain_kernel(decay_ref, in_ref, out_ref):
    count = in_ref.shape[0]

    @pl.when(pl.program_id(0) == 0)
    def _():
        total = jnp.zeros(in_ref.shape[3:], F32)
        for at in range(count):
            out_ref[at, 0, 0] = total
            total = decay_ref[at] * total + in_ref[at, 0, 0]

    @pl.when(pl.program_id(0) == 1)
    def _():
        total = jnp.zeros(in_ref.shape[3:], F32)
        for at in reversed(range(count)):
            out_ref[at, 0, 0] = total
            total = decay_ref[at] * total + in_ref[at, 0, 0]


def intra_kernel(info, x_ref, g_ref, b_ref, c_ref, dt_ref, bias_ref, alog_ref,
                 dx_ref, db_ref, dc_ref, diff_ref, col_ref, skip_ref,
                 y_sc, d_sc, xs_sc, g_sc):
    heads = dt_ref.shape[1]
    seq, blk = pl.program_id(0), pl.program_id(1)
    ones_rows = spread_matrix(heads)
    step = softplus(dt_ref[0] + bias_ref[...])
    cum = running_sum(step * -jnp.exp(alog_ref[...]), upper_ones())
    cum_t = cum.T
    live = live_rows(info[0] + blk * QB, info[1 + seq], QB)
    x_full = x_ref[0].astype(F32)
    g_full = jnp.where(live, g_ref[0].astype(F32), 0.0)
    g_sc[...] = g_full.astype(BF16)
    step_rows = spread(step, ones_rows)
    xs_full = x_full * step_rows
    xs_sc[...] = xs_full.astype(BF16)
    skip_ref[0, 0] = jnp.sum(x_full * g_full, axis=0, keepdims=True)
    gram = dot(c_ref[0], b_ref[0], NT)
    mid = cum[:, HALF - 1 : HALF]
    early = spread(jnp.exp(mid - cum[:, :HALF]), ones_rows)
    late = spread(jnp.exp(cum[:, HALF:] - mid), ones_rows)
    x_early = (xs_sc[:HALF].astype(F32) * early).astype(BF16)
    g_late = (g_full[HALF:] * late).astype(BF16)
    gram_low = gram[HALF:, :HALF].astype(BF16)
    y_low = dot(gram_low, x_early, NN)
    dx_low = dot(gram_low, g_late, TN)
    dgram_low = dot(g_late, x_early, NT)
    row_low = head_sums(g_late.astype(F32) * y_low, ones_rows, heads)
    col_low = head_sums(x_early.astype(F32) * dx_low, ones_rows, heads)
    causal = (
        lax.broadcasted_iota(jnp.int32, (HALF, HALF), 0)
        >= lax.broadcasted_iota(jnp.int32, (HALF, HALF), 1)
    )
    left = lax.broadcasted_iota(jnp.int32, (HALF, 2 * HP), 1) < HP
    zero = jnp.zeros((HALF, 2 * HP), BF16)
    dgrams = []
    for half in range(2):
        rows = slice(half * HALF, (half + 1) * HALF)
        gram_here = jnp.where(causal, gram[rows, rows], 0.0)
        dgram = jnp.zeros((HALF, HALF), F32)
        for pair in range(heads // 2):
            lanes = slice(pair * 2 * HP, (pair + 1) * 2 * HP)
            xs = xs_sc[rows, lanes]
            gg = g_sc[rows, lanes]
            g_two = jnp.concatenate([jnp.where(left, gg, zero), jnp.where(left, zero, gg)], axis=0)
            x_two = jnp.concatenate([jnp.where(left, xs, zero), jnp.where(left, zero, xs)], axis=0)
            dweights = dot(g_two, xs, NT)
            weights = []
            for one in range(2):
                head = 2 * pair + one
                decay = jnp.exp(
                    jnp.minimum(cum_t[rows, head : head + 1] - cum[head : head + 1, rows], 0.0)
                )
                weights.append((gram_here * decay).astype(BF16))
                dgram = dgram + dweights[one * HALF : (one + 1) * HALF] * decay
            y_sc[rows, lanes] = dot(jnp.concatenate(weights, axis=1), x_two, NN)
            d_sc[rows, lanes] = dot(jnp.concatenate(weights, axis=0), g_two, TN)
        dgrams.append(jnp.where(causal, dgram, 0.0))
    row = head_sums(g_full * y_sc[...], ones_rows, heads)
    col = head_sums(xs_sc[...].astype(F32) * d_sc[...], ones_rows, heads)
    none = jnp.zeros((heads, HALF), F32)
    row = row + jnp.concatenate([none, row_low], axis=1)
    col = col + jnp.concatenate([col_low, none], axis=1)
    diff_ref[0] = row - col
    col_ref[0] = col
    dx_ref[0, :HALF] = step_rows[:HALF] * (d_sc[:HALF] + early * dx_low)
    dx_ref[0, HALF:] = step_rows[HALF:] * d_sc[HALF:]
    dgram = jnp.concatenate(
        [
            jnp.concatenate([dgrams[0], jnp.zeros((HALF, HALF), F32)], axis=1),
            jnp.concatenate([dgram_low, dgrams[1]], axis=1),
        ],
        axis=0,
    ).astype(BF16)
    dc_ref[0] = dot(dgram, b_ref[0], NN)
    db_ref[0] = dot(dgram, c_ref[0], TN)


def final_kernel(info, gate_ref, x_ref, g_ref, b_ref, c_ref, dt_ref, bias_ref, alog_ref, skip_ref,
                 enter_ref, leave_ref, first_ref, last_ref, dxi_ref, dbi_ref, dci_ref,
                 diff_ref, col_ref,
                 dx_ref, db_ref, dc_ref, ddt_ref, par_ref):
    heads = dt_ref.shape[1]
    width = heads * HP
    seq = pl.program_id(0)
    gate = gate_ref[seq]
    ones_rows = spread_matrix(heads)
    ones_upper = upper_ones()
    raw = dt_ref[0] + bias_ref[...]
    step = softplus(raw)
    rate = -jnp.exp(alog_ref[...])
    logs = step * rate
    skip_row = spread(jnp.broadcast_to(skip_ref[...], (heads, 8)), ones_rows)[0:1]
    enter = enter_ref[:, 0, 0].reshape(NS, width)
    leave = leave_ref[:, 0, 0].reshape(NS, width)
    cums = [running_sum(logs[:, b * QB : (b + 1) * QB], ones_upper) for b in range(2)]
    grows = [spread(jnp.exp(cum), ones_rows) for cum in cums]
    ends = [grow[QB - 1 : QB] for grow in grows]
    states = [enter, ends[0] * enter + first_ref[0]]
    dstates = [ends[1] * leave + last_ref[0], leave]
    ga = jnp.zeros((heads, 1), F32)
    gb = jnp.zeros((heads, 1), F32)
    for blk in range(2):
        rows = slice(blk * QB, (blk + 1) * QB)
        cum = cums[blk]
        state = states[blk].astype(BF16)
        dstate = dstates[blk].astype(BF16)
        live = live_rows(info[0] + blk * QB, info[1 + seq], QB)
        g_full = jnp.where(live, g_ref[0, rows].astype(F32), 0.0)
        g_grow = g_full * grows[blk]
        y = dot(c_ref[0, rows], state, NN)
        row = head_sums(g_grow * y, ones_rows, heads)
        dc = dot(g_grow.astype(BF16), state, NT)
        tail = spread(jnp.exp(cum[:, QB - 1 : QB] - cum) * step[:, rows], ones_rows)
        u = tail * dot(b_ref[0, rows], dstate, NN)
        x_full = x_ref[0, rows].astype(F32)
        col = head_sums(x_full * u, ones_rows, heads)
        db = dot((x_full * tail).astype(BF16), dstate, NT)
        dx_ref[0, rows] = (gate * (dxi_ref[0, rows] + u + skip_row * g_full)).astype(BF16)
        dc_ref[0, rows] = (gate * (dci_ref[0, rows] + dc)).astype(BF16)
        db_ref[0, rows] = (gate * (dbi_ref[0, rows] + db)).astype(BF16)
        through = jnp.sum(states[blk] * dstates[blk], axis=0, keepdims=True) * ends[blk]
        through = head_sums(jnp.broadcast_to(through, (8, width)), ones_rows, heads)[:, 0:1]
        both = diff_ref[0, :, rows] + row
        later = dot(both, ones_upper, NT, HIGH)
        earlier = dot(col, ones_upper, NN, HIGH) - col
        dlogs = later + earlier + through
        step_here = step[:, rows]
        dstep = (col_ref[0, :, rows] + col) / step_here + rate * dlogs
        ddt = gate * dstep * jax.nn.sigmoid(raw[:, rows])
        ddt_ref[0, :, rows] = ddt
        gb = gb + jnp.sum(ddt, axis=1, keepdims=True)
        ga = ga + gate * rate * jnp.sum(step_here * dlogs, axis=1, keepdims=True)
    par_ref[0, 0] = jnp.broadcast_to(ga, (heads, 128))
    par_ref[0, 1] = jnp.broadcast_to(gb, (heads, 128))


def on_device(
    seq_inputs, b_proj, c_proj, dt_raw, dt_bias, a_log, d_skip, out_grad, log_ratio, lengths
):
    seqs, toks, width = seq_inputs.shape
    heads = dt_bias.shape[0]
    count = lax.axis_size("context")
    ratio_rows = log_ratio.shape[1]
    ratio_pos = lax.axis_index(("context", "tensor")) * ratio_rows + jnp.arange(
        ratio_rows, dtype=jnp.int32
    )
    ratio_live = (ratio_pos[None, :] < lengths[:, None]).astype(F32)
    totals = lax.psum(jnp.sum(ratio_live * log_ratio, axis=1), ("context", "tensor"))
    signs = jnp.where(jnp.arange(2, dtype=jnp.int32) == 0, -1.0, 1.0).astype(F32)
    margin = -jnp.sum(signs * totals)
    gate = signs * BETA * jax.nn.sigmoid(-BETA * margin)
    info = jnp.concatenate(
        [(lax.axis_index("context") * toks).astype(jnp.int32)[None], lengths]
    )
    bias_col = dt_bias[:, None]
    alog_col = a_log[:, None]
    logs = jnp.sum(
        jax.nn.softplus(dt_raw + dt_bias[None, :, None]) * -jnp.exp(a_log)[None, :, None], axis=2
    )
    decays = jnp.exp(lax.all_gather(logs, "context"))
    decays = jnp.repeat(decays, HP, axis=2)[:, :, None, :]

    smem = pl.BlockSpec(memory_space=pltpu.SMEM)
    params = pltpu.CompilerParams(vmem_limit_bytes=VMEM)
    per_seq = lambda *shape: pl.BlockSpec((1,) + shape, lambda s: (s,) + (0,) * len(shape))
    whole = lambda *shape: pl.BlockSpec(shape, lambda *at: (0,) * len(shape))
    piece = NS // count
    seq_specs = [
        per_seq(toks, width), per_seq(toks, width), per_seq(toks, NS), per_seq(toks, NS),
        per_seq(heads, toks), whole(heads, 1), whole(heads, 1),
    ]
    local, first, last = pl.pallas_call(
        states_kernel,
        grid=(seqs,),
        in_specs=[smem] + seq_specs,
        out_specs=[
            pl.BlockSpec((count, 2, 1, piece, width), lambda s: (0, 0, s, 0, 0)),
            per_seq(NS, width), per_seq(NS, width),
        ],
        out_shape=[
            jax.ShapeDtypeStruct((count, 2, seqs, piece, width), F32),
            jax.ShapeDtypeStruct((seqs, NS, width), F32),
            jax.ShapeDtypeStruct((seqs, NS, width), F32),
        ],
        compiler_params=params,
        name="states",
    )(info, seq_inputs, out_grad, b_proj, c_proj, dt_raw, bias_col, alog_col)

    gathered = lax.all_to_all(local, "context", 0, 0)
    chained = pl.pallas_call(
        chain_kernel,
        grid=(2, seqs),
        in_specs=[
            pl.BlockSpec((count, None, 1, width), lambda k, s: (0, s, 0, 0)),
            pl.BlockSpec((count, 1, 1, piece, width), lambda k, s: (0, k, s, 0, 0)),
        ],
        out_specs=pl.BlockSpec((count, 1, 1, piece, width), lambda k, s: (0, k, s, 0, 0)),
        out_shape=jax.ShapeDtypeStruct((count, 2, seqs, piece, width), F32),
        compiler_params=params,
        name="chain",
    )(decays, gathered)
    entering = lax.all_to_all(chained, "context", 0, 0)

    tok_spec = lambda w: pl.BlockSpec((1, QB, w), lambda s, b: (s, b, 0))
    head_spec = pl.BlockSpec((1, heads, QB), lambda s, b: (s, 0, b))
    blocks = toks // QB
    dxi, dbi, dci, diff, col, skips = pl.pallas_call(
        intra_kernel,
        grid=(seqs, blocks),
        in_specs=[smem, tok_spec(width), tok_spec(width), tok_spec(NS), tok_spec(NS),
                  head_spec, whole(heads, 1), whole(heads, 1)],
        out_specs=[tok_spec(width), tok_spec(NS), tok_spec(NS), head_spec, head_spec,
                   pl.BlockSpec((1, 1, 1, width), lambda s, b: (s, b, 0, 0))],
        out_shape=[
            jax.ShapeDtypeStruct((seqs, toks, width), F32),
            jax.ShapeDtypeStruct((seqs, toks, NS), F32),
            jax.ShapeDtypeStruct((seqs, toks, NS), F32),
            jax.ShapeDtypeStruct((seqs, heads, toks), F32),
            jax.ShapeDtypeStruct((seqs, heads, toks), F32),
            jax.ShapeDtypeStruct((seqs, blocks, 1, width), F32),
        ],
        scratch_shapes=[
            pltpu.VMEM((QB, width), F32), pltpu.VMEM((QB, width), F32),
            pltpu.VMEM((QB, width), BF16), pltpu.VMEM((QB, width), BF16),
        ],
        compiler_params=params,
        name="intra",
    )(info, seq_inputs, out_grad, b_proj, c_proj, dt_raw, bias_col, alog_col)

    state_spec = lambda k: pl.BlockSpec((count, 1, 1, piece, width), lambda s: (0, k, s, 0, 0))
    dx, db, dc, ddt, pars = pl.pallas_call(
        final_kernel,
        grid=(seqs,),
        in_specs=[smem, smem] + seq_specs + [
            whole(heads, 1), state_spec(0), state_spec(1), per_seq(NS, width), per_seq(NS, width),
            per_seq(toks, width), per_seq(toks, NS), per_seq(toks, NS),
            per_seq(heads, toks), per_seq(heads, toks),
        ],
        out_specs=[per_seq(toks, width), per_seq(toks, NS), per_seq(toks, NS),
                   per_seq(heads, toks), per_seq(2, heads, 128)],
        out_shape=[
            jax.ShapeDtypeStruct((seqs, toks, width), BF16),
            jax.ShapeDtypeStruct((seqs, toks, NS), BF16),
            jax.ShapeDtypeStruct((seqs, toks, NS), BF16),
            jax.ShapeDtypeStruct((seqs, heads, toks), F32),
            jax.ShapeDtypeStruct((seqs, 2, heads, 128), F32),
        ],
        compiler_params=params,
        name="final",
    )(info, gate, seq_inputs, out_grad, b_proj, c_proj, dt_raw, bias_col, alog_col,
      d_skip[:, None], entering, entering, first, last, dxi, dbi, dci, diff, col)
    skip_part = jnp.sum(
        gate[:, None] * jnp.sum(skips.reshape(seqs, blocks, heads, HP), axis=(1, 3)), axis=0
    )
    sums = lax.psum(
        jnp.concatenate([jnp.sum(pars[:, :, :, 0], axis=0), skip_part[None]], axis=0), "context"
    )
    return dx, db, dc, ddt, sums[0], sums[1], sums[2]


def solution(mesh):
    return jax.shard_map(
        on_device,
        mesh=mesh,
        in_specs=(
            P(None, "context", "tensor"),
            P(None, "context", "tensor"),
            P(None, "context", "tensor"),
            P(None, "tensor", "context"),
            P("tensor"),
            P("tensor"),
            P("tensor"),
            P(None, "context", "tensor"),
            P(None, ("context", "tensor")),
            P(),
        ),
        out_specs=(
            P(None, "context", "tensor"),
            P(None, "context", "tensor"),
            P(None, "context", "tensor"),
            P(None, "tensor", "context"),
            P("tensor"),
            P("tensor"),
            P("tensor"),
        ),
        check_vma=False,
    )
```

```python
import jax
import jax.numpy as jnp
from jax import lax
from jax.experimental import pallas as pl
from jax.experimental.pallas import tpu as pltpu
from jax.sharding import PartitionSpec as P

HP = 64
NS = 256
QB = 256
HALF = 128
BETA = 0.5
PAIR = 2 * HP
LANES = 8 * HP
TILE = 8
VMEM = 56 * 1024 * 1024
F32 = jnp.float32
BF16 = jnp.bfloat16
HIGH = lax.Precision.HIGHEST


def dot(lhs, rhs, dims, precision=None):
    return lax.dot_general(
        lhs, rhs, (dims, ((), ())), precision=precision, preferred_element_type=F32
    )


NN = ((1,), (0,))
NT = ((1,), (1,))
TN = ((0,), (0,))


def split3(value):
    top = value.astype(BF16)
    rest = value - top.astype(F32)
    mid = rest.astype(BF16)
    return top, mid, (rest - mid.astype(F32)).astype(BF16)


def spread_matrix(heads):
    row = lax.broadcasted_iota(jnp.int32, (3 * heads, heads * HP), 0)
    lane = lax.broadcasted_iota(jnp.int32, (3 * heads, heads * HP), 1)
    return (lax.rem(row, heads) == lax.div(lane, HP)).astype(BF16)


def spread(values, ones_rows):
    return dot(jnp.concatenate(split3(values), axis=0), ones_rows, TN)


def head_sums(product, ones_rows, heads):
    top = product.astype(BF16)
    low = (product - top.astype(F32)).astype(BF16)
    ones = ones_rows[:heads]
    return dot(ones, top, NT) + dot(ones, low, NT)


def softplus(value):
    return jnp.maximum(value, 0.0) + jnp.log1p(jnp.exp(-jnp.abs(value)))


def upper_ones():
    row = lax.broadcasted_iota(jnp.int32, (QB, QB), 0)
    col = lax.broadcasted_iota(jnp.int32, (QB, QB), 1)
    return (row <= col).astype(F32)


def running_sum(values, ones_upper):
    return dot(values, ones_upper, NN, HIGH)


def live_rows(base, length, count):
    row = lax.broadcasted_iota(jnp.int32, (count, 1), 0)
    return base + row < length


def column(row_ref):
    heads = row_ref.shape[1]
    same = lax.broadcasted_iota(jnp.int32, (heads, heads), 0) == lax.broadcasted_iota(
        jnp.int32, (heads, heads), 1
    )
    return jnp.sum(jnp.where(same, row_ref[...], 0.0), axis=1, keepdims=True)


def token_base(toks):
    return lax.axis_index("context") * toks


def flat(column_values, lanes):
    heads = column_values.shape[0]
    same = lax.broadcasted_iota(jnp.int32, (heads, lanes), 0) == lax.broadcasted_iota(
        jnp.int32, (heads, lanes), 1
    )
    return jnp.sum(jnp.where(same, column_values, 0.0), axis=0, keepdims=True)


def scale_columns(tail, grow):
    rows = jnp.concatenate([tail, grow, jnp.zeros((128 - 2 * tail.shape[0], tail.shape[1]), F32)], axis=0)
    return jnp.concatenate(split3(rows.T), axis=1)


def spread_part(heads, first, lane0, lanes):
    row = lax.rem(lax.broadcasted_iota(jnp.int32, (3 * 128, lanes), 0), 128)
    lane = lax.broadcasted_iota(jnp.int32, (3 * 128, lanes), 1) + lane0
    return (row - first == lax.div(lane, HP)).astype(BF16)


def lane_sums(product, ones_part):
    top = product.astype(BF16)
    low = (product - top.astype(F32)).astype(BF16)
    return dot(top, ones_part, NT) + dot(low, ones_part, NT)


def sum_part(heads, lane0, lanes):
    row = lax.broadcasted_iota(jnp.int32, (128, lanes), 0)
    lane = lax.broadcasted_iota(jnp.int32, (128, lanes), 1) + lane0
    return (row == lax.div(lane, HP)).astype(BF16)


def exact_dot(lhs, rhs, dims):
    top = rhs.astype(BF16)
    low = (rhs - top.astype(F32)).astype(BF16)
    return dot(lhs, top, dims) + dot(lhs, low, dims)


def states_kernel(len_ref, x_ref, g_ref, b_ref, c_ref, dt_ref, bias_ref, alog_ref, ratio_ref,
                  out_ref, first_ref, last_ref, turned_sc, scal_sc, tile_sc):
    heads = dt_ref.shape[1]
    toks = x_ref.shape[1]
    pieces = out_ref.shape[0]
    piece = NS // pieces
    at = pl.program_id(0)
    parts = heads * HP // LANES
    work = 2 * parts

    @pl.when(at < work)
    def _():
        seq, part = lax.div(at, parts), lax.rem(at, parts)

        @pl.when(part == 0)
        def _():
            ones_upper = upper_ones()
            step = softplus(dt_ref[0] + column(bias_ref))
            logs = step * -jnp.exp(column(alog_ref))
            total = jnp.zeros((heads, 1), F32)
            for blk in range(2):
                rows = slice(blk * QB, (blk + 1) * QB)
                cum = running_sum(logs[:, rows], ones_upper)
                last = cum[:, QB - 1 : QB]
                total = total + last
                scal_sc[blk] = scale_columns(jnp.exp(last - cum) * step[:, rows], jnp.exp(cum))
                turned_sc[blk] = b_ref[0, rows].astype(F32).T.astype(BF16)
                turned_sc[2 + blk] = c_ref[0, rows].astype(F32).T.astype(BF16)
            tile_sc[pl.ds(seq, 1)] = flat(jnp.exp(total), 128)

        tail_part = spread_part(heads, 0, part * LANES, LANES)
        grow_part = spread_part(heads, heads, part * LANES, LANES)
        fresh, pulls, ends = [], [], []
        for blk in range(2):
            rows = slice(blk * QB, (blk + 1) * QB)
            tail = dot(scal_sc[blk], tail_part, NN)
            grow = dot(scal_sc[blk], grow_part, NN)
            ends.append(grow[QB - 1 : QB])
            x_tail = (x_ref[0, rows].astype(F32) * tail).astype(BF16)
            fresh.append(dot(turned_sc[blk], x_tail, NN))
            live = live_rows(token_base(toks) + blk * QB, len_ref[seq], QB)
            g_grow = jnp.where(live, g_ref[0, rows].astype(F32) * grow, 0.0).astype(BF16)
            pulls.append(dot(turned_sc[2 + blk], g_grow, NN))
        first_ref[0] = fresh[0]
        last_ref[0] = pulls[1]
        whole = (ends[1] * fresh[0] + fresh[1], pulls[0] + ends[0] * pulls[1])
        for scan in range(2):
            for pair in range(LANES // PAIR):
                row = (scan * (LANES // PAIR) + pair) * piece
                out_ref[:, row : row + piece] = whole[scan][:, pair * PAIR : (pair + 1) * PAIR].reshape(
                    pieces, piece, PAIR
                )

    @pl.when(at == work)
    def _():
        ratio = ratio_ref[...]
        rows = ratio.shape[1]
        first = lax.axis_index(("context", "tensor")) * rows
        place = lax.broadcasted_iota(jnp.int32, ratio.shape, 1) + first
        seq = lax.broadcasted_iota(jnp.int32, ratio.shape, 0)
        length = jnp.where(seq == 0, len_ref[0], len_ref[1])
        totals = jnp.sum(jnp.where(place < length, ratio, 0.0), axis=1, keepdims=True)
        tile_sc[2:4] = jnp.broadcast_to(totals, (2, 128))
        tile_sc[4:] = jnp.zeros((TILE - 4, 128), F32)
        out_ref[:, 0:TILE] = jnp.broadcast_to(tile_sc[...][None], (pieces, TILE, 128))


def chain_kernel(seq, heads, tile_ref, in_ref, out_ref, sums_ref, decay_sc):
    count = in_ref.shape[0]
    piece = NS // count
    part = pl.program_id(0)

    @pl.when(part == 0)
    def _():
        tiles = [tile_ref[at] for at in range(count)]
        sums_ref[...] = sum(tiles[1:], tiles[0])
        decay = jnp.concatenate([tile[seq : seq + 1] for tile in tiles], axis=0)
        columns = jnp.concatenate(split3(decay), axis=1)
        wide = dot(columns, spread_part(heads, 0, 0, heads * HP), NN)
        for pair in range(heads // 2):
            decay_sc[pair] = wide[:, pair * PAIR : (pair + 1) * PAIR]

    pairs = LANES // PAIR
    for pair in range(pairs):
        decay = decay_sc[part * pairs + pair]
        rows = slice(pair * piece, (pair + 1) * piece)
        total = jnp.zeros((piece, PAIR), F32)
        for at in range(count):
            out_ref[at, rows] = total
            total = decay[at : at + 1] * total + in_ref[at, rows]
        rows = slice((pairs + pair) * piece, (pairs + pair + 1) * piece)
        total = jnp.zeros((piece, PAIR), F32)
        for at in reversed(range(count)):
            out_ref[at, rows] = total
            total = decay[at : at + 1] * total + in_ref[at, rows]


def intra_kernel(len_ref, x_ref, g_ref, b_ref, c_ref, dt_ref, bias_ref, alog_ref, gain_ref,
                 dx_ref, db_ref, dc_ref, diff_ref, col_ref, skip_ref, xv_ref, gg_ref, scal_ref,
                 y_sc, d_sc, g_sc):
    heads = dt_ref.shape[1]
    seq, blk = pl.program_id(0), pl.program_id(1)
    ones_rows = spread_matrix(heads)
    step = softplus(dt_ref[0] + column(bias_ref))
    cum = running_sum(step * -jnp.exp(column(alog_ref)), upper_ones())
    cum_t = cum.T
    live = live_rows(token_base(pl.num_programs(1) * QB) + blk * QB, len_ref[seq], QB)
    x_full = x_ref[0].astype(F32)
    g_full = jnp.where(live, g_ref[0].astype(F32), 0.0)
    g_sc[...] = g_full.astype(BF16)
    skip_ref[0, 0] = jnp.sum(x_full * g_full, axis=0, keepdims=True)
    tail = jnp.exp(cum[:, QB - 1 : QB] - cum) * step
    scal_ref[0] = scale_columns(tail, jnp.exp(cum))
    xv_ref[0] = (x_full * spread(tail, ones_rows)).astype(BF16)
    gg_ref[0] = (g_full * spread(jnp.exp(cum), ones_rows)).astype(BF16)
    gram = dot(c_ref[0], b_ref[0], NT)
    causal = (
        lax.broadcasted_iota(jnp.int32, (HALF, HALF), 0)
        >= lax.broadcasted_iota(jnp.int32, (HALF, HALF), 1)
    )
    low, high = slice(0, HALF), slice(HALF, QB)
    tiles = ((low, low), (high, low), (high, high))
    grams = [jnp.where(causal, gram[t, k], 0.0) if t is k else gram[t, k] for t, k in tiles]
    left = lax.broadcasted_iota(jnp.int32, (QB, PAIR), 1) < HP
    zero = jnp.zeros((QB, PAIR), BF16)
    dgrams = [jnp.zeros((HALF, HALF), F32) for _ in tiles]
    for pair in range(heads // 2):
        lanes = slice(pair * PAIR, (pair + 1) * PAIR)
        xx = x_ref[0, :, lanes]
        gg = g_sc[:, lanes]
        gs = [jnp.where(left, gg, zero), jnp.where(left, zero, gg)]
        xs = [jnp.where(left, xx, zero), jnp.where(left, zero, xx)]
        weights = []
        for one in range(2):
            head = 2 * pair + one
            mine = []
            dlow = dot(gs[one], xx[low], NT)
            dhigh = dot(gs[one][high], xx[high], NT)
            dparts = (dlow[low], dlow[high], dhigh)
            for which, (t, k) in enumerate(tiles):
                gap = cum_t[t, head : head + 1] - cum[head : head + 1, k]
                if t is k:
                    gap = jnp.minimum(gap, 0.0)
                decay = jnp.exp(gap) * step[head : head + 1, k]
                mine.append((grams[which] * decay).astype(BF16))
                dgrams[which] = dgrams[which] + dparts[which] * decay
            weights.append(mine)
        (a0, a1, a2), (b0, b1, b2) = weights
        y_sc[low, lanes] = dot(
            jnp.concatenate([a0, b0], axis=1), jnp.concatenate([xs[0][low], xs[1][low]], axis=0), NN
        )
        y_sc[high, lanes] = dot(
            jnp.concatenate([a1, a2, b1, b2], axis=1), jnp.concatenate(xs, axis=0), NN
        )
        d_sc[low, lanes] = dot(
            jnp.concatenate([a0, a1, b0, b1], axis=0), jnp.concatenate(gs, axis=0), TN
        )
        d_sc[high, lanes] = dot(
            jnp.concatenate([a2, b2], axis=0),
            jnp.concatenate([gs[0][high], gs[1][high]], axis=0), TN,
        )
    row = head_sums(g_full * y_sc[...], ones_rows, heads)
    col = head_sums(x_full * d_sc[...], ones_rows, heads)
    diff_ref[0] = row - col
    col_ref[0] = col
    gain = spread(jnp.broadcast_to(column(gain_ref), (heads, 8)), ones_rows)[0:1]
    dx_ref[0] = d_sc[...] + gain * g_full
    dgram = jnp.concatenate(
        [
            jnp.concatenate(
                [jnp.where(causal, dgrams[0], 0.0), jnp.zeros((HALF, HALF), F32)], axis=1
            ),
            jnp.concatenate([dgrams[1], jnp.where(causal, dgrams[2], 0.0)], axis=1),
        ],
        axis=0,
    ).astype(BF16)
    dc_ref[0] = dot(dgram, b_ref[0], NN)
    db_ref[0] = dot(dgram, c_ref[0], TN)


def final_kernel(seq, refs, len_ref, gate_ref, x_ref, g_ref, b_ref, c_ref, dt_ref, bias_ref,
                 alog_ref, ends_ref, first_ref, last_ref, scal_ref, diff_ref, col_ref, skip_ref):
    ddt_ref, par_ref, state_ref, dstate_ref, more_ref, sum_sc, thru_sc = refs
    heads = dt_ref.shape[1]
    toks = x_ref.shape[1]
    part = pl.program_id(0)
    gate = gate_ref[seq]
    pieces = ends_ref.shape[0]
    piece = NS // pieces
    pairs = LANES // PAIR

    @pl.when(part == 0)
    def _():
        sum_sc[...] = jnp.zeros_like(sum_sc)
        thru_sc[...] = jnp.zeros_like(thru_sc)

    tail_part = spread_part(heads, 0, part * LANES, LANES)
    grow_part = spread_part(heads, heads, part * LANES, LANES)
    ones_part = sum_part(heads, part * LANES, LANES)

    def state_of(scan):
        return jnp.concatenate(
            [
                ends_ref[:, (scan * pairs + p) * piece : (scan * pairs + p + 1) * piece].reshape(
                    NS, PAIR
                )
                for p in range(pairs)
            ],
            axis=1,
        )

    grows = [dot(scal_ref[0, b * QB : (b + 1) * QB], grow_part, NN) for b in range(2)]
    ends = [grow[QB - 1 : QB] for grow in grows]
    enter, leave = state_of(0), state_of(1)
    states = [enter, ends[0] * enter + first_ref[0]]
    dstates = [ends[1] * leave + last_ref[0], leave]
    for blk in range(2):
        rows = slice(blk * QB, (blk + 1) * QB)
        state_ref[blk] = states[blk].astype(BF16)
        dstate_ref[blk] = dstates[blk].astype(BF16)
        live = live_rows(token_base(toks) + blk * QB, len_ref[seq], QB)
        g_grow = jnp.where(live, g_ref[0, rows].astype(F32) * grows[blk], 0.0)
        y = exact_dot(c_ref[0, rows], states[blk], NN)
        sum_sc[0, rows] += lane_sums(g_grow * y, ones_part)
        tail = dot(scal_ref[0, rows], tail_part, NN)
        u = tail * exact_dot(b_ref[0, rows], dstates[blk], NN)
        sum_sc[1, rows] += lane_sums(x_ref[0, rows].astype(F32) * u, ones_part)
        through = ends[blk] * jnp.sum(states[blk] * dstates[blk], axis=0, keepdims=True)
        thru_sc[blk] += lane_sums(jnp.broadcast_to(through, (8, LANES)), ones_part)

    @pl.when(part == pl.num_programs(0) - 1)
    def _():
        ones_upper = upper_ones()
        raw = dt_ref[0] + column(bias_ref)
        step = softplus(raw)
        rate = -jnp.exp(column(alog_ref))
        ga = jnp.zeros((heads, 1), F32)
        gb = jnp.zeros((heads, 1), F32)
        for blk in range(2):
            rows = slice(blk * QB, (blk + 1) * QB)
            row = sum_sc[0, rows].T[:heads]
            col = sum_sc[1, rows].T[:heads]
            through = thru_sc[blk].T[:heads, 0:1]
            later = dot(diff_ref[0, :, rows] + row, ones_upper, NT, HIGH)
            earlier = dot(col, ones_upper, NN, HIGH) - col
            dlogs = later + earlier + through
            step_here = step[:, rows]
            dstep = (col_ref[0, :, rows] + col) / step_here + rate * dlogs
            ddt = gate * dstep * jax.nn.sigmoid(raw[:, rows])
            ddt_ref[0, :, rows] = ddt
            gb = gb + jnp.sum(ddt, axis=1, keepdims=True)
            ga = ga + gate * rate * jnp.sum(step_here * dlogs, axis=1, keepdims=True)
        skips = gate * jnp.sum(skip_ref[0], axis=0)
        skips = lane_sums(jnp.broadcast_to(skips, (8, heads * HP)), sum_part(heads, 0, heads * HP))
        rows = [flat(ga, 128), flat(gb, 128), skips[0:1]]
        tile = jnp.concatenate(rows + [jnp.zeros((TILE - 3, 128), F32)], axis=0)
        if more_ref is not None:
            tile = tile + more_ref[0]
        par_ref[...] = jnp.broadcast_to(tile[None], par_ref.shape)


def final_first(len_ref, gate_ref, *refs):
    final_kernel(0, (*refs[14:18], None, *refs[18:]), len_ref, gate_ref, *refs[:14])


def final_second(len_ref, gate_ref, *refs):
    final_kernel(1, (*refs[16:20], refs[14], *refs[20:]), len_ref, gate_ref, *refs[:14])


def groups_kernel(seq, gate_ref, b_ref, scal_ref, xv_ref, gg_ref, state_ref, dstate_ref, dxi_ref,
                  dbi_ref, dci_ref, *refs):
    dx_ref, db_ref, dc_ref, db_sc, dc_sc = refs[-5:]
    part = pl.program_id(0)
    gate = gate_ref[seq]

    @pl.when(part == 0)
    def _():
        db_sc[...] = dbi_ref[0]
        dc_sc[...] = dci_ref[0]

    tail_part = spread_part(NS // 16, 0, part * LANES, LANES)
    for blk in range(2):
        rows = slice(blk * QB, (blk + 1) * QB)
        db_sc[rows] += dot(xv_ref[0, rows], dstate_ref[blk], NT)
        dc_sc[rows] += dot(gg_ref[0, rows], state_ref[blk], NT)
        tail = dot(scal_ref[0, rows], tail_part, NN)
        u = tail * dot(b_ref[0, rows], dstate_ref[blk], NN)
        dx_ref[0, rows] = (gate * (dxi_ref[0, rows] + u)).astype(BF16)

    @pl.when(part == pl.num_programs(0) - 1)
    def _():
        db_ref[0] = (gate * db_sc[...]).astype(BF16)
        dc_ref[0] = (gate * dc_sc[...]).astype(BF16)


def sum_tensor(value):
    count = lax.axis_size("tensor")
    if count == 1:
        return value
    value = value + lax.ppermute(value, "tensor", [(i, i ^ 1) for i in range(count)])
    parts = [
        lax.ppermute(value, "tensor", [(i, (i + 2 * turn) % count) for i in range(count)])
        for turn in range(1, count // 2)
    ]
    return sum(parts, value)


def on_device(
    seq_inputs, b_proj, c_proj, dt_raw, dt_bias, a_log, d_skip, out_grad, log_ratio, lengths
):
    seqs, toks, width = seq_inputs.shape
    heads = dt_bias.shape[0]
    count = lax.axis_size("context")
    parts = width // LANES
    piece = NS // count
    chunk = 2 * (LANES // PAIR) * piece
    bias_row, alog_row, gain_row = dt_bias[None], a_log[None], d_skip[None]
    smem = pl.BlockSpec(memory_space=pltpu.SMEM)
    anywhere = pl.BlockSpec(memory_space=pl.ANY)
    params = pltpu.CompilerParams(vmem_limit_bytes=VMEM)
    whole = lambda *shape: pl.BlockSpec(shape, lambda *at: (0,) * len(shape))
    small = [whole(1, heads), whole(1, heads)]

    work = seqs * parts
    wide = pl.BlockSpec(
        (1, toks, LANES),
        lambda i: (jnp.minimum(i, work - 1) // parts, 0, jnp.minimum(i, work - 1) % parts),
    )
    thin = pl.BlockSpec((1, toks, NS), lambda i: (jnp.minimum(i, work - 1) // parts, 0, 0))
    state_out = pl.BlockSpec(
        (1, NS, LANES),
        lambda i: (jnp.minimum(i, work - 1) // parts, 0, jnp.minimum(i, work - 1) % parts),
    )
    local, first, last = pl.pallas_call(
        states_kernel,
        grid=(work + 1,),
        in_specs=[
            smem, wide, wide, thin, thin,
            pl.BlockSpec((1, heads, toks), lambda i: (jnp.minimum(i, work - 1) // parts, 0, 0)),
            *small, whole(*log_ratio.shape),
        ],
        out_specs=[pl.BlockSpec((count, chunk, PAIR), lambda i: (0, i, 0)), state_out, state_out],
        out_shape=[
            jax.ShapeDtypeStruct((count, work * chunk + TILE, PAIR), F32),
            jax.ShapeDtypeStruct((seqs, NS, width), F32),
            jax.ShapeDtypeStruct((seqs, NS, width), F32),
        ],
        scratch_shapes=[
            pltpu.VMEM((4, NS, QB), BF16), pltpu.VMEM((2, QB, 3 * 128), BF16),
            pltpu.VMEM((TILE, 128), F32),
        ],
        compiler_params=params,
        name="states",
    )(lengths, seq_inputs, out_grad, b_proj, c_proj, dt_raw, bias_row, alog_row, log_ratio)

    owned = lax.all_to_all(local, "context", 0, 0)

    tok_spec = lambda w: pl.BlockSpec((1, QB, w), lambda s, b: (s, b, 0))
    head_spec = pl.BlockSpec((1, heads, QB), lambda s, b: (s, 0, b))
    blocks = toks // QB
    dxi, dbi, dci, diff, col, skips, xv, gg, scal = pl.pallas_call(
        intra_kernel,
        grid=(seqs, blocks),
        in_specs=[smem, tok_spec(width), tok_spec(width), tok_spec(NS), tok_spec(NS),
                  head_spec, *small, whole(1, heads)],
        out_specs=[tok_spec(width), tok_spec(NS), tok_spec(NS), head_spec, head_spec,
                   pl.BlockSpec((1, 1, 1, width), lambda s, b: (s, b, 0, 0)),
                   tok_spec(width), tok_spec(width), tok_spec(3 * 128)],
        out_shape=[
            jax.ShapeDtypeStruct((seqs, toks, width), F32),
            jax.ShapeDtypeStruct((seqs, toks, NS), F32),
            jax.ShapeDtypeStruct((seqs, toks, NS), F32),
            jax.ShapeDtypeStruct((seqs, heads, toks), F32),
            jax.ShapeDtypeStruct((seqs, heads, toks), F32),
            jax.ShapeDtypeStruct((seqs, blocks, 1, width), F32),
            jax.ShapeDtypeStruct((seqs, toks, width), BF16),
            jax.ShapeDtypeStruct((seqs, toks, width), BF16),
            jax.ShapeDtypeStruct((seqs, toks, 3 * 128), BF16),
        ],
        scratch_shapes=[
            pltpu.VMEM((QB, width), F32), pltpu.VMEM((QB, width), F32),
            pltpu.VMEM((QB, width), BF16),
        ],
        compiler_params=params,
        name="intra",
    )(lengths, seq_inputs, out_grad, b_proj, c_proj, dt_raw, bias_row, alog_row, gain_row)

    def chained(seq):
        return pl.pallas_call(
            lambda *refs: chain_kernel(seq, heads, *refs),
            grid=(parts,),
            in_specs=[
                pl.BlockSpec((count, TILE, PAIR), lambda p: (0, work * chunk // TILE, 0)),
                pl.BlockSpec((count, chunk, PAIR), lambda p: (0, seq * parts + p, 0)),
            ],
            out_specs=[pl.BlockSpec((count, chunk, PAIR), lambda p: (0, p, 0)), whole(TILE, 128)],
            out_shape=[
                jax.ShapeDtypeStruct((count, parts * chunk, PAIR), F32),
                jax.ShapeDtypeStruct((TILE, 128), F32),
            ],
            scratch_shapes=[pltpu.VMEM((heads // 2, count, PAIR), F32)],
            compiler_params=params,
            name="chain",
        )(owned, owned)

    owned, dxi = lax.optimization_barrier((owned, dxi))
    chain0, sums = chained(0)
    back0 = lax.all_to_all(chain0, "context", 0, 0)
    chain1, _ = chained(1)
    back1 = lax.all_to_all(chain1, "context", 0, 0)
    totals = sum_tensor(sums[2:4])[:, 0]
    signs = jnp.where(jnp.arange(2, dtype=jnp.int32) == 0, -1.0, 1.0).astype(F32)
    margin = -jnp.sum(signs * totals)
    gate = signs * BETA * jax.nn.sigmoid(-BETA * margin)

    def final(seq, back, *before):
        of_seq = lambda *shape: pl.BlockSpec((1,) + shape, lambda p: (seq,) + (0,) * len(shape))
        laned = lambda rows: pl.BlockSpec((1, rows, LANES), lambda p: (seq, 0, p))
        halves = pl.BlockSpec((2, NS, LANES), lambda p: (0, 0, p))
        return pl.pallas_call(
            final_second if seq else final_first,
            grid=(parts,),
            in_specs=[
                smem, smem, laned(toks), laned(toks), of_seq(toks, NS), of_seq(toks, NS),
                of_seq(heads, toks), *small,
                pl.BlockSpec((count, chunk, PAIR), lambda p: (0, p, 0)),
                laned(NS), laned(NS), of_seq(toks, 3 * 128), of_seq(heads, toks),
                of_seq(heads, toks), of_seq(blocks, 1, width),
            ] + ([whole(1, TILE, 128), anywhere] if seq else []),
            out_specs=[of_seq(heads, toks), whole(count, TILE, 128), halves, halves],
            out_shape=[
                jax.ShapeDtypeStruct((seqs, heads, toks), F32),
                jax.ShapeDtypeStruct((count, TILE, 128), F32),
                jax.ShapeDtypeStruct((2, NS, width), BF16),
                jax.ShapeDtypeStruct((2, NS, width), BF16),
            ],
            scratch_shapes=[pltpu.VMEM((2, toks, 128), F32), pltpu.VMEM((2, 8, 128), F32)],
            input_output_aliases={17: 0} if seq else {},
            compiler_params=params,
            name="final",
        )(lengths, gate, seq_inputs, out_grad, b_proj, c_proj, dt_raw, bias_row, alog_row,
          back, first, last, scal, diff, col, skips, *before)

    def groups(seq, state, dstate, *before):
        of_seq = lambda *shape: pl.BlockSpec((1,) + shape, lambda p: (seq,) + (0,) * len(shape))
        laned = lambda rows: pl.BlockSpec((1, rows, LANES), lambda p: (seq, 0, p))
        halves = pl.BlockSpec((2, NS, LANES), lambda p: (0, 0, p))
        thin_of = of_seq(toks, NS)
        return pl.pallas_call(
            lambda *refs: groups_kernel(seq, *refs),
            grid=(parts,),
            in_specs=[smem, thin_of, of_seq(toks, 3 * 128), laned(toks), laned(toks), halves, halves,
                      laned(toks), thin_of, thin_of] + [anywhere] * len(before),
            out_specs=[laned(toks), thin_of, thin_of],
            out_shape=[jax.ShapeDtypeStruct((seqs, toks, w), BF16) for w in (width, NS, NS)],
            scratch_shapes=[pltpu.VMEM((toks, NS), F32), pltpu.VMEM((toks, NS), F32)],
            input_output_aliases={10: 0, 11: 1, 12: 2} if before else {},
            compiler_params=params,
            name="groups",
        )(gate, b_proj, scal, xv, gg, state, dstate, dxi, dbi, dci, *before)

    ddt, pars, state, dstate = final(0, back0)
    dx, db, dc = groups(0, state, dstate)
    back1, dx = lax.optimization_barrier((back1, dx))
    ddt, pars, state, dstate = final(1, back1, pars, ddt)
    closing = lax.all_to_all(pars, "context", 0, 0)
    dx, db, dc = groups(1, state, dstate, dx, db, dc)
    sums = jnp.sum(closing, axis=0)[:3, :heads]
    return dx, db, dc, ddt, sums[0], sums[1], sums[2]


def solution(mesh):
    return jax.shard_map(
        on_device,
        mesh=mesh,
        in_specs=(
            P(None, "context", "tensor"),
            P(None, "context", "tensor"),
            P(None, "context", "tensor"),
            P(None, "tensor", "context"),
            P("tensor"),
            P("tensor"),
            P("tensor"),
            P(None, "context", "tensor"),
            P(None, ("context", "tensor")),
            P(),
        ),
        out_specs=(
            P(None, "context", "tensor"),
            P(None, "context", "tensor"),
            P(None, "context", "tensor"),
            P(None, "tensor", "context"),
            P("tensor"),
            P("tensor"),
            P("tensor"),
        ),
        check_vma=False,
    )
```

```python
import jax
import jax.numpy as jnp
import numpy as np
from jax import lax
from jax.experimental import pallas as pl
from jax.experimental.pallas import tpu as pltpu
from jax.sharding import PartitionSpec as P

HP = 64
NS = 256
QB = 256
HALF = 128
BETA = 0.5
PAIR = 2 * HP
LANES = 8 * HP
TILE = 8
VMEM = 56 * 1024 * 1024
F32 = jnp.float32
BF16 = jnp.bfloat16
HIGH = lax.Precision.HIGHEST


def dot(lhs, rhs, dims, precision=None):
    return lax.dot_general(
        lhs, rhs, (dims, ((), ())), precision=precision, preferred_element_type=F32
    )


NN = ((1,), (0,))
NT = ((1,), (1,))
TN = ((0,), (0,))


def split3(value):
    top = value.astype(BF16)
    rest = value - top.astype(F32)
    mid = rest.astype(BF16)
    return top, mid, (rest - mid.astype(F32)).astype(BF16)


def spread_matrix(heads):
    row = lax.broadcasted_iota(jnp.int32, (3 * heads, heads * HP), 0)
    lane = lax.broadcasted_iota(jnp.int32, (3 * heads, heads * HP), 1)
    return (lax.rem(row, heads) == lax.div(lane, HP)).astype(BF16)


def spread(values, ones_rows):
    return dot(jnp.concatenate(split3(values), axis=0), ones_rows, TN)


def head_sums(product, ones_rows, heads):
    top = product.astype(BF16)
    low = (product - top.astype(F32)).astype(BF16)
    ones = ones_rows[:heads]
    return dot(ones, top, NT) + dot(ones, low, NT)


def softplus(value):
    return jnp.maximum(value, 0.0) + jnp.log1p(jnp.exp(-jnp.abs(value)))


def upper_ones():
    row = lax.broadcasted_iota(jnp.int32, (QB, QB), 0)
    col = lax.broadcasted_iota(jnp.int32, (QB, QB), 1)
    return (row <= col).astype(BF16)


def running_sum(values, ones, dims=NN):
    rows = values.shape[0]
    sums = dot(jnp.concatenate(split3(values), axis=0), ones, dims)
    return sums[:rows] + sums[rows : 2 * rows] + sums[2 * rows :]


def live_rows(base, length, count):
    row = lax.broadcasted_iota(jnp.int32, (count, 1), 0)
    return base + row < length


def column(row_ref):
    heads = row_ref.shape[1]
    same = lax.broadcasted_iota(jnp.int32, (heads, heads), 0) == lax.broadcasted_iota(
        jnp.int32, (heads, heads), 1
    )
    return jnp.sum(jnp.where(same, row_ref[...], 0.0), axis=1, keepdims=True)


def token_base(toks):
    return lax.axis_index("context") * toks


def flat(column_values, lanes):
    heads = column_values.shape[0]
    same = lax.broadcasted_iota(jnp.int32, (heads, lanes), 0) == lax.broadcasted_iota(
        jnp.int32, (heads, lanes), 1
    )
    return jnp.sum(jnp.where(same, column_values, 0.0), axis=0, keepdims=True)


GAP = 32


def scale_columns(tail, grow):
    rows = jnp.concatenate([tail, grow], axis=0)
    parts = [part.astype(F32) for part in split3(rows)]
    return jnp.concatenate(parts + [jnp.zeros_like(rows)], axis=0).T.astype(BF16)


def spreads(heads):
    row, lane = np.arange(128)[:, None], np.arange(heads * HP)[None, :] // HP
    used = row < 3 * GAP
    return np.stack([used & (row % GAP == lane), used & (row % GAP == lane + GAP // 2)])


def gathers(heads):
    lane, col = np.arange(heads * HP)[:, None] // HP, np.arange(128)[None, :]
    return np.stack([lane == col, lane == col - GAP // 2])


def lane_sums(product, ones_part):
    top = product.astype(BF16)
    low = (product - top.astype(F32)).astype(BF16)
    return dot(top, ones_part, NN) + dot(low, ones_part, NN)


def exact_dot(lhs, rhs, dims):
    top = rhs.astype(BF16)
    low = (rhs - top.astype(F32)).astype(BF16)
    return dot(lhs, top, dims) + dot(lhs, low, dims)


def device_sums(step, rate, ones):
    logs = step * rate
    heads = step.shape[0]
    both = running_sum(jnp.concatenate([logs[:, :QB], logs[:, QB:]], axis=0), ones)
    return both[:heads], both[heads:]


def states_kernel(len_ref, x_ref, g_ref, b_ref, c_ref, dt_ref, bias_ref, alog_ref, ratio_ref,
                  spread_ref, out_ref, scal_sc, tile_sc):
    heads = dt_ref.shape[1]
    toks = x_ref.shape[1]
    pieces = out_ref.shape[0]
    piece = NS // pieces
    at = pl.program_id(0)
    work = 2

    @pl.when(at == 0)
    def _():
        ones = upper_ones()
        bias, rate = column(bias_ref), -jnp.exp(column(alog_ref))
        for seq in range(2):
            step = softplus(dt_ref[seq] + bias)
            cums = device_sums(step, rate, ones)
            mid = cums[0][:, QB - 1 : QB]
            last = mid + cums[1][:, QB - 1 : QB]
            for blk in range(2):
                rows = slice(blk * QB, (blk + 1) * QB)
                cum = cums[blk] + blk * mid
                scal_sc[seq, rows] = scale_columns(jnp.exp(last - cum) * step[:, rows], jnp.exp(cum))
            tile_sc[seq : seq + 1] = flat(jnp.exp(last), 128)

    @pl.when(at < work)
    def _():
        scal = scal_sc[at]
        x_tail = x_ref[0].astype(F32) * dot(scal, spread_ref[0], NN)
        live = live_rows(token_base(toks), len_ref[at], toks)
        g_grow = jnp.where(live, g_ref[0].astype(F32) * dot(scal, spread_ref[1], NN), 0.0)
        whole = (exact_dot(b_ref[0].T, x_tail, NN), exact_dot(c_ref[0].T, g_grow, NN))
        for scan in range(2):
            for pair in range(heads // 2):
                row = (2 * pair + scan) * piece
                out_ref[:, row : row + piece] = whole[scan][:, pair * PAIR : (pair + 1) * PAIR].reshape(
                    pieces, piece, PAIR
                )

    @pl.when(at == work)
    def _():
        ratio = ratio_ref[...]
        rows = ratio.shape[1]
        first = lax.axis_index(("context", "tensor")) * rows
        place = lax.broadcasted_iota(jnp.int32, ratio.shape, 1) + first
        seq = lax.broadcasted_iota(jnp.int32, ratio.shape, 0)
        length = jnp.where(seq == 0, len_ref[0], len_ref[1])
        totals = jnp.sum(jnp.where(place < length, ratio, 0.0), axis=1, keepdims=True)
        tile_sc[2:4] = jnp.broadcast_to(totals, (2, 128))
        tile_sc[4:] = jnp.zeros((TILE - 4, 128), F32)
        out_ref[:, 0:TILE] = jnp.broadcast_to(tile_sc[...][None], (pieces, TILE, 128))


def chain_kernel(unit, heads, tile_ref, in_ref, spread_ref, out_ref, sums_ref, decay_sc):
    count = in_ref.shape[0]
    piece = NS // count
    parts = heads * HP // LANES
    at = pl.program_id(0) + unit
    part = lax.rem(at, parts)

    @pl.when(pl.program_id(0) == 0)
    def _():
        tiles = [tile_ref[src] for src in range(count)]
        sums_ref[...] = sum(tiles[1:], tiles[0])
        decay = jnp.concatenate(
            [tile[seq : seq + 1] for seq in range(2) for tile in tiles], axis=0
        )
        top, mid, low = [split.astype(F32) for split in split3(decay)]
        columns = top + pltpu.roll(mid, GAP, 1) + pltpu.roll(low, 2 * GAP, 1)
        wide = dot(columns.astype(BF16), spread_ref[0], NN)
        for seq in range(2):
            for pair in range(heads // 2):
                decay_sc[seq * (heads // 2) + pair] = wide[
                    seq * count : (seq + 1) * count, pair * PAIR : (pair + 1) * PAIR
                ]

    pairs = LANES // PAIR
    for pair in range(pairs):
        decay = decay_sc[lax.div(at, parts) * (heads // 2) + part * pairs + pair]
        rows = slice(2 * pair * piece, (2 * pair + 1) * piece)
        total = jnp.zeros((piece, PAIR), F32)
        for src in range(count):
            out_ref[src, rows] = total
            total = decay[src : src + 1] * total + in_ref[src, rows]
        rows = slice((2 * pair + 1) * piece, (2 * pair + 2) * piece)
        total = jnp.zeros((piece, PAIR), F32)
        for src in reversed(range(count)):
            out_ref[src, rows] = total
            total = decay[src : src + 1] * total + in_ref[src, rows]


def intra_kernel(len_ref, x_ref, g_ref, b_ref, c_ref, dt_ref, bias_ref, alog_ref, gain_ref, gather_ref,
                 dx_ref, db_ref, dc_ref, diff_ref, col_ref, skip_ref, xv_ref, gg_ref, scal_ref, near_ref, aux_ref,
                 y_sc, d_sc, g_sc):
    heads = dt_ref.shape[1]
    seq, blk = pl.program_id(0), pl.program_id(1)
    ones_rows = spread_matrix(heads)
    raw = dt_ref[0] + column(bias_ref)
    step_all = softplus(raw)
    rate = -jnp.exp(column(alog_ref))
    cums = device_sums(step_all, rate, upper_ones())
    first = blk == 0
    cum = jnp.where(first, cums[0], cums[1])
    step = jnp.where(first, step_all[:, :QB], step_all[:, QB:])
    raw = jnp.where(first, raw[:, :QB], raw[:, QB:])
    cum_t = cum.T
    mid, over = cums[0][:, QB - 1 : QB], cums[1][:, QB - 1 : QB]
    slope = jax.nn.sigmoid(raw)
    aux_ref[0, 0] = slope / step
    aux_ref[0, 1] = slope * rate
    aux_ref[0, 2] = step * rate
    tail = jnp.exp(cum[:, QB - 1 : QB] - cum) * step
    grow = jnp.exp(cum)
    near_ref[0] = scale_columns(tail, grow)
    tail = jnp.exp(jnp.where(first, mid + over, over) - cum) * step
    grow = jnp.exp(cum + jnp.where(first, 0.0, mid))
    scal_ref[0] = scale_columns(tail, grow)
    live = live_rows(token_base(pl.num_programs(1) * QB) + blk * QB, len_ref[seq], QB)
    x_full = x_ref[0].astype(F32)
    g_full = jnp.where(live, g_ref[0].astype(F32), 0.0)
    g_sc[...] = g_full.astype(BF16)
    skips = jnp.sum(x_full * g_full, axis=0, keepdims=True)
    skip_ref[0, 0] = lane_sums(jnp.broadcast_to(skips, (TILE, heads * HP)), gather_ref[0])
    xv_ref[0] = (x_full * spread(tail, ones_rows)).astype(BF16)
    gg_ref[0] = (g_full * spread(grow, ones_rows)).astype(BF16)
    gram = dot(c_ref[0], b_ref[0], NT)
    causal = (
        lax.broadcasted_iota(jnp.int32, (HALF, HALF), 0)
        >= lax.broadcasted_iota(jnp.int32, (HALF, HALF), 1)
    )
    low, high = slice(0, HALF), slice(HALF, QB)
    tiles = ((low, low), (high, low), (high, high))
    grams = [jnp.where(causal, gram[t, k], 0.0) if t is k else gram[t, k] for t, k in tiles]
    left = lax.broadcasted_iota(jnp.int32, (QB, PAIR), 1) < HP
    zero = jnp.zeros((QB, PAIR), BF16)
    dgrams = [jnp.zeros((HALF, HALF), F32) for _ in tiles]
    for pair in range(heads // 2):
        lanes = slice(pair * PAIR, (pair + 1) * PAIR)
        xx = x_ref[0, :, lanes]
        gg = g_sc[:, lanes]
        gs = [jnp.where(left, gg, zero), jnp.where(left, zero, gg)]
        xs = [jnp.where(left, xx, zero), jnp.where(left, zero, xx)]
        weights = []
        for one in range(2):
            head = 2 * pair + one
            mine = []
            dlow = dot(gs[one], xx[low], NT)
            dhigh = dot(gs[one][high], xx[high], NT)
            dparts = (dlow[low], dlow[high], dhigh)
            for which, (t, k) in enumerate(tiles):
                gap = cum_t[t, head : head + 1] - cum[head : head + 1, k]
                if t is k:
                    gap = jnp.minimum(gap, 0.0)
                decay = jnp.exp(gap) * step[head : head + 1, k]
                mine.append((grams[which] * decay).astype(BF16))
                dgrams[which] = dgrams[which] + dparts[which] * decay
            weights.append(mine)
        (a0, a1, a2), (b0, b1, b2) = weights
        y_sc[low, lanes] = dot(
            jnp.concatenate([a0, b0], axis=1), jnp.concatenate([xs[0][low], xs[1][low]], axis=0), NN
        )
        y_sc[high, lanes] = dot(
            jnp.concatenate([a1, a2, b1, b2], axis=1), jnp.concatenate(xs, axis=0), NN
        )
        d_sc[low, lanes] = dot(
            jnp.concatenate([a0, a1, b0, b1], axis=0), jnp.concatenate(gs, axis=0), TN
        )
        d_sc[high, lanes] = dot(
            jnp.concatenate([a2, b2], axis=0),
            jnp.concatenate([gs[0][high], gs[1][high]], axis=0), TN,
        )
    row = head_sums(g_full * y_sc[...], ones_rows, heads)
    col = head_sums(x_full * d_sc[...], ones_rows, heads)
    diff_ref[0] = row - col
    col_ref[0] = col
    gain = spread(jnp.broadcast_to(column(gain_ref), (heads, 8)), ones_rows)[0:1]
    dx_ref[0] = d_sc[...] + gain * g_full
    dgram = jnp.concatenate(
        [
            jnp.concatenate(
                [jnp.where(causal, dgrams[0], 0.0), jnp.zeros((HALF, HALF), F32)], axis=1
            ),
            jnp.concatenate([dgrams[1], jnp.where(causal, dgrams[2], 0.0)], axis=1),
        ],
        axis=0,
    ).astype(BF16)
    dc_ref[0] = dot(dgram, b_ref[0], NN)
    db_ref[0] = dot(dgram, c_ref[0], TN)


def cross_kernel(len_ref, x_ref, g_ref, b_ref, c_ref, near_ref, spread_ref, gather_ref,
                 diff_ref, col_ref, dxi_ref, dbi_ref, dci_ref,
                 dlog_ref, cols_ref, dx_ref, db_ref, dc_ref):
    heads = diff_ref.shape[1]
    seq = pl.program_id(0)
    toks = near_ref.shape[1]
    x_tail = x_ref[0].astype(F32) * dot(near_ref[0, :QB], spread_ref[0], NN)
    live = live_rows(token_base(toks) + QB, len_ref[seq], QB)
    g_grow = jnp.where(live, g_ref[0].astype(F32), 0.0) * dot(near_ref[0, QB:], spread_ref[1], NN)
    early, late = x_tail.astype(BF16), g_grow.astype(BF16)
    b_early, c_late = b_ref[0], c_ref[0]
    gram = dot(c_late, b_early, NT)
    y, back = 0.0, 0.0
    for part in split3(gram)[:2]:
        y = y + exact_dot(part, x_tail, NN)
        back = back + exact_dot(part, g_grow, TN)
    dgram = dot(late, early, NT).astype(BF16)
    dc_ref[0] = dci_ref[0] + dot(dgram, b_early, NN)
    db_ref[0] = dbi_ref[0] + dot(dgram, c_late, TN)
    dx_ref[0] = dxi_ref[0] + dot(near_ref[0, :QB], spread_ref[0], NN) * back
    row = lane_sums(g_grow * y, gather_ref[0]).T[:heads]
    col = lane_sums(x_tail * back, gather_ref[0]).T[:heads]
    ones = upper_ones()
    dlog_ref[0, :, :QB] = (
        running_sum(diff_ref[0, :, :QB], ones, NT) + running_sum(col, ones) - col
    )
    dlog_ref[0, :, QB:] = running_sum(diff_ref[0, :, QB:] + row, ones, NT)
    cols_ref[0, :, :QB] = col_ref[0, :, :QB] + col
    cols_ref[0, :, QB:] = col_ref[0, :, QB:]


def state_of(ends_ref, scan):
    piece = NS // ends_ref.shape[0]
    pairs = ends_ref.shape[1] // (2 * piece)
    return jnp.concatenate(
        [
            ends_ref[:, (2 * p + scan) * piece : (2 * p + scan + 1) * piece].reshape(NS, PAIR)
            for p in range(pairs)
        ],
        axis=1,
    )


def final_kernel(unit, heads, len_ref, gate_ref, x_ref, g_ref, b_ref, c_ref, ends_ref, scal_ref,
                 aux_ref, dlog_ref, cols_ref, skip_ref, spread_ref, gather_ref, *refs):
    ddt_ref, par_ref, part_ref, thru_ref, sum_sc, thru_sc, tile_sc = refs[-7:]
    before = refs[:-7]
    toks = x_ref.shape[1]
    parts = heads * HP // LANES
    at = pl.program_id(0) + unit
    seq, part = lax.div(at, parts), lax.rem(at, parts)
    gate = gate_ref[seq]

    @pl.when(pl.program_id(0) == 0)
    def _():
        tile_sc[...] = before[0][0] if before else jnp.zeros_like(tile_sc)
        if before:
            sum_sc[...] = before[1][...]
            thru_sc[...] = before[2][...]

    @pl.when(part == 0)
    def _():
        sum_sc[...] = jnp.zeros_like(sum_sc)
        thru_sc[...] = jnp.zeros_like(thru_sc)

    enter, leave = state_of(ends_ref, 0), state_of(ends_ref, 1)
    for blk in range(2):
        rows = slice(blk * QB, (blk + 1) * QB)
        live = live_rows(token_base(toks) + blk * QB, len_ref[seq], QB)
        grow = dot(scal_ref[0, rows], spread_ref[1], NN)
        g_grow = jnp.where(live, g_ref[0, rows].astype(F32) * grow, 0.0)
        y = exact_dot(c_ref[0, rows], enter, NN)
        tail = dot(scal_ref[0, rows], spread_ref[0], NN)
        u = tail * exact_dot(b_ref[0, rows], leave, NN)
        sum_sc[rows] += lane_sums(g_grow * y, gather_ref[0]) + lane_sums(
            x_ref[0, rows].astype(F32) * u, gather_ref[1]
        )
    product = grow[QB - 1 : QB] * jnp.sum(enter * leave, axis=0, keepdims=True)
    thru_sc[...] += lane_sums(jnp.broadcast_to(product, (TILE, LANES)), gather_ref[0])

    @pl.when(part == parts - 1)
    def _():
        ones = upper_ones()
        halves = [slice(blk * QB, (blk + 1) * QB) for blk in range(2)]
        sums = [sum_sc[rows].T for rows in halves]
        both = jnp.concatenate([half[:heads] for half in sums], axis=0)
        cols = jnp.concatenate([half[heads : 2 * heads] for half in sums], axis=0)
        later = running_sum(both, ones, NT)
        earlier = running_sum(cols, ones)
        thru = thru_sc[...].T[:heads, 0:1]
        rest = (
            later[heads:, 0:1] + thru,
            earlier[:heads, QB - 1 : QB] + thru,
        )
        gb = jnp.zeros((heads, 1), F32)
        ga = jnp.zeros((heads, 1), F32)
        for blk, rows in enumerate(halves):
            mine = slice(blk * heads, (blk + 1) * heads)
            dlog = dlog_ref[0, :, rows] + later[mine] + earlier[mine] - cols[mine] + rest[blk]
            col = cols_ref[0, :, rows] + cols[mine]
            ddt = gate * (aux_ref[0, 0, :, rows] * col + aux_ref[0, 1, :, rows] * dlog)
            ddt_ref[0, :, rows] = ddt
            gb = gb + jnp.sum(ddt, axis=1, keepdims=True)
            ga = ga + gate * jnp.sum(aux_ref[0, 2, :, rows] * dlog, axis=1, keepdims=True)
        skips = gate * (skip_ref[0, 0] + skip_ref[0, 1])
        rows = [flat(ga, 128), flat(gb, 128), skips[0:1]]
        tile_sc[...] += jnp.concatenate(rows + [jnp.zeros((TILE - 3, 128), F32)], axis=0)

    @pl.when(pl.program_id(0) == pl.num_programs(0) - 1)
    def _():
        par_ref[...] = jnp.broadcast_to(tile_sc[...][None], par_ref.shape)
        part_ref[...] = sum_sc[...]
        thru_ref[...] = thru_sc[...]


def groups_kernel(seq, gate_ref, b_ref, scal_ref, xv_ref, gg_ref, dxi_ref, dbi_ref, dci_ref,
                  spread_ref, *refs):
    dx_ref, db_ref, dc_ref, db_sc, dc_sc = refs[-5:]
    ends = refs[:2] if seq else refs[:1]
    part = pl.program_id(0)
    gate = gate_ref[seq]

    @pl.when(part == 0)
    def _():
        db_sc[...] = dbi_ref[0]
        dc_sc[...] = dci_ref[0]

    def add(ends_ref):
        enter = state_of(ends_ref, 0).astype(BF16)
        leave = state_of(ends_ref, 1).astype(BF16)
        db_sc[...] += dot(xv_ref[0], leave, NT)
        dc_sc[...] += dot(gg_ref[0], enter, NT)
        u = dot(scal_ref[0], spread_ref[0], NN) * dot(b_ref[0], leave, NN)
        dx_ref[0] = (gate * (dxi_ref[0] + u)).astype(BF16)

    if seq:
        pl.when(part == 0)(lambda: add(ends[0]))
        pl.when(part == 1)(lambda: add(ends[1]))
    else:
        add(ends[0])

    @pl.when(part == pl.num_programs(0) - 1)
    def _():
        db_ref[0] = (gate * db_sc[...]).astype(BF16)
        dc_ref[0] = (gate * dc_sc[...]).astype(BF16)


def sum_tensor(value):
    count = lax.axis_size("tensor")
    if count == 1:
        return value
    value = value + lax.ppermute(value, "tensor", [(i, i ^ 1) for i in range(count)])
    parts = [
        lax.ppermute(value, "tensor", [(i, (i + 2 * turn) % count) for i in range(count)])
        for turn in range(1, count // 2)
    ]
    return sum(parts, value)


def on_device(
    seq_inputs, b_proj, c_proj, dt_raw, dt_bias, a_log, d_skip, out_grad, log_ratio, lengths
):
    seqs, toks, width = seq_inputs.shape
    heads = dt_bias.shape[0]
    count = lax.axis_size("context")
    parts = width // LANES
    units = seqs * parts
    head_units = units - 1
    chunk = 2 * (LANES // PAIR) * (NS // count)
    spread_ones = jnp.asarray(spreads(heads), BF16)
    gather_ones = jnp.asarray(gathers(heads), BF16)
    bias_row, alog_row, gain_row = dt_bias[None], a_log[None], d_skip[None]
    smem = pl.BlockSpec(memory_space=pltpu.SMEM)
    anywhere = pl.BlockSpec(memory_space=pl.ANY)
    params = pltpu.CompilerParams(vmem_limit_bytes=VMEM)
    whole = lambda *shape: pl.BlockSpec(shape, lambda *at: (0,) * len(shape))
    small = [whole(1, heads), whole(1, heads)]

    of_either = lambda *shape: pl.BlockSpec(
        (1,) + shape, lambda i: (jnp.minimum(i, seqs - 1),) + (0,) * len(shape)
    )
    local = pl.pallas_call(
        states_kernel,
        grid=(seqs + 1,),
        in_specs=[
            smem, of_either(toks, width), of_either(toks, width), of_either(toks, NS),
            of_either(toks, NS), whole(*dt_raw.shape), *small, whole(*log_ratio.shape),
            whole(2, 128, width),
        ],
        out_specs=pl.BlockSpec((count, parts * chunk, PAIR), lambda i: (0, i, 0)),
        out_shape=jax.ShapeDtypeStruct((count, units * chunk + TILE, PAIR), F32),
        scratch_shapes=[pltpu.VMEM((seqs, toks, 128), BF16), pltpu.VMEM((TILE, 128), F32)],
        compiler_params=params,
        name="states",
    )(lengths, seq_inputs, out_grad, b_proj, c_proj, dt_raw, bias_row, alog_row, log_ratio,
      spread_ones)

    owned = lax.all_to_all(local, "context", 0, 0)

    tok_spec = lambda w: pl.BlockSpec((1, QB, w), lambda s, b: (s, b, 0))
    head_spec = pl.BlockSpec((1, heads, QB), lambda s, b: (s, 0, b))
    blocks = toks // QB
    dxi, dbi, dci, diff, col, skips, xv, gg, scal, near, aux = pl.pallas_call(
        intra_kernel,
        grid=(seqs, blocks),
        in_specs=[smem, tok_spec(width), tok_spec(width), tok_spec(NS), tok_spec(NS),
                  pl.BlockSpec((1, heads, toks), lambda s, b: (s, 0, 0)), *small, whole(1, heads),
                  whole(2, width, 128)],
        out_specs=[tok_spec(width), tok_spec(NS), tok_spec(NS), head_spec, head_spec,
                   pl.BlockSpec((1, 1, TILE, 128), lambda s, b: (s, b, 0, 0)),
                   tok_spec(width), tok_spec(width), tok_spec(128), tok_spec(128),
                   pl.BlockSpec((1, 3, heads, QB), lambda s, b: (s, 0, 0, b))],
        out_shape=[
            jax.ShapeDtypeStruct((seqs, toks, width), F32),
            jax.ShapeDtypeStruct((seqs, toks, NS), F32),
            jax.ShapeDtypeStruct((seqs, toks, NS), F32),
            jax.ShapeDtypeStruct((seqs, heads, toks), F32),
            jax.ShapeDtypeStruct((seqs, heads, toks), F32),
            jax.ShapeDtypeStruct((seqs, blocks, TILE, 128), F32),
            jax.ShapeDtypeStruct((seqs, toks, width), BF16),
            jax.ShapeDtypeStruct((seqs, toks, width), BF16),
            jax.ShapeDtypeStruct((seqs, toks, 128), BF16),
            jax.ShapeDtypeStruct((seqs, toks, 128), BF16),
            jax.ShapeDtypeStruct((seqs, 3, heads, toks), F32),
        ],
        scratch_shapes=[
            pltpu.VMEM((QB, width), F32), pltpu.VMEM((QB, width), F32),
            pltpu.VMEM((QB, width), BF16),
        ],
        compiler_params=params,
        name="intra",
    )(lengths, seq_inputs, out_grad, b_proj, c_proj, dt_raw, bias_row, alog_row, gain_row,
      gather_ones)

    of_seq = lambda *shape: pl.BlockSpec((1,) + shape, lambda i: (i,) + (0,) * len(shape))
    early = lambda w: pl.BlockSpec((1, QB, w), lambda i: (i, 0, 0))
    late = lambda w: pl.BlockSpec((1, QB, w), lambda i: (i, 1, 0))
    dlog, cols, dxi, dbi, dci = pl.pallas_call(
        cross_kernel,
        grid=(seqs,),
        in_specs=[smem, early(width), late(width), early(NS), late(NS), of_seq(toks, 128),
                  whole(2, 128, width), whole(2, width, 128), of_seq(heads, toks),
                  of_seq(heads, toks), early(width), early(NS), late(NS)],
        out_specs=[of_seq(heads, toks), of_seq(heads, toks), early(width), early(NS), late(NS)],
        out_shape=[
            jax.ShapeDtypeStruct((seqs, heads, toks), F32),
            jax.ShapeDtypeStruct((seqs, heads, toks), F32),
            jax.ShapeDtypeStruct((seqs, toks, width), F32),
            jax.ShapeDtypeStruct((seqs, toks, NS), F32),
            jax.ShapeDtypeStruct((seqs, toks, NS), F32),
        ],
        input_output_aliases={10: 2, 11: 3, 12: 4},
        compiler_params=params,
        name="cross",
    )(lengths, seq_inputs, out_grad, b_proj, c_proj, near, spread_ones, gather_ones, diff, col,
      dxi, dbi, dci)

    def chained(unit, number):
        return pl.pallas_call(
            lambda *refs: chain_kernel(unit, heads, *refs),
            grid=(number,),
            in_specs=[
                pl.BlockSpec((count, TILE, PAIR), lambda i: (0, units * chunk // TILE, 0)),
                pl.BlockSpec((count, chunk, PAIR), lambda i: (0, i + unit, 0)),
                whole(2, 128, width),
            ],
            out_specs=[pl.BlockSpec((count, chunk, PAIR), lambda i: (0, i, 0)), whole(TILE, 128)],
            out_shape=[
                jax.ShapeDtypeStruct((count, number * chunk, PAIR), F32),
                jax.ShapeDtypeStruct((TILE, 128), F32),
            ],
            scratch_shapes=[pltpu.VMEM((seqs * heads // 2, count, PAIR), F32)],
            compiler_params=params,
            name="chain",
        )(owned, owned, spread_ones)

    owned, dxi = lax.optimization_barrier((owned, dxi))
    most, sums = chained(0, head_units)
    most = lax.all_to_all(most, "context", 0, 0)
    least, _ = chained(head_units, units - head_units)
    least = lax.all_to_all(least, "context", 0, 0)
    totals = sum_tensor(sums[2:4])[:, 0]
    signs = jnp.where(jnp.arange(2, dtype=jnp.int32) == 0, -1.0, 1.0).astype(F32)
    margin = -jnp.sum(signs * totals)
    gate = signs * BETA * jax.nn.sigmoid(-BETA * margin)

    def final(unit, number, back, *before):
        at_seq = lambda *shape: pl.BlockSpec(
            (1,) + shape, lambda i: ((i + unit) // parts,) + (0,) * len(shape)
        )
        laned = pl.BlockSpec(
            (1, toks, LANES), lambda i: ((i + unit) // parts, 0, (i + unit) % parts)
        )
        return pl.pallas_call(
            lambda *refs: final_kernel(unit, heads, *refs),
            grid=(number,),
            in_specs=[
                smem, smem, laned, laned, at_seq(toks, NS), at_seq(toks, NS),
                pl.BlockSpec((count, chunk, PAIR), lambda i: (0, i, 0)),
                at_seq(toks, 128), at_seq(3, heads, toks), at_seq(heads, toks),
                at_seq(heads, toks), at_seq(blocks, TILE, 128),
                pl.BlockSpec((2, 128, LANES), lambda i: (0, 0, (i + unit) % parts)),
                pl.BlockSpec((2, LANES, 128), lambda i: (0, (i + unit) % parts, 0)),
            ] + ([whole(1, TILE, 128), whole(toks, 128), whole(TILE, 128), anywhere] if before else []),
            out_specs=[at_seq(heads, toks), whole(count, TILE, 128), whole(toks, 128),
                       whole(TILE, 128)],
            out_shape=[
                jax.ShapeDtypeStruct((seqs, heads, toks), F32),
                jax.ShapeDtypeStruct((count, TILE, 128), F32),
                jax.ShapeDtypeStruct((toks, 128), F32),
                jax.ShapeDtypeStruct((TILE, 128), F32),
            ],
            scratch_shapes=[pltpu.VMEM((toks, 128), F32), pltpu.VMEM((TILE, 128), F32),
                            pltpu.VMEM((TILE, 128), F32)],
            input_output_aliases={17: 0} if before else {},
            compiler_params=params,
            name="final",
        )(lengths, gate, seq_inputs, out_grad, b_proj, c_proj, back, scal, aux, dlog, cols, skips,
          spread_ones, gather_ones, *before)

    def groups(seq, states, *before):
        of_seq = lambda *shape: pl.BlockSpec((1,) + shape, lambda p: (seq,) + (0,) * len(shape))
        laned = pl.BlockSpec((1, toks, LANES), lambda p: (seq, 0, p))
        if seq:
            last = pl.BlockSpec((count, chunk, PAIR), lambda p: (0, 0, 0))
            ends = [pl.BlockSpec((count, chunk, PAIR), lambda p: (0, head_units - 1, 0)), last]
        else:
            ends = [pl.BlockSpec((count, chunk, PAIR), lambda p: (0, p, 0))]
        return pl.pallas_call(
            lambda *refs: groups_kernel(seq, *refs),
            grid=(parts,),
            in_specs=[smem, of_seq(toks, NS), of_seq(toks, 128), laned, laned, laned,
                      of_seq(toks, NS), of_seq(toks, NS),
                      pl.BlockSpec((2, 128, LANES), lambda p: (0, 0, p))]
            + ends + [anywhere] * len(before),
            out_specs=[laned, of_seq(toks, NS), of_seq(toks, NS)],
            out_shape=[jax.ShapeDtypeStruct((seqs, toks, w), BF16) for w in (width, NS, NS)],
            scratch_shapes=[pltpu.VMEM((toks, NS), F32), pltpu.VMEM((toks, NS), F32)],
            input_output_aliases={9 + len(ends) + k: k for k in range(len(before))},
            compiler_params=params,
            name="groups",
        )(gate, b_proj, scal, xv, gg, dxi, dbi, dci, spread_ones, *states, *before)

    ddt, pars, some, thru = final(0, head_units, most)
    dx, db, dc = groups(0, (most,))
    least, dx, some = lax.optimization_barrier((least, dx, some))
    ddt, pars, _, _ = final(head_units, units - head_units, least, pars, some, thru, ddt)
    closing = lax.all_to_all(pars, "context", 0, 0)
    dx, db, dc = groups(1, (most, least), dx, db, dc)
    sums = jnp.sum(closing, axis=0)[:3, :heads]
    return dx, db, dc, ddt, sums[0], sums[1], sums[2]


def solution(mesh):
    return jax.shard_map(
        on_device,
        mesh=mesh,
        in_specs=(
            P(None, "context", "tensor"),
            P(None, "context", "tensor"),
            P(None, "context", "tensor"),
            P(None, "tensor", "context"),
            P("tensor"),
            P("tensor"),
            P("tensor"),
            P(None, "context", "tensor"),
            P(None, ("context", "tensor")),
            P(),
        ),
        out_specs=(
            P(None, "context", "tensor"),
            P(None, "context", "tensor"),
            P(None, "context", "tensor"),
            P(None, "tensor", "context"),
            P("tensor"),
            P("tensor"),
            P("tensor"),
        ),
        check_vma=False,
    )
```

```python
import jax
import jax.numpy as jnp
import numpy as np
from jax import lax
from jax.experimental import pallas as pl
from jax.experimental.pallas import tpu as pltpu
from jax.sharding import PartitionSpec as P

HP = 64
NS = 256
QB = 256
HALF = 128
BETA = 0.5
PAIR = 2 * HP
LANES = 8 * HP
TILE = 8
VMEM = 56 * 1024 * 1024
F32 = jnp.float32
BF16 = jnp.bfloat16
HIGH = lax.Precision.HIGHEST


def dot(lhs, rhs, dims, precision=None):
    return lax.dot_general(
        lhs, rhs, (dims, ((), ())), precision=precision, preferred_element_type=F32
    )


NN = ((1,), (0,))
NT = ((1,), (1,))
TN = ((0,), (0,))


def split3(value):
    top = value.astype(BF16)
    rest = value - top.astype(F32)
    mid = rest.astype(BF16)
    return top, mid, (rest - mid.astype(F32)).astype(BF16)


def spread_matrix(heads):
    row = lax.broadcasted_iota(jnp.int32, (3 * heads, heads * HP), 0)
    lane = lax.broadcasted_iota(jnp.int32, (3 * heads, heads * HP), 1)
    return (lax.rem(row, heads) == lax.div(lane, HP)).astype(BF16)


def spread(values, ones_rows):
    return dot(jnp.concatenate(split3(values), axis=0), ones_rows, TN)


def head_sums(product, ones_rows, heads):
    top = product.astype(BF16)
    low = (product - top.astype(F32)).astype(BF16)
    ones = ones_rows[:heads]
    return dot(ones, top, NT) + dot(ones, low, NT)


def softplus(value):
    return jnp.maximum(value, 0.0) + jnp.log1p(jnp.exp(-jnp.abs(value)))


def upper_ones():
    row = lax.broadcasted_iota(jnp.int32, (QB, QB), 0)
    col = lax.broadcasted_iota(jnp.int32, (QB, QB), 1)
    return (row <= col).astype(BF16)


def running_sum(values, ones, dims=NN):
    rows = values.shape[0]
    sums = dot(jnp.concatenate(split3(values), axis=0), ones, dims)
    return sums[:rows] + sums[rows : 2 * rows] + sums[2 * rows :]


def live_rows(base, length, count):
    row = lax.broadcasted_iota(jnp.int32, (count, 1), 0)
    return base + row < length


def column(row_ref):
    heads = row_ref.shape[1]
    same = lax.broadcasted_iota(jnp.int32, (heads, heads), 0) == lax.broadcasted_iota(
        jnp.int32, (heads, heads), 1
    )
    return jnp.sum(jnp.where(same, row_ref[...], 0.0), axis=1, keepdims=True)


def token_base(toks):
    return lax.axis_index("context") * toks


def flat(column_values, lanes):
    heads = column_values.shape[0]
    same = lax.broadcasted_iota(jnp.int32, (heads, lanes), 0) == lax.broadcasted_iota(
        jnp.int32, (heads, lanes), 1
    )
    return jnp.sum(jnp.where(same, column_values, 0.0), axis=0, keepdims=True)


GAP = 32


def scale_columns(tail, grow):
    rows = jnp.concatenate([tail, grow], axis=0)
    parts = [part.astype(F32) for part in split3(rows)]
    return jnp.concatenate(parts + [jnp.zeros_like(rows)], axis=0).T.astype(BF16)


def spreads(heads):
    row, lane = np.arange(128)[:, None], np.arange(heads * HP)[None, :] // HP
    used = row < 3 * GAP
    return np.stack([used & (row % GAP == lane), used & (row % GAP == lane + GAP // 2)])


def gathers(heads):
    lane, col = np.arange(heads * HP)[:, None] // HP, np.arange(128)[None, :]
    return np.stack([lane == col, lane == col - GAP // 2])


def lane_sums(product, ones_part):
    top = product.astype(BF16)
    low = (product - top.astype(F32)).astype(BF16)
    return dot(top, ones_part, NN) + dot(low, ones_part, NN)


def exact_dot(lhs, rhs, dims):
    top = rhs.astype(BF16)
    low = (rhs - top.astype(F32)).astype(BF16)
    return dot(lhs, top, dims) + dot(lhs, low, dims)


def device_sums(step, rate, ones):
    logs = step * rate
    heads = step.shape[0]
    both = running_sum(jnp.concatenate([logs[:, :QB], logs[:, QB:]], axis=0), ones)
    return both[:heads], both[heads:]


def states_kernel(len_ref, x_ref, g_ref, b_ref, c_ref, dt_ref, bias_ref, alog_ref, ratio_ref,
                  spread_ref, out_ref, scal_sc, tile_sc):
    heads = dt_ref.shape[1]
    toks = x_ref.shape[1]
    pieces = out_ref.shape[0]
    piece = NS // pieces
    at = pl.program_id(0)
    work = 2

    @pl.when(at == 0)
    def _():
        ones = upper_ones()
        bias, rate = column(bias_ref), -jnp.exp(column(alog_ref))
        for seq in range(2):
            step = softplus(dt_ref[seq] + bias)
            cums = device_sums(step, rate, ones)
            mid = cums[0][:, QB - 1 : QB]
            last = mid + cums[1][:, QB - 1 : QB]
            for blk in range(2):
                rows = slice(blk * QB, (blk + 1) * QB)
                cum = cums[blk] + blk * mid
                scal_sc[seq, rows] = scale_columns(jnp.exp(last - cum) * step[:, rows], jnp.exp(cum))
            tile_sc[seq : seq + 1] = flat(jnp.exp(last), 128)

    @pl.when(at < work)
    def _():
        scal = scal_sc[at]
        x_tail = x_ref[0].astype(F32) * dot(scal, spread_ref[0], NN)
        live = live_rows(token_base(toks), len_ref[at], toks)
        g_grow = jnp.where(live, g_ref[0].astype(F32) * dot(scal, spread_ref[1], NN), 0.0)
        whole = (exact_dot(b_ref[0].T, x_tail, NN), exact_dot(c_ref[0].T, g_grow, NN))
        for scan in range(2):
            for pair in range(heads // 2):
                row = (2 * pair + scan) * piece
                out_ref[:, row : row + piece] = whole[scan][:, pair * PAIR : (pair + 1) * PAIR].reshape(
                    pieces, piece, PAIR
                )

    @pl.when(at == work)
    def _():
        ratio = ratio_ref[...]
        rows = ratio.shape[1]
        first = lax.axis_index(("context", "tensor")) * rows
        place = lax.broadcasted_iota(jnp.int32, ratio.shape, 1) + first
        seq = lax.broadcasted_iota(jnp.int32, ratio.shape, 0)
        length = jnp.where(seq == 0, len_ref[0], len_ref[1])
        totals = jnp.sum(jnp.where(place < length, ratio, 0.0), axis=1, keepdims=True)
        tile_sc[2:4] = jnp.broadcast_to(totals, (2, 128))
        tile_sc[4:] = jnp.zeros((TILE - 4, 128), F32)
        out_ref[:, 0:TILE] = jnp.broadcast_to(tile_sc[...][None], (pieces, TILE, 128))


def chain_kernel(unit, heads, tile_ref, in_ref, spread_ref, out_ref, sums_ref, decay_sc):
    count = in_ref.shape[0]
    piece = NS // count
    parts = heads * HP // LANES
    at = pl.program_id(0) + unit
    part = lax.rem(at, parts)

    @pl.when(pl.program_id(0) == 0)
    def _():
        tiles = [tile_ref[src] for src in range(count)]
        sums_ref[...] = sum(tiles[1:], tiles[0])
        decay = jnp.concatenate(
            [tile[seq : seq + 1] for seq in range(2) for tile in tiles], axis=0
        )
        top, mid, low = [split.astype(F32) for split in split3(decay)]
        columns = top + pltpu.roll(mid, GAP, 1) + pltpu.roll(low, 2 * GAP, 1)
        wide = dot(columns.astype(BF16), spread_ref[0], NN)
        for seq in range(2):
            for pair in range(heads // 2):
                decay_sc[seq * (heads // 2) + pair] = wide[
                    seq * count : (seq + 1) * count, pair * PAIR : (pair + 1) * PAIR
                ]

    pairs = LANES // PAIR
    for pair in range(pairs):
        decay = decay_sc[lax.div(at, parts) * (heads // 2) + part * pairs + pair]
        rows = slice(2 * pair * piece, (2 * pair + 1) * piece)
        total = jnp.zeros((piece, PAIR), F32)
        for src in range(count):
            out_ref[src, rows] = total
            total = decay[src : src + 1] * total + in_ref[src, rows]
        rows = slice((2 * pair + 1) * piece, (2 * pair + 2) * piece)
        total = jnp.zeros((piece, PAIR), F32)
        for src in reversed(range(count)):
            out_ref[src, rows] = total
            total = decay[src : src + 1] * total + in_ref[src, rows]


def intra_kernel(len_ref, x_ref, g_ref, b_ref, c_ref, dt_ref, bias_ref, alog_ref, gain_ref, gather_ref,
                 dx_ref, db_ref, dc_ref, diff_ref, col_ref, skip_ref, xv_ref, gg_ref, scal_ref, near_ref, aux_ref,
                 y_sc, d_sc, g_sc):
    heads = dt_ref.shape[1]
    seq, blk = pl.program_id(0), pl.program_id(1)
    ones_rows = spread_matrix(heads)
    raw = dt_ref[0] + column(bias_ref)
    step_all = softplus(raw)
    rate = -jnp.exp(column(alog_ref))
    cums = device_sums(step_all, rate, upper_ones())
    first = blk == 0
    cum = jnp.where(first, cums[0], cums[1])
    step = jnp.where(first, step_all[:, :QB], step_all[:, QB:])
    raw = jnp.where(first, raw[:, :QB], raw[:, QB:])
    cum_t = cum.T
    mid, over = cums[0][:, QB - 1 : QB], cums[1][:, QB - 1 : QB]
    slope = jax.nn.sigmoid(raw)
    aux_ref[0, 0] = slope / step
    aux_ref[0, 1] = slope * rate
    aux_ref[0, 2] = step * rate
    tail = jnp.exp(cum[:, QB - 1 : QB] - cum) * step
    grow = jnp.exp(cum)
    near_ref[0] = scale_columns(tail, grow)
    tail = jnp.exp(jnp.where(first, mid + over, over) - cum) * step
    grow = jnp.exp(cum + jnp.where(first, 0.0, mid))
    scal_ref[0] = scale_columns(tail, grow)
    live = live_rows(token_base(pl.num_programs(1) * QB) + blk * QB, len_ref[seq], QB)
    x_full = x_ref[0].astype(F32)
    g_full = jnp.where(live, g_ref[0].astype(F32), 0.0)
    g_sc[...] = g_full.astype(BF16)
    skips = jnp.sum(x_full * g_full, axis=0, keepdims=True)
    skip_ref[0, 0] = lane_sums(jnp.broadcast_to(skips, (TILE, heads * HP)), gather_ref[0])
    xv_ref[0] = (x_full * spread(tail, ones_rows)).astype(BF16)
    gg_ref[0] = (g_full * spread(grow, ones_rows)).astype(BF16)
    gram = dot(c_ref[0], b_ref[0], NT)
    causal = (
        lax.broadcasted_iota(jnp.int32, (HALF, HALF), 0)
        >= lax.broadcasted_iota(jnp.int32, (HALF, HALF), 1)
    )
    low, high = slice(0, HALF), slice(HALF, QB)
    tiles = ((low, low), (high, low), (high, high))
    grams = [jnp.where(causal, gram[t, k], 0.0) if t is k else gram[t, k] for t, k in tiles]
    left = lax.broadcasted_iota(jnp.int32, (QB, PAIR), 1) < HP
    zero = jnp.zeros((QB, PAIR), BF16)
    dgrams = [jnp.zeros((HALF, HALF), F32) for _ in tiles]
    for pair in range(heads // 2):
        lanes = slice(pair * PAIR, (pair + 1) * PAIR)
        xx = x_ref[0, :, lanes]
        gg = g_sc[:, lanes]
        gs = [jnp.where(left, gg, zero), jnp.where(left, zero, gg)]
        xs = [jnp.where(left, xx, zero), jnp.where(left, zero, xx)]
        weights = []
        for one in range(2):
            head = 2 * pair + one
            mine = []
            dlow = dot(gs[one], xx[low], NT)
            dhigh = dot(gs[one][high], xx[high], NT)
            dparts = (dlow[low], dlow[high], dhigh)
            for which, (t, k) in enumerate(tiles):
                gap = cum_t[t, head : head + 1] - cum[head : head + 1, k]
                if t is k:
                    gap = jnp.minimum(gap, 0.0)
                decay = jnp.exp(gap) * step[head : head + 1, k]
                mine.append((grams[which] * decay).astype(BF16))
                dgrams[which] = dgrams[which] + dparts[which] * decay
            weights.append(mine)
        (a0, a1, a2), (b0, b1, b2) = weights
        y_sc[low, lanes] = dot(
            jnp.concatenate([a0, b0], axis=1), jnp.concatenate([xs[0][low], xs[1][low]], axis=0), NN
        )
        y_sc[high, lanes] = dot(
            jnp.concatenate([a1, a2, b1, b2], axis=1), jnp.concatenate(xs, axis=0), NN
        )
        d_sc[low, lanes] = dot(
            jnp.concatenate([a0, a1, b0, b1], axis=0), jnp.concatenate(gs, axis=0), TN
        )
        d_sc[high, lanes] = dot(
            jnp.concatenate([a2, b2], axis=0),
            jnp.concatenate([gs[0][high], gs[1][high]], axis=0), TN,
        )
    row = head_sums(g_full * y_sc[...], ones_rows, heads)
    col = head_sums(x_full * d_sc[...], ones_rows, heads)
    diff_ref[0] = row - col
    col_ref[0] = col
    gain = spread(jnp.broadcast_to(column(gain_ref), (heads, 8)), ones_rows)[0:1]
    dx_ref[0] = d_sc[...] + gain * g_full
    dgram = jnp.concatenate(
        [
            jnp.concatenate(
                [jnp.where(causal, dgrams[0], 0.0), jnp.zeros((HALF, HALF), F32)], axis=1
            ),
            jnp.concatenate([dgrams[1], jnp.where(causal, dgrams[2], 0.0)], axis=1),
        ],
        axis=0,
    ).astype(BF16)
    dc_ref[0] = dot(dgram, b_ref[0], NN)
    db_ref[0] = dot(dgram, c_ref[0], TN)


def cross_kernel(len_ref, x_ref, g_ref, b_ref, c_ref, near_ref, spread_ref, gather_ref,
                 diff_ref, col_ref, dxi_ref, dbi_ref, dci_ref,
                 dlog_ref, cols_ref, dx_ref, db_ref, dc_ref):
    heads = diff_ref.shape[1]
    seq = pl.program_id(0)
    toks = near_ref.shape[1]
    x_tail = x_ref[0].astype(F32) * dot(near_ref[0, :QB], spread_ref[0], NN)
    live = live_rows(token_base(toks) + QB, len_ref[seq], QB)
    g_grow = jnp.where(live, g_ref[0].astype(F32), 0.0) * dot(near_ref[0, QB:], spread_ref[1], NN)
    early, late = x_tail.astype(BF16), g_grow.astype(BF16)
    b_early, c_late = b_ref[0], c_ref[0]
    gram = dot(c_late, b_early, NT)
    y, back = 0.0, 0.0
    for part in split3(gram)[:2]:
        y = y + exact_dot(part, x_tail, NN)
        back = back + exact_dot(part, g_grow, TN)
    dgram = dot(late, early, NT).astype(BF16)
    dc_ref[0] = dci_ref[0] + dot(dgram, b_early, NN)
    db_ref[0] = dbi_ref[0] + dot(dgram, c_late, TN)
    dx_ref[0] = dxi_ref[0] + dot(near_ref[0, :QB], spread_ref[0], NN) * back
    row = lane_sums(g_grow * y, gather_ref[0]).T[:heads]
    col = lane_sums(x_tail * back, gather_ref[0]).T[:heads]
    ones = upper_ones()
    dlog_ref[0, :, :QB] = (
        running_sum(diff_ref[0, :, :QB], ones, NT) + running_sum(col, ones) - col
    )
    dlog_ref[0, :, QB:] = running_sum(diff_ref[0, :, QB:] + row, ones, NT)
    cols_ref[0, :, :QB] = col_ref[0, :, :QB] + col
    cols_ref[0, :, QB:] = col_ref[0, :, QB:]


def state_of(ends_ref, scan):
    piece = NS // ends_ref.shape[0]
    pairs = ends_ref.shape[1] // (2 * piece)
    return jnp.concatenate(
        [
            ends_ref[:, (2 * p + scan) * piece : (2 * p + scan + 1) * piece].reshape(NS, PAIR)
            for p in range(pairs)
        ],
        axis=1,
    )


def final_kernel(unit, heads, len_ref, gate_ref, x_ref, g_ref, b_ref, c_ref, ends_ref, scal_ref,
                 aux_ref, dlog_ref, cols_ref, skip_ref, spread_ref, gather_ref, *refs):
    ddt_ref, par_ref, part_ref, thru_ref, sum_sc, thru_sc, tile_sc = refs[-7:]
    before = refs[:-7]
    toks = x_ref.shape[1]
    parts = heads * HP // LANES
    at = pl.program_id(0) + unit
    seq, part = lax.div(at, parts), lax.rem(at, parts)
    gate = gate_ref[seq]

    @pl.when(pl.program_id(0) == 0)
    def _():
        tile_sc[...] = before[0][0] if before else jnp.zeros_like(tile_sc)
        if before:
            sum_sc[...] = before[1][...]
            thru_sc[...] = before[2][...]

    @pl.when(part == 0)
    def _():
        sum_sc[...] = jnp.zeros_like(sum_sc)
        thru_sc[...] = jnp.zeros_like(thru_sc)

    enter, leave = state_of(ends_ref, 0), state_of(ends_ref, 1)
    for blk in range(2):
        rows = slice(blk * QB, (blk + 1) * QB)
        live = live_rows(token_base(toks) + blk * QB, len_ref[seq], QB)
        grow = dot(scal_ref[0, rows], spread_ref[1], NN)
        g_grow = jnp.where(live, g_ref[0, rows].astype(F32) * grow, 0.0)
        y = exact_dot(c_ref[0, rows], enter, NN)
        tail = dot(scal_ref[0, rows], spread_ref[0], NN)
        u = tail * exact_dot(b_ref[0, rows], leave, NN)
        sum_sc[rows] += lane_sums(g_grow * y, gather_ref[0]) + lane_sums(
            x_ref[0, rows].astype(F32) * u, gather_ref[1]
        )
    product = grow[QB - 1 : QB] * jnp.sum(enter * leave, axis=0, keepdims=True)
    thru_sc[...] += lane_sums(jnp.broadcast_to(product, (TILE, LANES)), gather_ref[0])

    @pl.when(part == parts - 1)
    def _():
        ones = upper_ones()
        halves = [slice(blk * QB, (blk + 1) * QB) for blk in range(2)]
        sums = [sum_sc[rows].T for rows in halves]
        both = jnp.concatenate([half[:heads] for half in sums], axis=0)
        cols = jnp.concatenate([half[heads : 2 * heads] for half in sums], axis=0)
        later = running_sum(both, ones, NT)
        earlier = running_sum(cols, ones)
        thru = thru_sc[...].T[:heads, 0:1]
        rest = (
            later[heads:, 0:1] + thru,
            earlier[:heads, QB - 1 : QB] + thru,
        )
        gb = jnp.zeros((heads, 1), F32)
        ga = jnp.zeros((heads, 1), F32)
        for blk, rows in enumerate(halves):
            mine = slice(blk * heads, (blk + 1) * heads)
            dlog = dlog_ref[0, :, rows] + later[mine] + earlier[mine] - cols[mine] + rest[blk]
            col = cols_ref[0, :, rows] + cols[mine]
            ddt = gate * (aux_ref[0, 0, :, rows] * col + aux_ref[0, 1, :, rows] * dlog)
            ddt_ref[0, :, rows] = ddt
            gb = gb + jnp.sum(ddt, axis=1, keepdims=True)
            ga = ga + gate * jnp.sum(aux_ref[0, 2, :, rows] * dlog, axis=1, keepdims=True)
        skips = gate * (skip_ref[0, 0] + skip_ref[0, 1])
        rows = [flat(ga, 128), flat(gb, 128), skips[0:1]]
        tile_sc[...] += jnp.concatenate(rows + [jnp.zeros((TILE - 3, 128), F32)], axis=0)

    @pl.when(pl.program_id(0) == pl.num_programs(0) - 1)
    def _():
        par_ref[...] = jnp.broadcast_to(tile_sc[...][None], par_ref.shape)
        part_ref[...] = sum_sc[...]
        thru_ref[...] = thru_sc[...]


def groups_kernel(seq, gate_ref, b_ref, scal_ref, xv_ref, gg_ref, dxi_ref, dbi_ref, dci_ref,
                  spread_ref, *refs):
    dx_ref, db_ref, dc_ref, db_sc, dc_sc = refs[-5:]
    ends = refs[:2] if seq else refs[:1]
    part = pl.program_id(0)
    gate = gate_ref[seq]

    @pl.when(part == 0)
    def _():
        db_sc[...] = dbi_ref[0]
        dc_sc[...] = dci_ref[0]

    def add(ends_ref):
        enter = state_of(ends_ref, 0).astype(BF16)
        leave = state_of(ends_ref, 1).astype(BF16)
        db_sc[...] += dot(xv_ref[0], leave, NT)
        dc_sc[...] += dot(gg_ref[0], enter, NT)
        u = dot(scal_ref[0], spread_ref[0], NN) * dot(b_ref[0], leave, NN)
        dx_ref[0] = (gate * (dxi_ref[0] + u)).astype(BF16)

    if seq:
        pl.when(part == 0)(lambda: add(ends[0]))
        pl.when(part == 1)(lambda: add(ends[1]))
    else:
        add(ends[0])

    @pl.when(part == pl.num_programs(0) - 1)
    def _():
        db_ref[0] = (gate * db_sc[...]).astype(BF16)
        dc_ref[0] = (gate * dc_sc[...]).astype(BF16)


def sum_tensor(value):
    count = lax.axis_size("tensor")
    if count == 1:
        return value
    value = value + lax.ppermute(value, "tensor", [(i, i ^ 1) for i in range(count)])
    parts = [
        lax.ppermute(value, "tensor", [(i, (i + 2 * turn) % count) for i in range(count)])
        for turn in range(1, count // 2)
    ]
    return sum(parts, value)


def on_device(
    seq_inputs, b_proj, c_proj, dt_raw, dt_bias, a_log, d_skip, out_grad, log_ratio, lengths
):
    seqs, toks, width = seq_inputs.shape
    heads = dt_bias.shape[0]
    count = lax.axis_size("context")
    parts = width // LANES
    units = seqs * parts
    head_units = units - 1
    chunk = 2 * (LANES // PAIR) * (NS // count)
    spread_ones = jnp.asarray(spreads(heads), BF16)
    gather_ones = jnp.asarray(gathers(heads), BF16)
    bias_row, alog_row, gain_row = dt_bias[None], a_log[None], d_skip[None]
    smem = pl.BlockSpec(memory_space=pltpu.SMEM)
    anywhere = pl.BlockSpec(memory_space=pl.ANY)
    params = pltpu.CompilerParams(vmem_limit_bytes=VMEM)
    whole = lambda *shape: pl.BlockSpec(shape, lambda *at: (0,) * len(shape))
    small = [whole(1, heads), whole(1, heads)]

    of_either = lambda *shape: pl.BlockSpec(
        (1,) + shape, lambda i: (jnp.minimum(i, seqs - 1),) + (0,) * len(shape)
    )
    local = pl.pallas_call(
        states_kernel,
        grid=(seqs + 1,),
        in_specs=[
            smem, of_either(toks, width), of_either(toks, width), of_either(toks, NS),
            of_either(toks, NS), whole(*dt_raw.shape), *small, whole(*log_ratio.shape),
            whole(2, 128, width),
        ],
        out_specs=pl.BlockSpec((count, parts * chunk, PAIR), lambda i: (0, i, 0)),
        out_shape=jax.ShapeDtypeStruct((count, units * chunk + TILE, PAIR), F32),
        scratch_shapes=[pltpu.VMEM((seqs, toks, 128), BF16), pltpu.VMEM((TILE, 128), F32)],
        compiler_params=params,
        name="states",
    )(lengths, seq_inputs, out_grad, b_proj, c_proj, dt_raw, bias_row, alog_row, log_ratio,
      spread_ones)

    owned = lax.all_to_all(local, "context", 0, 0)

    def chained(unit, number):
        return pl.pallas_call(
            lambda *refs: chain_kernel(unit, heads, *refs),
            grid=(number,),
            in_specs=[
                pl.BlockSpec((count, TILE, PAIR), lambda i: (0, units * chunk // TILE, 0)),
                pl.BlockSpec((count, chunk, PAIR), lambda i: (0, i + unit, 0)),
                whole(2, 128, width),
            ],
            out_specs=[pl.BlockSpec((count, chunk, PAIR), lambda i: (0, i, 0)), whole(TILE, 128)],
            out_shape=[
                jax.ShapeDtypeStruct((count, number * chunk, PAIR), F32),
                jax.ShapeDtypeStruct((TILE, 128), F32),
            ],
            scratch_shapes=[pltpu.VMEM((seqs * heads // 2, count, PAIR), F32)],
            compiler_params=params,
            name="chain",
        )(owned, owned, spread_ones)

    most, sums = chained(0, head_units)
    most, dt_raw = lax.optimization_barrier((most, dt_raw))
    most = lax.all_to_all(most, "context", 0, 0)

    tok_spec = lambda w: pl.BlockSpec((1, QB, w), lambda s, b: (s, b, 0))
    head_spec = pl.BlockSpec((1, heads, QB), lambda s, b: (s, 0, b))
    blocks = toks // QB
    dxi, dbi, dci, diff, col, skips, xv, gg, scal, near, aux = pl.pallas_call(
        intra_kernel,
        grid=(seqs, blocks),
        in_specs=[smem, tok_spec(width), tok_spec(width), tok_spec(NS), tok_spec(NS),
                  pl.BlockSpec((1, heads, toks), lambda s, b: (s, 0, 0)), *small, whole(1, heads),
                  whole(2, width, 128)],
        out_specs=[tok_spec(width), tok_spec(NS), tok_spec(NS), head_spec, head_spec,
                   pl.BlockSpec((1, 1, TILE, 128), lambda s, b: (s, b, 0, 0)),
                   tok_spec(width), tok_spec(width), tok_spec(128), tok_spec(128),
                   pl.BlockSpec((1, 3, heads, QB), lambda s, b: (s, 0, 0, b))],
        out_shape=[
            jax.ShapeDtypeStruct((seqs, toks, width), F32),
            jax.ShapeDtypeStruct((seqs, toks, NS), F32),
            jax.ShapeDtypeStruct((seqs, toks, NS), F32),
            jax.ShapeDtypeStruct((seqs, heads, toks), F32),
            jax.ShapeDtypeStruct((seqs, heads, toks), F32),
            jax.ShapeDtypeStruct((seqs, blocks, TILE, 128), F32),
            jax.ShapeDtypeStruct((seqs, toks, width), BF16),
            jax.ShapeDtypeStruct((seqs, toks, width), BF16),
            jax.ShapeDtypeStruct((seqs, toks, 128), BF16),
            jax.ShapeDtypeStruct((seqs, toks, 128), BF16),
            jax.ShapeDtypeStruct((seqs, 3, heads, toks), F32),
        ],
        scratch_shapes=[
            pltpu.VMEM((QB, width), F32), pltpu.VMEM((QB, width), F32),
            pltpu.VMEM((QB, width), BF16),
        ],
        compiler_params=params,
        name="intra",
    )(lengths, seq_inputs, out_grad, b_proj, c_proj, dt_raw, bias_row, alog_row, gain_row,
      gather_ones)

    of_seq = lambda *shape: pl.BlockSpec((1,) + shape, lambda i: (i,) + (0,) * len(shape))
    early = lambda w: pl.BlockSpec((1, QB, w), lambda i: (i, 0, 0))
    late = lambda w: pl.BlockSpec((1, QB, w), lambda i: (i, 1, 0))
    dlog, cols, dxi, dbi, dci = pl.pallas_call(
        cross_kernel,
        grid=(seqs,),
        in_specs=[smem, early(width), late(width), early(NS), late(NS), of_seq(toks, 128),
                  whole(2, 128, width), whole(2, width, 128), of_seq(heads, toks),
                  of_seq(heads, toks), early(width), early(NS), late(NS)],
        out_specs=[of_seq(heads, toks), of_seq(heads, toks), early(width), early(NS), late(NS)],
        out_shape=[
            jax.ShapeDtypeStruct((seqs, heads, toks), F32),
            jax.ShapeDtypeStruct((seqs, heads, toks), F32),
            jax.ShapeDtypeStruct((seqs, toks, width), F32),
            jax.ShapeDtypeStruct((seqs, toks, NS), F32),
            jax.ShapeDtypeStruct((seqs, toks, NS), F32),
        ],
        input_output_aliases={10: 2, 11: 3, 12: 4},
        compiler_params=params,
        name="cross",
    )(lengths, seq_inputs, out_grad, b_proj, c_proj, near, spread_ones, gather_ones, diff, col,
      dxi, dbi, dci)

    least, _ = chained(head_units, units - head_units)
    totals = sum_tensor(sums[2:4])[:, 0]
    signs = jnp.where(jnp.arange(2, dtype=jnp.int32) == 0, -1.0, 1.0).astype(F32)
    margin = -jnp.sum(signs * totals)
    gate = signs * BETA * jax.nn.sigmoid(-BETA * margin)
    least, gate, dxi = lax.optimization_barrier((least, gate, dxi))
    least = lax.all_to_all(least, "context", 0, 0)

    def final(unit, number, back, *before):
        at_seq = lambda *shape: pl.BlockSpec(
            (1,) + shape, lambda i: ((i + unit) // parts,) + (0,) * len(shape)
        )
        laned = pl.BlockSpec(
            (1, toks, LANES), lambda i: ((i + unit) // parts, 0, (i + unit) % parts)
        )
        return pl.pallas_call(
            lambda *refs: final_kernel(unit, heads, *refs),
            grid=(number,),
            in_specs=[
                smem, smem, laned, laned, at_seq(toks, NS), at_seq(toks, NS),
                pl.BlockSpec((count, chunk, PAIR), lambda i: (0, i, 0)),
                at_seq(toks, 128), at_seq(3, heads, toks), at_seq(heads, toks),
                at_seq(heads, toks), at_seq(blocks, TILE, 128),
                pl.BlockSpec((2, 128, LANES), lambda i: (0, 0, (i + unit) % parts)),
                pl.BlockSpec((2, LANES, 128), lambda i: (0, (i + unit) % parts, 0)),
            ] + ([whole(1, TILE, 128), whole(toks, 128), whole(TILE, 128), anywhere] if before else []),
            out_specs=[at_seq(heads, toks), whole(count, TILE, 128), whole(toks, 128),
                       whole(TILE, 128)],
            out_shape=[
                jax.ShapeDtypeStruct((seqs, heads, toks), F32),
                jax.ShapeDtypeStruct((count, TILE, 128), F32),
                jax.ShapeDtypeStruct((toks, 128), F32),
                jax.ShapeDtypeStruct((TILE, 128), F32),
            ],
            scratch_shapes=[pltpu.VMEM((toks, 128), F32), pltpu.VMEM((TILE, 128), F32),
                            pltpu.VMEM((TILE, 128), F32)],
            input_output_aliases={17: 0} if before else {},
            compiler_params=params,
            name="final",
        )(lengths, gate, seq_inputs, out_grad, b_proj, c_proj, back, scal, aux, dlog, cols, skips,
          spread_ones, gather_ones, *before)

    def groups(seq, states, *before):
        of_seq = lambda *shape: pl.BlockSpec((1,) + shape, lambda p: (seq,) + (0,) * len(shape))
        laned = pl.BlockSpec((1, toks, LANES), lambda p: (seq, 0, p))
        if seq:
            last = pl.BlockSpec((count, chunk, PAIR), lambda p: (0, 0, 0))
            ends = [pl.BlockSpec((count, chunk, PAIR), lambda p: (0, head_units - 1, 0)), last]
        else:
            ends = [pl.BlockSpec((count, chunk, PAIR), lambda p: (0, p, 0))]
        return pl.pallas_call(
            lambda *refs: groups_kernel(seq, *refs),
            grid=(parts,),
            in_specs=[smem, of_seq(toks, NS), of_seq(toks, 128), laned, laned, laned,
                      of_seq(toks, NS), of_seq(toks, NS),
                      pl.BlockSpec((2, 128, LANES), lambda p: (0, 0, p))]
            + ends + [anywhere] * len(before),
            out_specs=[laned, of_seq(toks, NS), of_seq(toks, NS)],
            out_shape=[jax.ShapeDtypeStruct((seqs, toks, w), BF16) for w in (width, NS, NS)],
            scratch_shapes=[pltpu.VMEM((toks, NS), F32), pltpu.VMEM((toks, NS), F32)],
            input_output_aliases={9 + len(ends) + k: k for k in range(len(before))},
            compiler_params=params,
            name="groups",
        )(gate, b_proj, scal, xv, gg, dxi, dbi, dci, spread_ones, *states, *before)

    ddt, pars, some, thru = final(0, head_units, most)
    dx, db, dc = groups(0, (most,))
    least, dx, some = lax.optimization_barrier((least, dx, some))
    ddt, pars, _, _ = final(head_units, units - head_units, least, pars, some, thru, ddt)
    closing = lax.all_to_all(pars, "context", 0, 0)
    dx, db, dc = groups(1, (most, least), dx, db, dc)
    sums = jnp.sum(closing, axis=0)[:3, :heads]
    return dx, db, dc, ddt, sums[0], sums[1], sums[2]


def solution(mesh):
    return jax.shard_map(
        on_device,
        mesh=mesh,
        in_specs=(
            P(None, "context", "tensor"),
            P(None, "context", "tensor"),
            P(None, "context", "tensor"),
            P(None, "tensor", "context"),
            P("tensor"),
            P("tensor"),
            P("tensor"),
            P(None, "context", "tensor"),
            P(None, ("context", "tensor")),
            P(),
        ),
        out_specs=(
            P(None, "context", "tensor"),
            P(None, "context", "tensor"),
            P(None, "context", "tensor"),
            P(None, "tensor", "context"),
            P("tensor"),
            P("tensor"),
            P("tensor"),
        ),
        check_vma=False,
    )
```

```python
import jax
import jax.numpy as jnp
import numpy as np
from jax import lax
from jax.experimental import pallas as pl
from jax.experimental.pallas import tpu as pltpu
from jax.sharding import PartitionSpec as P

HP = 64
NS = 256
QB = 256
HALF = 128
BETA = 0.5
PAIR = 2 * HP
LANES = 8 * HP
TILE = 8
COLS = 4
VMEM = 56 * 1024 * 1024
F32 = jnp.float32
BF16 = jnp.bfloat16
HIGH = lax.Precision.HIGHEST


def dot(lhs, rhs, dims, precision=None):
    return lax.dot_general(
        lhs, rhs, (dims, ((), ())), precision=precision, preferred_element_type=F32
    )


NN = ((1,), (0,))
NT = ((1,), (1,))
TN = ((0,), (0,))


def split3(value):
    top = value.astype(BF16)
    rest = value - top.astype(F32)
    mid = rest.astype(BF16)
    return top, mid, (rest - mid.astype(F32)).astype(BF16)


def softplus(value):
    return jnp.maximum(value, 0.0) + jnp.log1p(jnp.exp(-jnp.abs(value)))


def upper_ones():
    row = lax.broadcasted_iota(jnp.int32, (QB, QB), 0)
    col = lax.broadcasted_iota(jnp.int32, (QB, QB), 1)
    return (row <= col).astype(BF16)


def running_sum(values, ones, dims=NN):
    rows = values.shape[0]
    sums = dot(jnp.concatenate(split3(values), axis=0), ones, dims)
    return sums[:rows] + sums[rows : 2 * rows] + sums[2 * rows :]


def live_rows(base, length, count):
    row = lax.broadcasted_iota(jnp.int32, (count, 1), 0)
    return base + row < length


def column(row_ref):
    heads = row_ref.shape[1]
    same = lax.broadcasted_iota(jnp.int32, (heads, heads), 0) == lax.broadcasted_iota(
        jnp.int32, (heads, heads), 1
    )
    return jnp.sum(jnp.where(same, row_ref[...], 0.0), axis=1, keepdims=True)


def token_base(toks):
    return lax.axis_index("context") * toks


def flat(column_values, lanes):
    heads = column_values.shape[0]
    same = lax.broadcasted_iota(jnp.int32, (heads, lanes), 0) == lax.broadcasted_iota(
        jnp.int32, (heads, lanes), 1
    )
    return jnp.sum(jnp.where(same, column_values, 0.0), axis=0, keepdims=True)


GAP = 32


def scale_columns(tail, grow):
    rows = jnp.concatenate([tail, grow], axis=0)
    parts = [part.astype(F32) for part in split3(rows)]
    return jnp.concatenate(parts + [jnp.zeros_like(rows)], axis=0).T.astype(BF16)


def spreads(heads):
    row, lane = np.arange(128)[:, None], np.arange(heads * HP)[None, :] // HP
    used = row < 3 * GAP
    return np.stack([used & (row % GAP == lane), used & (row % GAP == lane + GAP // 2)])


def gathers(heads):
    lane, col = np.arange(heads * HP)[:, None] // HP, np.arange(128)[None, :]
    return np.stack([lane == col, lane == col - GAP // 2])


def lane_sums(product, ones_part):
    top = product.astype(BF16)
    low = (product - top.astype(F32)).astype(BF16)
    return dot(top, ones_part, NN) + dot(low, ones_part, NN)


def exact_dot(lhs, rhs, dims):
    top = rhs.astype(BF16)
    low = (rhs - top.astype(F32)).astype(BF16)
    return dot(lhs, top, dims) + dot(lhs, low, dims)


def device_sums(step, rate, ones):
    logs = step * rate
    heads = step.shape[0]
    both = running_sum(jnp.concatenate([logs[:, :QB], logs[:, QB:]], axis=0), ones)
    return both[:heads], both[heads:]


def states_kernel(len_ref, x_ref, g_ref, b_ref, c_ref, dt_ref, bias_ref, alog_ref, ratio_ref,
                  spread_ref, out_ref, scal_sc, tile_sc):
    heads = dt_ref.shape[1]
    toks = x_ref.shape[1]
    pieces = out_ref.shape[0]
    piece = NS // pieces
    at = pl.program_id(0)
    work = 2

    @pl.when(at == 0)
    def _():
        ones = upper_ones()
        bias, rate = column(bias_ref), -jnp.exp(column(alog_ref))
        for seq in range(2):
            step = softplus(dt_ref[seq] + bias)
            cums = device_sums(step, rate, ones)
            mid = cums[0][:, QB - 1 : QB]
            last = mid + cums[1][:, QB - 1 : QB]
            for blk in range(2):
                rows = slice(blk * QB, (blk + 1) * QB)
                cum = cums[blk] + blk * mid
                scal_sc[seq, rows] = scale_columns(jnp.exp(last - cum) * step[:, rows], jnp.exp(cum))
            tile_sc[seq : seq + 1] = flat(jnp.exp(last), 128)

    @pl.when(at < work)
    def _():
        scal = scal_sc[at]
        x_tail = x_ref[0].astype(F32) * dot(scal, spread_ref[0], NN)
        live = live_rows(token_base(toks), len_ref[at], toks)
        g_grow = jnp.where(live, g_ref[0].astype(F32) * dot(scal, spread_ref[1], NN), 0.0)
        whole = (exact_dot(b_ref[0].T, x_tail, NN), exact_dot(c_ref[0].T, g_grow, NN))
        for scan in range(2):
            for pair in range(heads // 2):
                row = (2 * pair + scan) * piece
                out_ref[:, row : row + piece] = whole[scan][:, pair * PAIR : (pair + 1) * PAIR].reshape(
                    pieces, piece, PAIR
                )

    @pl.when(at == work)
    def _():
        ratio = ratio_ref[...]
        rows = ratio.shape[1]
        first = lax.axis_index(("context", "tensor")) * rows
        place = lax.broadcasted_iota(jnp.int32, ratio.shape, 1) + first
        seq = lax.broadcasted_iota(jnp.int32, ratio.shape, 0)
        length = jnp.where(seq == 0, len_ref[0], len_ref[1])
        totals = jnp.sum(jnp.where(place < length, ratio, 0.0), axis=1, keepdims=True)
        tile_sc[2:4] = jnp.broadcast_to(totals, (2, 128))
        tile_sc[4:] = jnp.zeros((TILE - 4, 128), F32)
        out_ref[:, 0:TILE] = jnp.broadcast_to(tile_sc[...][None], (pieces, TILE, 128))


def chain_kernel(unit, heads, tile_ref, in_ref, spread_ref, out_ref, sums_ref, decay_sc):
    count = in_ref.shape[0]
    piece = NS // count
    parts = heads * HP // LANES
    at = pl.program_id(0) + unit
    part = lax.rem(at, parts)

    @pl.when(pl.program_id(0) == 0)
    def _():
        tiles = [tile_ref[src] for src in range(count)]
        sums_ref[...] = sum(tiles[1:], tiles[0])
        decay = jnp.concatenate(
            [tile[seq : seq + 1] for seq in range(2) for tile in tiles], axis=0
        )
        top, mid, low = [split.astype(F32) for split in split3(decay)]
        columns = top + pltpu.roll(mid, GAP, 1) + pltpu.roll(low, 2 * GAP, 1)
        wide = dot(columns.astype(BF16), spread_ref[0], NN)
        for seq in range(2):
            for pair in range(heads // 2):
                decay_sc[seq * (heads // 2) + pair] = wide[
                    seq * count : (seq + 1) * count, pair * PAIR : (pair + 1) * PAIR
                ]

    order = np.argsort(snake(count)).tolist()
    pairs = LANES // PAIR
    for pair in range(pairs):
        decay = decay_sc[lax.div(at, parts) * (heads // 2) + part * pairs + pair]
        rows = slice(2 * pair * piece, (2 * pair + 1) * piece)
        total = jnp.zeros((piece, PAIR), F32)
        for src in order:
            out_ref[src, rows] = total
            total = decay[src : src + 1] * total + in_ref[src, rows]
        rows = slice((2 * pair + 1) * piece, (2 * pair + 2) * piece)
        total = jnp.zeros((piece, PAIR), F32)
        for src in reversed(order):
            out_ref[src, rows] = total
            total = decay[src : src + 1] * total + in_ref[src, rows]


def intra_kernel(len_ref, x_ref, g_ref, b_ref, c_ref, dt_ref, bias_ref, alog_ref, gain_ref, spread_ref,
                 gather_ref, dx_ref, db_ref, dc_ref, diff_ref, col_ref, skip_ref, xv_ref, gg_ref, scal_ref, near_ref, aux_ref,
                 y_sc, d_sc, g_sc):
    heads = dt_ref.shape[1]
    seq, blk = pl.program_id(0), pl.program_id(1)
    raw = dt_ref[0] + column(bias_ref)
    step_all = softplus(raw)
    rate = -jnp.exp(column(alog_ref))
    cums = device_sums(step_all, rate, upper_ones())
    first = blk == 0
    cum = jnp.where(first, cums[0], cums[1])
    step = jnp.where(first, step_all[:, :QB], step_all[:, QB:])
    raw = jnp.where(first, raw[:, :QB], raw[:, QB:])
    cum_t = cum.T
    mid, over = cums[0][:, QB - 1 : QB], cums[1][:, QB - 1 : QB]
    slope = jax.nn.sigmoid(raw)
    aux_ref[0, 0] = slope / step
    aux_ref[0, 1] = slope * rate
    aux_ref[0, 2] = step * rate
    tail = jnp.exp(cum[:, QB - 1 : QB] - cum) * step
    grow = jnp.exp(cum)
    near_ref[0] = scale_columns(tail, grow)
    gain = jnp.broadcast_to(column(gain_ref), (heads, TILE))
    gain = dot(scale_columns(gain, gain), spread_ref[0], NN)[0:1]
    tail = jnp.exp(jnp.where(first, mid + over, over) - cum) * step
    grow = jnp.exp(cum + jnp.where(first, 0.0, mid))
    scal = scale_columns(tail, grow)
    scal_ref[0] = scal
    live = live_rows(token_base(pl.num_programs(1) * QB) + blk * QB, len_ref[seq], QB)
    x_full = x_ref[0].astype(F32)
    g_full = jnp.where(live, g_ref[0].astype(F32), 0.0)
    g_sc[...] = g_full.astype(BF16)
    skips = jnp.sum(x_full * g_full, axis=0, keepdims=True)
    skip_ref[0, 0] = lane_sums(jnp.broadcast_to(skips, (TILE, heads * HP)), gather_ref[0])
    xv_ref[0] = (x_full * dot(scal, spread_ref[0], NN)).astype(BF16)
    gg_ref[0] = (g_full * dot(scal, spread_ref[1], NN)).astype(BF16)
    gram = dot(c_ref[0], b_ref[0], NT)
    causal = (
        lax.broadcasted_iota(jnp.int32, (HALF, HALF), 0)
        >= lax.broadcasted_iota(jnp.int32, (HALF, HALF), 1)
    )
    low, high = slice(0, HALF), slice(HALF, QB)
    tiles = ((low, low), (high, low), (high, high))
    grams = [jnp.where(causal, gram[t, k], 0.0) if t is k else gram[t, k] for t, k in tiles]
    left = lax.broadcasted_iota(jnp.int32, (QB, PAIR), 1) < HP
    zero = jnp.zeros((QB, PAIR), BF16)
    dgrams = [jnp.zeros((HALF, HALF), F32) for _ in tiles]
    for pair in range(heads // 2):
        lanes = slice(pair * PAIR, (pair + 1) * PAIR)
        xx = x_ref[0, :, lanes]
        gg = g_sc[:, lanes]
        gs = [jnp.where(left, gg, zero), jnp.where(left, zero, gg)]
        xs = [jnp.where(left, xx, zero), jnp.where(left, zero, xx)]
        weights = []
        for one in range(2):
            head = 2 * pair + one
            mine = []
            dlow = dot(gs[one], xx[low], NT)
            dhigh = dot(gs[one][high], xx[high], NT)
            dparts = (dlow[low], dlow[high], dhigh)
            for which, (t, k) in enumerate(tiles):
                gap = cum_t[t, head : head + 1] - cum[head : head + 1, k]
                if t is k:
                    gap = jnp.minimum(gap, 0.0)
                decay = jnp.exp(gap) * step[head : head + 1, k]
                mine.append((grams[which] * decay).astype(BF16))
                dgrams[which] = dgrams[which] + dparts[which] * decay
            weights.append(mine)
        (a0, a1, a2), (b0, b1, b2) = weights
        y_sc[low, lanes] = dot(
            jnp.concatenate([a0, b0], axis=1), jnp.concatenate([xs[0][low], xs[1][low]], axis=0), NN
        )
        y_sc[high, lanes] = dot(
            jnp.concatenate([a1, a2, b1, b2], axis=1), jnp.concatenate(xs, axis=0), NN
        )
        d_sc[low, lanes] = dot(
            jnp.concatenate([a0, a1, b0, b1], axis=0), jnp.concatenate(gs, axis=0), TN
        )
        d_sc[high, lanes] = dot(
            jnp.concatenate([a2, b2], axis=0),
            jnp.concatenate([gs[0][high], gs[1][high]], axis=0), TN,
        )
    sums = lane_sums(g_full * y_sc[...], gather_ref[0])
    sums = (sums + lane_sums(x_full * d_sc[...], gather_ref[1])).T
    row, col = sums[:heads], sums[heads : 2 * heads]
    diff_ref[0] = row - col
    col_ref[0] = col
    dx_ref[0] = d_sc[...] + gain * g_full
    dgram = jnp.concatenate(
        [
            jnp.concatenate(
                [jnp.where(causal, dgrams[0], 0.0), jnp.zeros((HALF, HALF), F32)], axis=1
            ),
            jnp.concatenate([dgrams[1], jnp.where(causal, dgrams[2], 0.0)], axis=1),
        ],
        axis=0,
    ).astype(BF16)
    dc_ref[0] = dot(dgram, b_ref[0], NN)
    db_ref[0] = dot(dgram, c_ref[0], TN)


def cross_kernel(len_ref, x_ref, g_ref, b_ref, c_ref, near_ref, spread_ref, gather_ref,
                 diff_ref, col_ref, dxi_ref, dbi_ref, dci_ref,
                 dlog_ref, cols_ref, dx_ref, db_ref, dc_ref):
    heads = diff_ref.shape[1]
    seq = pl.program_id(0)
    toks = near_ref.shape[1]
    x_tail = x_ref[0].astype(F32) * dot(near_ref[0, :QB], spread_ref[0], NN)
    live = live_rows(token_base(toks) + QB, len_ref[seq], QB)
    g_grow = jnp.where(live, g_ref[0].astype(F32), 0.0) * dot(near_ref[0, QB:], spread_ref[1], NN)
    early, late = x_tail.astype(BF16), g_grow.astype(BF16)
    b_early, c_late = b_ref[0], c_ref[0]
    gram = dot(c_late, b_early, NT)
    y, back = 0.0, 0.0
    for part in split3(gram)[:2]:
        y = y + exact_dot(part, x_tail, NN)
        back = back + exact_dot(part, g_grow, TN)
    dgram = dot(late, early, NT).astype(BF16)
    dc_ref[0] = dci_ref[0] + dot(dgram, b_early, NN)
    db_ref[0] = dbi_ref[0] + dot(dgram, c_late, TN)
    dx_ref[0] = dxi_ref[0] + dot(near_ref[0, :QB], spread_ref[0], NN) * back
    row = lane_sums(g_grow * y, gather_ref[0]).T[:heads]
    col = lane_sums(x_tail * back, gather_ref[0]).T[:heads]
    ones = upper_ones()
    dlog_ref[0, :, :QB] = (
        running_sum(diff_ref[0, :, :QB], ones, NT) + running_sum(col, ones) - col
    )
    dlog_ref[0, :, QB:] = running_sum(diff_ref[0, :, QB:] + row, ones, NT)
    cols_ref[0, :, :QB] = col_ref[0, :, :QB] + col
    cols_ref[0, :, QB:] = col_ref[0, :, QB:]


def state_of(ends_ref, scan):
    piece = NS // ends_ref.shape[0]
    pairs = ends_ref.shape[1] // (2 * piece)
    return jnp.concatenate(
        [
            ends_ref[:, (2 * p + scan) * piece : (2 * p + scan + 1) * piece].reshape(NS, PAIR)
            for p in range(pairs)
        ],
        axis=1,
    )


def final_kernel(unit, heads, len_ref, gate_ref, x_ref, g_ref, b_ref, c_ref, ends_ref, scal_ref,
                 aux_ref, dlog_ref, cols_ref, skip_ref, spread_ref, gather_ref, *refs):
    ddt_ref, par_ref, part_ref, thru_ref, sum_sc, thru_sc, tile_sc = refs[-7:]
    before = refs[:-7]
    toks = x_ref.shape[1]
    parts = heads * HP // LANES
    at = pl.program_id(0) + unit
    seq, part = lax.div(at, parts), lax.rem(at, parts)
    gate = gate_ref[seq]

    @pl.when(pl.program_id(0) == 0)
    def _():
        tile_sc[...] = before[0][0] if before else jnp.zeros_like(tile_sc)
        if before:
            sum_sc[...] = before[1][...]
            thru_sc[...] = before[2][...]

    @pl.when(part == 0)
    def _():
        sum_sc[...] = jnp.zeros_like(sum_sc)
        thru_sc[...] = jnp.zeros_like(thru_sc)

    enter, leave = state_of(ends_ref, 0), state_of(ends_ref, 1)
    live = live_rows(token_base(toks), len_ref[seq], toks)
    grow = dot(scal_ref[0], spread_ref[1], NN)
    g_grow = jnp.where(live, g_ref[0].astype(F32) * grow, 0.0)
    y = exact_dot(c_ref[0], enter, NN)
    tail = dot(scal_ref[0], spread_ref[0], NN)
    u = tail * exact_dot(b_ref[0], leave, NN)
    sum_sc[...] += lane_sums(g_grow * y, gather_ref[0]) + lane_sums(
        x_ref[0].astype(F32) * u, gather_ref[1]
    )
    product = grow[toks - 1 : toks] * jnp.sum(enter * leave, axis=0, keepdims=True)
    thru_sc[...] += lane_sums(jnp.broadcast_to(product, (TILE, LANES)), gather_ref[0])

    @pl.when(part == parts - 1)
    def _():
        ones = upper_ones()
        halves = [slice(blk * QB, (blk + 1) * QB) for blk in range(2)]
        sums = [sum_sc[rows].T for rows in halves]
        both = jnp.concatenate([half[:heads] for half in sums], axis=0)
        cols = jnp.concatenate([half[heads : 2 * heads] for half in sums], axis=0)
        later = running_sum(both, ones, NT)
        earlier = running_sum(cols, ones)
        thru = thru_sc[...].T[:heads, 0:1]
        rest = (
            later[heads:, 0:1] + thru,
            earlier[:heads, QB - 1 : QB] + thru,
        )
        gb = jnp.zeros((heads, 1), F32)
        ga = jnp.zeros((heads, 1), F32)
        for blk, rows in enumerate(halves):
            mine = slice(blk * heads, (blk + 1) * heads)
            dlog = dlog_ref[0, :, rows] + later[mine] + earlier[mine] - cols[mine] + rest[blk]
            col = cols_ref[0, :, rows] + cols[mine]
            ddt = gate * (aux_ref[0, 0, :, rows] * col + aux_ref[0, 1, :, rows] * dlog)
            ddt_ref[0, :, rows] = ddt
            gb = gb + jnp.sum(ddt, axis=1, keepdims=True)
            ga = ga + gate * jnp.sum(aux_ref[0, 2, :, rows] * dlog, axis=1, keepdims=True)
        skips = gate * (skip_ref[0, 0] + skip_ref[0, 1])
        rows = [flat(ga, 128), flat(gb, 128), skips[0:1]]
        tile_sc[...] += jnp.concatenate(rows + [jnp.zeros((TILE - 3, 128), F32)], axis=0)

    @pl.when(pl.program_id(0) == pl.num_programs(0) - 1)
    def _():
        par_ref[...] = jnp.broadcast_to(tile_sc[...][None], par_ref.shape)
        part_ref[...] = sum_sc[...]
        thru_ref[...] = thru_sc[...]


def groups_kernel(seq, gate_ref, b_ref, scal_ref, xv_ref, gg_ref, dxi_ref, dbi_ref, dci_ref,
                  spread_ref, *refs):
    dx_ref, db_ref, dc_ref, db_sc, dc_sc = refs[-5:]
    ends = refs[:2] if seq else refs[:1]
    part = pl.program_id(0)
    gate = gate_ref[seq]

    @pl.when(part == 0)
    def _():
        db_sc[...] = dbi_ref[0]
        dc_sc[...] = dci_ref[0]

    def add(ends_ref):
        enter = state_of(ends_ref, 0).astype(BF16)
        leave = state_of(ends_ref, 1).astype(BF16)
        db_sc[...] += dot(xv_ref[0], leave, NT)
        dc_sc[...] += dot(gg_ref[0], enter, NT)
        u = dot(scal_ref[0], spread_ref[0], NN) * dot(b_ref[0], leave, NN)
        dx_ref[0] = (gate * (dxi_ref[0] + u)).astype(BF16)

    if seq:
        pl.when(part == 0)(lambda: add(ends[0]))
        pl.when(part == 1)(lambda: add(ends[1]))
    else:
        add(ends[0])

    @pl.when(part == pl.num_programs(0) - 1)
    def _():
        db_ref[0] = (gate * db_sc[...]).astype(BF16)
        dc_ref[0] = (gate * dc_sc[...]).astype(BF16)


def snake(count):
    return [
        COLS * y + (x if y % 2 == 0 else COLS - 1 - x)
        for y in range(count // COLS)
        for x in range(COLS)
    ]


def exchange(value):
    order = snake(lax.axis_size("context"))
    return lax.all_to_all(value, "context", 0, 0, axis_index_groups=[order])


def sum_tensor(value):
    count = lax.axis_size("tensor")
    if count == 1:
        return value
    value = value + lax.ppermute(value, "tensor", [(i, i ^ 1) for i in range(count)])
    parts = [
        lax.ppermute(value, "tensor", [(i, (i + 2 * turn) % count) for i in range(count)])
        for turn in range(1, count // 2)
    ]
    return sum(parts, value)


def on_device(
    seq_inputs, b_proj, c_proj, dt_raw, dt_bias, a_log, d_skip, out_grad, log_ratio, lengths
):
    seqs, toks, width = seq_inputs.shape
    heads = dt_bias.shape[0]
    count = lax.axis_size("context")
    parts = width // LANES
    units = seqs * parts
    head_units = units - 1
    chunk = 2 * (LANES // PAIR) * (NS // count)
    spread_ones = jnp.asarray(spreads(heads), BF16)
    gather_ones = jnp.asarray(gathers(heads), BF16)
    bias_row, alog_row, gain_row = dt_bias[None], a_log[None], d_skip[None]
    smem = pl.BlockSpec(memory_space=pltpu.SMEM)
    anywhere = pl.BlockSpec(memory_space=pl.ANY)
    params = pltpu.CompilerParams(vmem_limit_bytes=VMEM)
    whole = lambda *shape: pl.BlockSpec(shape, lambda *at: (0,) * len(shape))
    small = [whole(1, heads), whole(1, heads)]

    of_either = lambda *shape: pl.BlockSpec(
        (1,) + shape, lambda i: (jnp.minimum(i, seqs - 1),) + (0,) * len(shape)
    )
    local = pl.pallas_call(
        states_kernel,
        grid=(seqs + 1,),
        in_specs=[
            smem, of_either(toks, width), of_either(toks, width), of_either(toks, NS),
            of_either(toks, NS), whole(*dt_raw.shape), *small, whole(*log_ratio.shape),
            whole(2, 128, width),
        ],
        out_specs=pl.BlockSpec((count, parts * chunk, PAIR), lambda i: (0, i, 0)),
        out_shape=jax.ShapeDtypeStruct((count, units * chunk + TILE, PAIR), F32),
        scratch_shapes=[pltpu.VMEM((seqs, toks, 128), BF16), pltpu.VMEM((TILE, 128), F32)],
        compiler_params=params,
        name="states",
    )(lengths, seq_inputs, out_grad, b_proj, c_proj, dt_raw, bias_row, alog_row, log_ratio,
      spread_ones)

    owned = exchange(local)

    def chained(unit, number):
        return pl.pallas_call(
            lambda *refs: chain_kernel(unit, heads, *refs),
            grid=(number,),
            in_specs=[
                pl.BlockSpec((count, TILE, PAIR), lambda i: (0, units * chunk // TILE, 0)),
                pl.BlockSpec((count, chunk, PAIR), lambda i: (0, i + unit, 0)),
                whole(2, 128, width),
            ],
            out_specs=[pl.BlockSpec((count, chunk, PAIR), lambda i: (0, i, 0)), whole(TILE, 128)],
            out_shape=[
                jax.ShapeDtypeStruct((count, number * chunk, PAIR), F32),
                jax.ShapeDtypeStruct((TILE, 128), F32),
            ],
            scratch_shapes=[pltpu.VMEM((seqs * heads // 2, count, PAIR), F32)],
            compiler_params=params,
            name="chain",
        )(owned, owned, spread_ones)

    most, sums = chained(0, head_units)
    most, dt_raw = lax.optimization_barrier((most, dt_raw))
    most = exchange(most)

    tok_spec = lambda w: pl.BlockSpec((1, QB, w), lambda s, b: (s, b, 0))
    head_spec = pl.BlockSpec((1, heads, QB), lambda s, b: (s, 0, b))
    blocks = toks // QB
    dxi, dbi, dci, diff, col, skips, xv, gg, scal, near, aux = pl.pallas_call(
        intra_kernel,
        grid=(seqs, blocks),
        in_specs=[smem, tok_spec(width), tok_spec(width), tok_spec(NS), tok_spec(NS),
                  pl.BlockSpec((1, heads, toks), lambda s, b: (s, 0, 0)), *small, whole(1, heads),
                  whole(2, 128, width), whole(2, width, 128)],
        out_specs=[tok_spec(width), tok_spec(NS), tok_spec(NS), head_spec, head_spec,
                   pl.BlockSpec((1, 1, TILE, 128), lambda s, b: (s, b, 0, 0)),
                   tok_spec(width), tok_spec(width), tok_spec(128), tok_spec(128),
                   pl.BlockSpec((1, 3, heads, QB), lambda s, b: (s, 0, 0, b))],
        out_shape=[
            jax.ShapeDtypeStruct((seqs, toks, width), F32),
            jax.ShapeDtypeStruct((seqs, toks, NS), F32),
            jax.ShapeDtypeStruct((seqs, toks, NS), F32),
            jax.ShapeDtypeStruct((seqs, heads, toks), F32),
            jax.ShapeDtypeStruct((seqs, heads, toks), F32),
            jax.ShapeDtypeStruct((seqs, blocks, TILE, 128), F32),
            jax.ShapeDtypeStruct((seqs, toks, width), BF16),
            jax.ShapeDtypeStruct((seqs, toks, width), BF16),
            jax.ShapeDtypeStruct((seqs, toks, 128), BF16),
            jax.ShapeDtypeStruct((seqs, toks, 128), BF16),
            jax.ShapeDtypeStruct((seqs, 3, heads, toks), F32),
        ],
        scratch_shapes=[
            pltpu.VMEM((QB, width), F32), pltpu.VMEM((QB, width), F32),
            pltpu.VMEM((QB, width), BF16),
        ],
        compiler_params=params,
        name="intra",
    )(lengths, seq_inputs, out_grad, b_proj, c_proj, dt_raw, bias_row, alog_row, gain_row,
      spread_ones, gather_ones)

    of_seq = lambda *shape: pl.BlockSpec((1,) + shape, lambda i: (i,) + (0,) * len(shape))
    early = lambda w: pl.BlockSpec((1, QB, w), lambda i: (i, 0, 0))
    late = lambda w: pl.BlockSpec((1, QB, w), lambda i: (i, 1, 0))
    dlog, cols, dxi, dbi, dci = pl.pallas_call(
        cross_kernel,
        grid=(seqs,),
        in_specs=[smem, early(width), late(width), early(NS), late(NS), of_seq(toks, 128),
                  whole(2, 128, width), whole(2, width, 128), of_seq(heads, toks),
                  of_seq(heads, toks), early(width), early(NS), late(NS)],
        out_specs=[of_seq(heads, toks), of_seq(heads, toks), early(width), early(NS), late(NS)],
        out_shape=[
            jax.ShapeDtypeStruct((seqs, heads, toks), F32),
            jax.ShapeDtypeStruct((seqs, heads, toks), F32),
            jax.ShapeDtypeStruct((seqs, toks, width), F32),
            jax.ShapeDtypeStruct((seqs, toks, NS), F32),
            jax.ShapeDtypeStruct((seqs, toks, NS), F32),
        ],
        input_output_aliases={10: 2, 11: 3, 12: 4},
        compiler_params=params,
        name="cross",
    )(lengths, seq_inputs, out_grad, b_proj, c_proj, near, spread_ones, gather_ones, diff, col,
      dxi, dbi, dci)

    least, _ = chained(head_units, units - head_units)
    totals = sum_tensor(sums[2:4])[:, 0]
    signs = jnp.where(jnp.arange(2, dtype=jnp.int32) == 0, -1.0, 1.0).astype(F32)
    margin = -jnp.sum(signs * totals)
    gate = signs * BETA * jax.nn.sigmoid(-BETA * margin)
    least, gate, dxi = lax.optimization_barrier((least, gate, dxi))
    least = exchange(least)

    def final(unit, number, back, *before):
        at_seq = lambda *shape: pl.BlockSpec(
            (1,) + shape, lambda i: ((i + unit) // parts,) + (0,) * len(shape)
        )
        laned = pl.BlockSpec(
            (1, toks, LANES), lambda i: ((i + unit) // parts, 0, (i + unit) % parts)
        )
        return pl.pallas_call(
            lambda *refs: final_kernel(unit, heads, *refs),
            grid=(number,),
            in_specs=[
                smem, smem, laned, laned, at_seq(toks, NS), at_seq(toks, NS),
                pl.BlockSpec((count, chunk, PAIR), lambda i: (0, i, 0)),
                at_seq(toks, 128), at_seq(3, heads, toks), at_seq(heads, toks),
                at_seq(heads, toks), at_seq(blocks, TILE, 128),
                pl.BlockSpec((2, 128, LANES), lambda i: (0, 0, (i + unit) % parts)),
                pl.BlockSpec((2, LANES, 128), lambda i: (0, (i + unit) % parts, 0)),
            ] + ([whole(1, TILE, 128), whole(toks, 128), whole(TILE, 128), anywhere] if before else []),
            out_specs=[at_seq(heads, toks), whole(count, TILE, 128), whole(toks, 128),
                       whole(TILE, 128)],
            out_shape=[
                jax.ShapeDtypeStruct((seqs, heads, toks), F32),
                jax.ShapeDtypeStruct((count, TILE, 128), F32),
                jax.ShapeDtypeStruct((toks, 128), F32),
                jax.ShapeDtypeStruct((TILE, 128), F32),
            ],
            scratch_shapes=[pltpu.VMEM((toks, 128), F32), pltpu.VMEM((TILE, 128), F32),
                            pltpu.VMEM((TILE, 128), F32)],
            input_output_aliases={17: 0} if before else {},
            compiler_params=params,
            name="final",
        )(lengths, gate, seq_inputs, out_grad, b_proj, c_proj, back, scal, aux, dlog, cols, skips,
          spread_ones, gather_ones, *before)

    def groups(seq, states, *before):
        of_seq = lambda *shape: pl.BlockSpec((1,) + shape, lambda p: (seq,) + (0,) * len(shape))
        laned = pl.BlockSpec((1, toks, LANES), lambda p: (seq, 0, p))
        if seq:
            last = pl.BlockSpec((count, chunk, PAIR), lambda p: (0, 0, 0))
            ends = [pl.BlockSpec((count, chunk, PAIR), lambda p: (0, head_units - 1, 0)), last]
        else:
            ends = [pl.BlockSpec((count, chunk, PAIR), lambda p: (0, p, 0))]
        return pl.pallas_call(
            lambda *refs: groups_kernel(seq, *refs),
            grid=(parts,),
            in_specs=[smem, of_seq(toks, NS), of_seq(toks, 128), laned, laned, laned,
                      of_seq(toks, NS), of_seq(toks, NS),
                      pl.BlockSpec((2, 128, LANES), lambda p: (0, 0, p))]
            + ends + [anywhere] * len(before),
            out_specs=[laned, of_seq(toks, NS), of_seq(toks, NS)],
            out_shape=[jax.ShapeDtypeStruct((seqs, toks, w), BF16) for w in (width, NS, NS)],
            scratch_shapes=[pltpu.VMEM((toks, NS), F32), pltpu.VMEM((toks, NS), F32)],
            input_output_aliases={9 + len(ends) + k: k for k in range(len(before))},
            compiler_params=params,
            name="groups",
        )(gate, b_proj, scal, xv, gg, dxi, dbi, dci, spread_ones, *states, *before)

    ddt, pars, some, thru = final(0, head_units, most)
    dx, db, dc = groups(0, (most,))
    least, dx, some = lax.optimization_barrier((least, dx, some))
    ddt, pars, _, _ = final(head_units, units - head_units, least, pars, some, thru, ddt)
    closing = exchange(pars)
    dx, db, dc = groups(1, (most, least), dx, db, dc)
    sums = jnp.sum(closing, axis=0)[:3, :heads]
    return dx, db, dc, ddt, sums[0], sums[1], sums[2]


def solution(mesh):
    return jax.shard_map(
        on_device,
        mesh=mesh,
        in_specs=(
            P(None, "context", "tensor"),
            P(None, "context", "tensor"),
            P(None, "context", "tensor"),
            P(None, "tensor", "context"),
            P("tensor"),
            P("tensor"),
            P("tensor"),
            P(None, "context", "tensor"),
            P(None, ("context", "tensor")),
            P(),
        ),
        out_specs=(
            P(None, "context", "tensor"),
            P(None, "context", "tensor"),
            P(None, "context", "tensor"),
            P(None, "tensor", "context"),
            P("tensor"),
            P("tensor"),
            P("tensor"),
        ),
        check_vma=False,
    )
```

```python
import jax
import jax.numpy as jnp
import numpy as np
from jax import lax
from jax.experimental import pallas as pl
from jax.experimental.pallas import tpu as pltpu
from jax.sharding import PartitionSpec as P

HP = 64
NS = 256
QB = 256
HALF = 128
BETA = 0.5
PAIR = 2 * HP
LANES = 8 * HP
TILE = 8
COLS = 4
VMEM = 56 * 1024 * 1024
F32 = jnp.float32
BF16 = jnp.bfloat16
HIGH = lax.Precision.HIGHEST


def dot(lhs, rhs, dims, precision=None):
    return lax.dot_general(
        lhs, rhs, (dims, ((), ())), precision=precision, preferred_element_type=F32
    )


NN = ((1,), (0,))
NT = ((1,), (1,))
TN = ((0,), (0,))


def split3(value):
    top = value.astype(BF16)
    rest = value - top.astype(F32)
    mid = rest.astype(BF16)
    return top, mid, (rest - mid.astype(F32)).astype(BF16)


def softplus(value):
    return jnp.maximum(value, 0.0) + jnp.log1p(jnp.exp(-jnp.abs(value)))


def upper_ones():
    row = lax.broadcasted_iota(jnp.int32, (QB, QB), 0)
    col = lax.broadcasted_iota(jnp.int32, (QB, QB), 1)
    return (row <= col).astype(BF16)


def running_sum(values, ones, dims=NN):
    rows = values.shape[0]
    sums = dot(jnp.concatenate(split3(values), axis=0), ones, dims)
    return sums[:rows] + sums[rows : 2 * rows] + sums[2 * rows :]


def live_rows(base, length, count):
    row = lax.broadcasted_iota(jnp.int32, (count, 1), 0)
    return base + row < length


def column(row_ref):
    heads = row_ref.shape[1]
    same = lax.broadcasted_iota(jnp.int32, (heads, heads), 0) == lax.broadcasted_iota(
        jnp.int32, (heads, heads), 1
    )
    return jnp.sum(jnp.where(same, row_ref[...], 0.0), axis=1, keepdims=True)


def token_base(toks):
    return lax.axis_index("context") * toks


def flat(column_values, lanes):
    heads = column_values.shape[0]
    same = lax.broadcasted_iota(jnp.int32, (heads, lanes), 0) == lax.broadcasted_iota(
        jnp.int32, (heads, lanes), 1
    )
    return jnp.sum(jnp.where(same, column_values, 0.0), axis=0, keepdims=True)


GAP = 32


def scale_columns(tail, grow):
    rows = jnp.concatenate([tail, grow], axis=0)
    parts = [part.astype(F32) for part in split3(rows)]
    return jnp.concatenate(parts + [jnp.zeros_like(rows)], axis=0).T.astype(BF16)


def spreads(heads):
    row, lane = np.arange(128)[:, None], np.arange(heads * HP)[None, :] // HP
    used = row < 3 * GAP
    return np.stack([used & (row % GAP == lane), used & (row % GAP == lane + GAP // 2)])


def gathers(heads):
    lane, col = np.arange(heads * HP)[:, None] // HP, np.arange(128)[None, :]
    return np.stack([lane == col, lane == col - GAP // 2])


def lane_sums(product, ones_part):
    top = product.astype(BF16)
    low = (product - top.astype(F32)).astype(BF16)
    return dot(top, ones_part, NN) + dot(low, ones_part, NN)


def exact_dot(lhs, rhs, dims):
    top = rhs.astype(BF16)
    low = (rhs - top.astype(F32)).astype(BF16)
    return dot(lhs, top, dims) + dot(lhs, low, dims)


def device_sums(step, rate, ones):
    logs = step * rate
    heads = step.shape[0]
    both = running_sum(jnp.concatenate([logs[:, :QB], logs[:, QB:]], axis=0), ones)
    return both[:heads], both[heads:]


def states_kernel(len_ref, x_ref, g_ref, b_ref, c_ref, dt_ref, bias_ref, alog_ref, ratio_ref,
                  spread_ref, out_ref, scal_sc, tile_sc):
    heads = dt_ref.shape[1]
    toks = x_ref.shape[1]
    pieces = out_ref.shape[0]
    piece = NS // pieces
    at = pl.program_id(0)
    work = 2

    @pl.when(at == 0)
    def _():
        ones = upper_ones()
        bias, rate = column(bias_ref), -jnp.exp(column(alog_ref))
        for seq in range(2):
            step = softplus(dt_ref[seq] + bias)
            cums = device_sums(step, rate, ones)
            mid = cums[0][:, QB - 1 : QB]
            last = mid + cums[1][:, QB - 1 : QB]
            for blk in range(2):
                rows = slice(blk * QB, (blk + 1) * QB)
                cum = cums[blk] + blk * mid
                scal_sc[seq, rows] = scale_columns(jnp.exp(last - cum) * step[:, rows], jnp.exp(cum))
            tile_sc[seq : seq + 1] = flat(jnp.exp(last), 128)

    @pl.when(at < work)
    def _():
        scal = scal_sc[at]
        x_tail = x_ref[0].astype(F32) * dot(scal, spread_ref[0], NN)
        live = live_rows(token_base(toks), len_ref[at], toks)
        g_grow = jnp.where(live, g_ref[0].astype(F32) * dot(scal, spread_ref[1], NN), 0.0)
        whole = (exact_dot(b_ref[0].T, x_tail, NN), exact_dot(c_ref[0].T, g_grow, NN))
        for scan in range(2):
            for pair in range(heads // 2):
                row = (2 * pair + scan) * piece
                out_ref[:, row : row + piece] = whole[scan][:, pair * PAIR : (pair + 1) * PAIR].reshape(
                    pieces, piece, PAIR
                )

    @pl.when(at == work)
    def _():
        ratio = ratio_ref[...]
        rows = ratio.shape[1]
        first = lax.axis_index(("context", "tensor")) * rows
        place = lax.broadcasted_iota(jnp.int32, ratio.shape, 1) + first
        seq = lax.broadcasted_iota(jnp.int32, ratio.shape, 0)
        length = jnp.where(seq == 0, len_ref[0], len_ref[1])
        totals = jnp.sum(jnp.where(place < length, ratio, 0.0), axis=1, keepdims=True)
        tile_sc[2:4] = jnp.broadcast_to(totals, (2, 128))
        tile_sc[4:] = jnp.zeros((TILE - 4, 128), F32)
        out_ref[:, 0:TILE] = jnp.broadcast_to(tile_sc[...][None], (pieces, TILE, 128))


def chain_kernel(unit, heads, tile_ref, in_ref, spread_ref, out_ref, sums_ref, decay_sc):
    count = in_ref.shape[0]
    piece = NS // count
    parts = heads * HP // LANES
    at = pl.program_id(0) + unit
    part = lax.rem(at, parts)

    @pl.when(pl.program_id(0) == 0)
    def _():
        tiles = [tile_ref[src] for src in range(count)]
        sums_ref[...] = sum(tiles[1:], tiles[0])
        decay = jnp.concatenate(
            [tile[seq : seq + 1] for seq in range(2) for tile in tiles], axis=0
        )
        top, mid, low = [split.astype(F32) for split in split3(decay)]
        columns = top + pltpu.roll(mid, GAP, 1) + pltpu.roll(low, 2 * GAP, 1)
        wide = dot(columns.astype(BF16), spread_ref[0], NN)
        for seq in range(2):
            for pair in range(heads // 2):
                decay_sc[seq * (heads // 2) + pair] = wide[
                    seq * count : (seq + 1) * count, pair * PAIR : (pair + 1) * PAIR
                ]

    came, goes = np.argsort(backwards(count)).tolist(), np.argsort(snake(count)).tolist()
    order = list(zip(came, goes))
    pairs = LANES // PAIR
    for pair in range(pairs):
        decay = decay_sc[lax.div(at, parts) * (heads // 2) + part * pairs + pair]
        rows = slice(2 * pair * piece, (2 * pair + 1) * piece)
        total = jnp.zeros((piece, PAIR), F32)
        for src, dst in order:
            out_ref[dst, rows] = total
            total = decay[src : src + 1] * total + in_ref[src, rows]
        rows = slice((2 * pair + 1) * piece, (2 * pair + 2) * piece)
        total = jnp.zeros((piece, PAIR), F32)
        for src, dst in reversed(order):
            out_ref[dst, rows] = total
            total = decay[src : src + 1] * total + in_ref[src, rows]


def intra_kernel(len_ref, x_ref, g_ref, b_ref, c_ref, dt_ref, bias_ref, alog_ref, gain_ref, spread_ref,
                 gather_ref, dx_ref, db_ref, dc_ref, diff_ref, col_ref, skip_ref, xv_ref, gg_ref, scal_ref, near_ref, aux_ref,
                 y_sc, d_sc, g_sc):
    heads = dt_ref.shape[1]
    seq, blk = pl.program_id(0), pl.program_id(1)
    raw = dt_ref[0] + column(bias_ref)
    step_all = softplus(raw)
    rate = -jnp.exp(column(alog_ref))
    cums = device_sums(step_all, rate, upper_ones())
    first = blk == 0
    cum = jnp.where(first, cums[0], cums[1])
    step = jnp.where(first, step_all[:, :QB], step_all[:, QB:])
    raw = jnp.where(first, raw[:, :QB], raw[:, QB:])
    cum_t = cum.T
    mid, over = cums[0][:, QB - 1 : QB], cums[1][:, QB - 1 : QB]
    slope = jax.nn.sigmoid(raw)
    aux_ref[0, 0] = slope / step
    aux_ref[0, 1] = slope * rate
    aux_ref[0, 2] = step * rate
    tail = jnp.exp(cum[:, QB - 1 : QB] - cum) * step
    grow = jnp.exp(cum)
    near_ref[0] = scale_columns(tail, grow)
    gain = jnp.broadcast_to(column(gain_ref), (heads, TILE))
    gain = dot(scale_columns(gain, gain), spread_ref[0], NN)[0:1]
    tail = jnp.exp(jnp.where(first, mid + over, over) - cum) * step
    grow = jnp.exp(cum + jnp.where(first, 0.0, mid))
    scal = scale_columns(tail, grow)
    scal_ref[0] = scal
    live = live_rows(token_base(pl.num_programs(1) * QB) + blk * QB, len_ref[seq], QB)
    x_full = x_ref[0].astype(F32)
    g_full = jnp.where(live, g_ref[0].astype(F32), 0.0)
    g_sc[...] = g_full.astype(BF16)
    skips = jnp.sum(x_full * g_full, axis=0, keepdims=True)
    skip_ref[0, 0] = lane_sums(jnp.broadcast_to(skips, (TILE, heads * HP)), gather_ref[0])
    xv_ref[0] = (x_full * dot(scal, spread_ref[0], NN)).astype(BF16)
    gg_ref[0] = (g_full * dot(scal, spread_ref[1], NN)).astype(BF16)
    gram = dot(c_ref[0], b_ref[0], NT)
    causal = (
        lax.broadcasted_iota(jnp.int32, (HALF, HALF), 0)
        >= lax.broadcasted_iota(jnp.int32, (HALF, HALF), 1)
    )
    low, high = slice(0, HALF), slice(HALF, QB)
    tiles = ((low, low), (high, low), (high, high))
    grams = [jnp.where(causal, gram[t, k], 0.0) if t is k else gram[t, k] for t, k in tiles]
    left = lax.broadcasted_iota(jnp.int32, (QB, PAIR), 1) < HP
    zero = jnp.zeros((QB, PAIR), BF16)
    dgrams = [jnp.zeros((HALF, HALF), F32) for _ in tiles]
    for pair in range(heads // 2):
        lanes = slice(pair * PAIR, (pair + 1) * PAIR)
        xx = x_ref[0, :, lanes]
        gg = g_sc[:, lanes]
        gs = [jnp.where(left, gg, zero), jnp.where(left, zero, gg)]
        xs = [jnp.where(left, xx, zero), jnp.where(left, zero, xx)]
        weights = []
        for one in range(2):
            head = 2 * pair + one
            mine = []
            dlow = dot(gs[one], xx[low], NT)
            dhigh = dot(gs[one][high], xx[high], NT)
            dparts = (dlow[low], dlow[high], dhigh)
            for which, (t, k) in enumerate(tiles):
                gap = cum_t[t, head : head + 1] - cum[head : head + 1, k]
                if t is k:
                    gap = jnp.minimum(gap, 0.0)
                decay = jnp.exp(gap) * step[head : head + 1, k]
                mine.append((grams[which] * decay).astype(BF16))
                dgrams[which] = dgrams[which] + dparts[which] * decay
            weights.append(mine)
        (a0, a1, a2), (b0, b1, b2) = weights
        y_sc[low, lanes] = dot(
            jnp.concatenate([a0, b0], axis=1), jnp.concatenate([xs[0][low], xs[1][low]], axis=0), NN
        )
        y_sc[high, lanes] = dot(
            jnp.concatenate([a1, a2, b1, b2], axis=1), jnp.concatenate(xs, axis=0), NN
        )
        d_sc[low, lanes] = dot(
            jnp.concatenate([a0, a1, b0, b1], axis=0), jnp.concatenate(gs, axis=0), TN
        )
        d_sc[high, lanes] = dot(
            jnp.concatenate([a2, b2], axis=0),
            jnp.concatenate([gs[0][high], gs[1][high]], axis=0), TN,
        )
    sums = lane_sums(g_full * y_sc[...], gather_ref[0])
    sums = (sums + lane_sums(x_full * d_sc[...], gather_ref[1])).T
    row, col = sums[:heads], sums[heads : 2 * heads]
    diff_ref[0] = row - col
    col_ref[0] = col
    dx_ref[0] = d_sc[...] + gain * g_full
    dgram = jnp.concatenate(
        [
            jnp.concatenate(
                [jnp.where(causal, dgrams[0], 0.0), jnp.zeros((HALF, HALF), F32)], axis=1
            ),
            jnp.concatenate([dgrams[1], jnp.where(causal, dgrams[2], 0.0)], axis=1),
        ],
        axis=0,
    ).astype(BF16)
    dc_ref[0] = dot(dgram, b_ref[0], NN)
    db_ref[0] = dot(dgram, c_ref[0], TN)


def cross_kernel(len_ref, x_ref, g_ref, b_ref, c_ref, near_ref, spread_ref, gather_ref,
                 diff_ref, col_ref, dxi_ref, dbi_ref, dci_ref,
                 dlog_ref, cols_ref, dx_ref, db_ref, dc_ref):
    heads = diff_ref.shape[1]
    seq = pl.program_id(0)
    toks = near_ref.shape[1]
    x_tail = x_ref[0].astype(F32) * dot(near_ref[0, :QB], spread_ref[0], NN)
    live = live_rows(token_base(toks) + QB, len_ref[seq], QB)
    g_grow = jnp.where(live, g_ref[0].astype(F32), 0.0) * dot(near_ref[0, QB:], spread_ref[1], NN)
    early, late = x_tail.astype(BF16), g_grow.astype(BF16)
    b_early, c_late = b_ref[0], c_ref[0]
    gram = dot(c_late, b_early, NT)
    top, low, _ = split3(gram)
    y = exact_dot(top, x_tail, NN) + dot(low, early, NN)
    back = exact_dot(top, g_grow, TN) + dot(low, late, TN)
    dgram = dot(late, early, NT).astype(BF16)
    dc_ref[0] = dci_ref[0] + dot(dgram, b_early, NN)
    db_ref[0] = dbi_ref[0] + dot(dgram, c_late, TN)
    dx_ref[0] = dxi_ref[0] + dot(near_ref[0, :QB], spread_ref[0], NN) * back
    row = lane_sums(g_grow * y, gather_ref[0]).T[:heads]
    col = lane_sums(x_tail * back, gather_ref[0]).T[:heads]
    ones = upper_ones()
    dlog_ref[0, :, :QB] = (
        running_sum(diff_ref[0, :, :QB], ones, NT) + running_sum(col, ones) - col
    )
    dlog_ref[0, :, QB:] = running_sum(diff_ref[0, :, QB:] + row, ones, NT)
    cols_ref[0, :, :QB] = col_ref[0, :, :QB] + col
    cols_ref[0, :, QB:] = col_ref[0, :, QB:]


def state_of(ends_ref, scan):
    count = ends_ref.shape[0]
    piece = NS // count
    pairs = ends_ref.shape[1] // (2 * piece)
    goes = np.argsort(snake(count))
    places = [int(goes[owner]) for owner in backwards(count)]
    columns = []
    for pair in range(pairs):
        rows = slice((2 * pair + scan) * piece, (2 * pair + scan + 1) * piece)
        columns.append(jnp.concatenate([ends_ref[place, rows] for place in places], axis=0))
    return jnp.concatenate(columns, axis=1)


def final_kernel(unit, heads, len_ref, gate_ref, x_ref, g_ref, b_ref, c_ref, ends_ref, scal_ref,
                 aux_ref, dlog_ref, cols_ref, skip_ref, spread_ref, gather_ref, *refs):
    ddt_ref, par_ref, part_ref, thru_ref, sum_sc, thru_sc, tile_sc = refs[-7:]
    before = refs[:-7]
    toks = x_ref.shape[1]
    parts = heads * HP // LANES
    at = pl.program_id(0) + unit
    seq, part = lax.div(at, parts), lax.rem(at, parts)
    gate = gate_ref[seq]

    @pl.when(pl.program_id(0) == 0)
    def _():
        tile_sc[...] = before[0][0] if before else jnp.zeros_like(tile_sc)
        if before:
            sum_sc[...] = before[1][...]
            thru_sc[...] = before[2][...]

    @pl.when(part == 0)
    def _():
        sum_sc[...] = jnp.zeros_like(sum_sc)
        thru_sc[...] = jnp.zeros_like(thru_sc)

    enter, leave = state_of(ends_ref, 0), state_of(ends_ref, 1)
    live = live_rows(token_base(toks), len_ref[seq], toks)
    grow = dot(scal_ref[0], spread_ref[1], NN)
    g_grow = jnp.where(live, g_ref[0].astype(F32) * grow, 0.0)
    y = exact_dot(c_ref[0], enter, NN)
    tail = dot(scal_ref[0], spread_ref[0], NN)
    u = tail * exact_dot(b_ref[0], leave, NN)
    sum_sc[...] += lane_sums(g_grow * y, gather_ref[0]) + lane_sums(
        x_ref[0].astype(F32) * u, gather_ref[1]
    )
    product = grow[toks - 1 : toks] * jnp.sum(enter * leave, axis=0, keepdims=True)
    thru_sc[...] += lane_sums(jnp.broadcast_to(product, (TILE, LANES)), gather_ref[0])

    @pl.when(part == parts - 1)
    def _():
        ones = upper_ones()
        halves = [slice(blk * QB, (blk + 1) * QB) for blk in range(2)]
        sums = [sum_sc[rows].T for rows in halves]
        both = jnp.concatenate([half[:heads] for half in sums], axis=0)
        cols = jnp.concatenate([half[heads : 2 * heads] for half in sums], axis=0)
        later = running_sum(both, ones, NT)
        earlier = running_sum(cols, ones)
        thru = thru_sc[...].T[:heads, 0:1]
        rest = (
            later[heads:, 0:1] + thru,
            earlier[:heads, QB - 1 : QB] + thru,
        )
        gb = jnp.zeros((heads, 1), F32)
        ga = jnp.zeros((heads, 1), F32)
        for blk, rows in enumerate(halves):
            mine = slice(blk * heads, (blk + 1) * heads)
            dlog = dlog_ref[0, :, rows] + later[mine] + earlier[mine] - cols[mine] + rest[blk]
            col = cols_ref[0, :, rows] + cols[mine]
            ddt = gate * (aux_ref[0, 0, :, rows] * col + aux_ref[0, 1, :, rows] * dlog)
            ddt_ref[0, :, rows] = ddt
            gb = gb + jnp.sum(ddt, axis=1, keepdims=True)
            ga = ga + gate * jnp.sum(aux_ref[0, 2, :, rows] * dlog, axis=1, keepdims=True)
        skips = gate * (skip_ref[0, 0] + skip_ref[0, 1])
        rows = [flat(ga, 128), flat(gb, 128), skips[0:1]]
        tile_sc[...] += jnp.concatenate(rows + [jnp.zeros((TILE - 3, 128), F32)], axis=0)

    @pl.when(pl.program_id(0) == pl.num_programs(0) - 1)
    def _():
        par_ref[...] = jnp.broadcast_to(tile_sc[...][None], par_ref.shape)
        part_ref[...] = sum_sc[...]
        thru_ref[...] = thru_sc[...]


def groups_kernel(seq, gate_ref, b_ref, scal_ref, xv_ref, gg_ref, dxi_ref, dbi_ref, dci_ref,
                  spread_ref, *refs):
    dx_ref, db_ref, dc_ref, db_sc, dc_sc = refs[-5:]
    ends = refs[:2] if seq else refs[:1]
    part = pl.program_id(0)
    gate = gate_ref[seq]

    @pl.when(part == 0)
    def _():
        db_sc[...] = dbi_ref[0]
        dc_sc[...] = dci_ref[0]

    def add(ends_ref):
        enter = state_of(ends_ref, 0).astype(BF16)
        leave = state_of(ends_ref, 1).astype(BF16)
        db_sc[...] += dot(xv_ref[0], leave, NT)
        dc_sc[...] += dot(gg_ref[0], enter, NT)
        u = dot(scal_ref[0], spread_ref[0], NN) * dot(b_ref[0], leave, NN)
        dx_ref[0] = (gate * (dxi_ref[0] + u)).astype(BF16)

    if seq:
        pl.when(part == 0)(lambda: add(ends[0]))
        pl.when(part == 1)(lambda: add(ends[1]))
    else:
        add(ends[0])

    @pl.when(part == pl.num_programs(0) - 1)
    def _():
        db_ref[0] = (gate * db_sc[...]).astype(BF16)
        dc_ref[0] = (gate * dc_sc[...]).astype(BF16)


def snake(count):
    return [
        COLS * y + (x if y % 2 == 0 else COLS - 1 - x)
        for y in range(count // COLS)
        for x in range(COLS)
    ]


def backwards(count):
    return list(range(count))[::-1]


def exchange(value, order):
    return lax.all_to_all(
        value, "context", 0, 0, axis_index_groups=[order(lax.axis_size("context"))]
    )


def sum_tensor(value):
    count = lax.axis_size("tensor")
    if count == 1:
        return value
    value = value + lax.ppermute(value, "tensor", [(i, i ^ 1) for i in range(count)])
    parts = [
        lax.ppermute(value, "tensor", [(i, (i + 2 * turn) % count) for i in range(count)])
        for turn in range(1, count // 2)
    ]
    return sum(parts, value)


def on_device(
    seq_inputs, b_proj, c_proj, dt_raw, dt_bias, a_log, d_skip, out_grad, log_ratio, lengths
):
    seqs, toks, width = seq_inputs.shape
    heads = dt_bias.shape[0]
    count = lax.axis_size("context")
    parts = width // LANES
    units = seqs * parts
    head_units = units - 1
    chunk = 2 * (LANES // PAIR) * (NS // count)
    spread_ones = jnp.asarray(spreads(heads), BF16)
    gather_ones = jnp.asarray(gathers(heads), BF16)
    bias_row, alog_row, gain_row = dt_bias[None], a_log[None], d_skip[None]
    smem = pl.BlockSpec(memory_space=pltpu.SMEM)
    anywhere = pl.BlockSpec(memory_space=pl.ANY)
    params = pltpu.CompilerParams(vmem_limit_bytes=VMEM)
    whole = lambda *shape: pl.BlockSpec(shape, lambda *at: (0,) * len(shape))
    small = [whole(1, heads), whole(1, heads)]

    of_either = lambda *shape: pl.BlockSpec(
        (1,) + shape, lambda i: (jnp.minimum(i, seqs - 1),) + (0,) * len(shape)
    )
    local = pl.pallas_call(
        states_kernel,
        grid=(seqs + 1,),
        in_specs=[
            smem, of_either(toks, width), of_either(toks, width), of_either(toks, NS),
            of_either(toks, NS), whole(*dt_raw.shape), *small, whole(*log_ratio.shape),
            whole(2, 128, width),
        ],
        out_specs=pl.BlockSpec((count, parts * chunk, PAIR), lambda i: (0, i, 0)),
        out_shape=jax.ShapeDtypeStruct((count, units * chunk + TILE, PAIR), F32),
        scratch_shapes=[pltpu.VMEM((seqs, toks, 128), BF16), pltpu.VMEM((TILE, 128), F32)],
        compiler_params=params,
        name="states",
    )(lengths, seq_inputs, out_grad, b_proj, c_proj, dt_raw, bias_row, alog_row, log_ratio,
      spread_ones)

    owned = exchange(local, backwards)

    def chained(unit, number):
        return pl.pallas_call(
            lambda *refs: chain_kernel(unit, heads, *refs),
            grid=(number,),
            in_specs=[
                pl.BlockSpec((count, TILE, PAIR), lambda i: (0, units * chunk // TILE, 0)),
                pl.BlockSpec((count, chunk, PAIR), lambda i: (0, i + unit, 0)),
                whole(2, 128, width),
            ],
            out_specs=[pl.BlockSpec((count, chunk, PAIR), lambda i: (0, i, 0)), whole(TILE, 128)],
            out_shape=[
                jax.ShapeDtypeStruct((count, number * chunk, PAIR), F32),
                jax.ShapeDtypeStruct((TILE, 128), F32),
            ],
            scratch_shapes=[pltpu.VMEM((seqs * heads // 2, count, PAIR), F32)],
            compiler_params=params,
            name="chain",
        )(owned, owned, spread_ones)

    most, sums = chained(0, head_units)
    most, dt_raw = lax.optimization_barrier((most, dt_raw))
    most = exchange(most, snake)

    tok_spec = lambda w: pl.BlockSpec((1, QB, w), lambda s, b: (s, b, 0))
    head_spec = pl.BlockSpec((1, heads, QB), lambda s, b: (s, 0, b))
    blocks = toks // QB
    dxi, dbi, dci, diff, col, skips, xv, gg, scal, near, aux = pl.pallas_call(
        intra_kernel,
        grid=(seqs, blocks),
        in_specs=[smem, tok_spec(width), tok_spec(width), tok_spec(NS), tok_spec(NS),
                  pl.BlockSpec((1, heads, toks), lambda s, b: (s, 0, 0)), *small, whole(1, heads),
                  whole(2, 128, width), whole(2, width, 128)],
        out_specs=[tok_spec(width), tok_spec(NS), tok_spec(NS), head_spec, head_spec,
                   pl.BlockSpec((1, 1, TILE, 128), lambda s, b: (s, b, 0, 0)),
                   tok_spec(width), tok_spec(width), tok_spec(128), tok_spec(128),
                   pl.BlockSpec((1, 3, heads, QB), lambda s, b: (s, 0, 0, b))],
        out_shape=[
            jax.ShapeDtypeStruct((seqs, toks, width), F32),
            jax.ShapeDtypeStruct((seqs, toks, NS), F32),
            jax.ShapeDtypeStruct((seqs, toks, NS), F32),
            jax.ShapeDtypeStruct((seqs, heads, toks), F32),
            jax.ShapeDtypeStruct((seqs, heads, toks), F32),
            jax.ShapeDtypeStruct((seqs, blocks, TILE, 128), F32),
            jax.ShapeDtypeStruct((seqs, toks, width), BF16),
            jax.ShapeDtypeStruct((seqs, toks, width), BF16),
            jax.ShapeDtypeStruct((seqs, toks, 128), BF16),
            jax.ShapeDtypeStruct((seqs, toks, 128), BF16),
            jax.ShapeDtypeStruct((seqs, 3, heads, toks), F32),
        ],
        scratch_shapes=[
            pltpu.VMEM((QB, width), F32), pltpu.VMEM((QB, width), F32),
            pltpu.VMEM((QB, width), BF16),
        ],
        compiler_params=params,
        name="intra",
    )(lengths, seq_inputs, out_grad, b_proj, c_proj, dt_raw, bias_row, alog_row, gain_row,
      spread_ones, gather_ones)

    of_seq = lambda *shape: pl.BlockSpec((1,) + shape, lambda i: (i,) + (0,) * len(shape))
    early = lambda w: pl.BlockSpec((1, QB, w), lambda i: (i, 0, 0))
    late = lambda w: pl.BlockSpec((1, QB, w), lambda i: (i, 1, 0))
    dlog, cols, dxi, dbi, dci = pl.pallas_call(
        cross_kernel,
        grid=(seqs,),
        in_specs=[smem, early(width), late(width), early(NS), late(NS), of_seq(toks, 128),
                  whole(2, 128, width), whole(2, width, 128), of_seq(heads, toks),
                  of_seq(heads, toks), early(width), early(NS), late(NS)],
        out_specs=[of_seq(heads, toks), of_seq(heads, toks), early(width), early(NS), late(NS)],
        out_shape=[
            jax.ShapeDtypeStruct((seqs, heads, toks), F32),
            jax.ShapeDtypeStruct((seqs, heads, toks), F32),
            jax.ShapeDtypeStruct((seqs, toks, width), F32),
            jax.ShapeDtypeStruct((seqs, toks, NS), F32),
            jax.ShapeDtypeStruct((seqs, toks, NS), F32),
        ],
        input_output_aliases={10: 2, 11: 3, 12: 4},
        compiler_params=params,
        name="cross",
    )(lengths, seq_inputs, out_grad, b_proj, c_proj, near, spread_ones, gather_ones, diff, col,
      dxi, dbi, dci)

    least, _ = chained(head_units, units - head_units)
    totals = sum_tensor(sums[2:4])[:, 0]
    signs = jnp.where(jnp.arange(2, dtype=jnp.int32) == 0, -1.0, 1.0).astype(F32)
    margin = -jnp.sum(signs * totals)
    gate = signs * BETA * jax.nn.sigmoid(-BETA * margin)
    least, gate, dxi = lax.optimization_barrier((least, gate, dxi))
    least = exchange(least, snake)

    def final(unit, number, back, *before):
        at_seq = lambda *shape: pl.BlockSpec(
            (1,) + shape, lambda i: ((i + unit) // parts,) + (0,) * len(shape)
        )
        laned = pl.BlockSpec(
            (1, toks, LANES), lambda i: ((i + unit) // parts, 0, (i + unit) % parts)
        )
        return pl.pallas_call(
            lambda *refs: final_kernel(unit, heads, *refs),
            grid=(number,),
            in_specs=[
                smem, smem, laned, laned, at_seq(toks, NS), at_seq(toks, NS),
                pl.BlockSpec((count, chunk, PAIR), lambda i: (0, i, 0)),
                at_seq(toks, 128), at_seq(3, heads, toks), at_seq(heads, toks),
                at_seq(heads, toks), at_seq(blocks, TILE, 128),
                pl.BlockSpec((2, 128, LANES), lambda i: (0, 0, (i + unit) % parts)),
                pl.BlockSpec((2, LANES, 128), lambda i: (0, (i + unit) % parts, 0)),
            ] + ([whole(1, TILE, 128), whole(toks, 128), whole(TILE, 128), anywhere] if before else []),
            out_specs=[at_seq(heads, toks), whole(count, TILE, 128), whole(toks, 128),
                       whole(TILE, 128)],
            out_shape=[
                jax.ShapeDtypeStruct((seqs, heads, toks), F32),
                jax.ShapeDtypeStruct((count, TILE, 128), F32),
                jax.ShapeDtypeStruct((toks, 128), F32),
                jax.ShapeDtypeStruct((TILE, 128), F32),
            ],
            scratch_shapes=[pltpu.VMEM((toks, 128), F32), pltpu.VMEM((TILE, 128), F32),
                            pltpu.VMEM((TILE, 128), F32)],
            input_output_aliases={17: 0} if before else {},
            compiler_params=params,
            name="final",
        )(lengths, gate, seq_inputs, out_grad, b_proj, c_proj, back, scal, aux, dlog, cols, skips,
          spread_ones, gather_ones, *before)

    def groups(seq, states, *before):
        of_seq = lambda *shape: pl.BlockSpec((1,) + shape, lambda p: (seq,) + (0,) * len(shape))
        laned = pl.BlockSpec((1, toks, LANES), lambda p: (seq, 0, p))
        if seq:
            last = pl.BlockSpec((count, chunk, PAIR), lambda p: (0, 0, 0))
            ends = [pl.BlockSpec((count, chunk, PAIR), lambda p: (0, head_units - 1, 0)), last]
        else:
            ends = [pl.BlockSpec((count, chunk, PAIR), lambda p: (0, p, 0))]
        return pl.pallas_call(
            lambda *refs: groups_kernel(seq, *refs),
            grid=(parts,),
            in_specs=[smem, of_seq(toks, NS), of_seq(toks, 128), laned, laned, laned,
                      of_seq(toks, NS), of_seq(toks, NS),
                      pl.BlockSpec((2, 128, LANES), lambda p: (0, 0, p))]
            + ends + [anywhere] * len(before),
            out_specs=[laned, of_seq(toks, NS), of_seq(toks, NS)],
            out_shape=[jax.ShapeDtypeStruct((seqs, toks, w), BF16) for w in (width, NS, NS)],
            scratch_shapes=[pltpu.VMEM((toks, NS), F32), pltpu.VMEM((toks, NS), F32)],
            input_output_aliases={9 + len(ends) + k: k for k in range(len(before))},
            compiler_params=params,
            name="groups",
        )(gate, b_proj, scal, xv, gg, dxi, dbi, dci, spread_ones, *states, *before)

    ddt, pars, some, thru = final(0, head_units, most)
    dx, db, dc = groups(0, (most,))
    least, dx, some = lax.optimization_barrier((least, dx, some))
    ddt, pars, _, _ = final(head_units, units - head_units, least, pars, some, thru, ddt)
    closing = exchange(pars, snake)
    dx, db, dc = groups(1, (most, least), dx, db, dc)
    sums = jnp.sum(closing, axis=0)[:3, :heads]
    return dx, db, dc, ddt, sums[0], sums[1], sums[2]


def solution(mesh):
    return jax.shard_map(
        on_device,
        mesh=mesh,
        in_specs=(
            P(None, "context", "tensor"),
            P(None, "context", "tensor"),
            P(None, "context", "tensor"),
            P(None, "tensor", "context"),
            P("tensor"),
            P("tensor"),
            P("tensor"),
            P(None, "context", "tensor"),
            P(None, ("context", "tensor")),
            P(),
        ),
        out_specs=(
            P(None, "context", "tensor"),
            P(None, "context", "tensor"),
            P(None, "context", "tensor"),
            P(None, "tensor", "context"),
            P("tensor"),
            P("tensor"),
            P("tensor"),
        ),
        check_vma=False,
    )
```

```python
import jax
import jax.numpy as jnp
import numpy as np
from jax import lax
from jax.experimental import pallas as pl
from jax.experimental.pallas import tpu as pltpu
from jax.sharding import PartitionSpec as P

HP = 64
NS = 256
QB = 256
HALF = 128
BETA = 0.5
PAIR = 2 * HP
LANES = 8 * HP
TILE = 8
COLS = 4
VMEM = 56 * 1024 * 1024
F32 = jnp.float32
BF16 = jnp.bfloat16
HIGH = lax.Precision.HIGHEST


def dot(lhs, rhs, dims, precision=None):
    return lax.dot_general(
        lhs, rhs, (dims, ((), ())), precision=precision, preferred_element_type=F32
    )


NN = ((1,), (0,))
NT = ((1,), (1,))
TN = ((0,), (0,))


def split3(value):
    top = value.astype(BF16)
    rest = value - top.astype(F32)
    mid = rest.astype(BF16)
    return top, mid, (rest - mid.astype(F32)).astype(BF16)


def softplus(value):
    return jnp.maximum(value, 0.0) + jnp.log1p(jnp.exp(-jnp.abs(value)))


def upper_ones():
    row = lax.broadcasted_iota(jnp.int32, (QB, QB), 0)
    col = lax.broadcasted_iota(jnp.int32, (QB, QB), 1)
    return (row <= col).astype(BF16)


def running_sum(values, ones, dims=NN):
    rows = values.shape[0]
    sums = dot(jnp.concatenate(split3(values), axis=0), ones, dims)
    return sums[:rows] + sums[rows : 2 * rows] + sums[2 * rows :]


def live_rows(base, length, count):
    row = lax.broadcasted_iota(jnp.int32, (count, 1), 0)
    return base + row < length


def column(row_ref):
    heads = row_ref.shape[1]
    same = lax.broadcasted_iota(jnp.int32, (heads, heads), 0) == lax.broadcasted_iota(
        jnp.int32, (heads, heads), 1
    )
    return jnp.sum(jnp.where(same, row_ref[...], 0.0), axis=1, keepdims=True)


def token_base(toks):
    return lax.axis_index("context") * toks


def flat(column_values, lanes):
    heads = column_values.shape[0]
    same = lax.broadcasted_iota(jnp.int32, (heads, lanes), 0) == lax.broadcasted_iota(
        jnp.int32, (heads, lanes), 1
    )
    return jnp.sum(jnp.where(same, column_values, 0.0), axis=0, keepdims=True)


GAP = 32


def scale_columns(tail, grow):
    rows = jnp.concatenate([tail, grow], axis=0)
    parts = [part.astype(F32) for part in split3(rows)]
    return jnp.concatenate(parts + [jnp.zeros_like(rows)], axis=0).T.astype(BF16)


def spreads(heads):
    row, lane = np.arange(128)[:, None], np.arange(heads * HP)[None, :] // HP
    used = row < 3 * GAP
    return np.stack([used & (row % GAP == lane), used & (row % GAP == lane + GAP // 2)])


def gathers(heads):
    lane, col = np.arange(heads * HP)[:, None] // HP, np.arange(128)[None, :]
    return np.stack([lane == col, lane == col - GAP // 2])


def lane_sums(product, ones_part):
    top = product.astype(BF16)
    low = (product - top.astype(F32)).astype(BF16)
    return dot(top, ones_part, NN) + dot(low, ones_part, NN)


def exact_dot(lhs, rhs, dims):
    top = rhs.astype(BF16)
    low = (rhs - top.astype(F32)).astype(BF16)
    return dot(lhs, top, dims) + dot(lhs, low, dims)


def device_sums(step, rate, ones):
    logs = step * rate
    heads = step.shape[0]
    both = running_sum(jnp.concatenate([logs[:, :QB], logs[:, QB:]], axis=0), ones)
    return both[:heads], both[heads:]


def states_kernel(len_ref, x_ref, g_ref, b_ref, c_ref, dt_ref, bias_ref, alog_ref, ratio_ref,
                  spread_ref, out_ref, scal_sc, tile_sc):
    heads = dt_ref.shape[1]
    toks = x_ref.shape[1]
    pieces = out_ref.shape[0]
    piece = NS // pieces
    at = pl.program_id(0)
    work = 2

    @pl.when(at == 0)
    def _():
        ones = upper_ones()
        bias, rate = column(bias_ref), -jnp.exp(column(alog_ref))
        for seq in range(2):
            step = softplus(dt_ref[seq] + bias)
            cums = device_sums(step, rate, ones)
            mid = cums[0][:, QB - 1 : QB]
            last = mid + cums[1][:, QB - 1 : QB]
            for blk in range(2):
                rows = slice(blk * QB, (blk + 1) * QB)
                cum = cums[blk] + blk * mid
                scal_sc[seq, rows] = scale_columns(jnp.exp(last - cum) * step[:, rows], jnp.exp(cum))
            tile_sc[seq : seq + 1] = flat(jnp.exp(last), 128)

    @pl.when(at < work)
    def _():
        scal = scal_sc[at]
        x_tail = x_ref[0].astype(F32) * dot(scal, spread_ref[0], NN)
        live = live_rows(token_base(toks), len_ref[at], toks)
        g_grow = jnp.where(live, g_ref[0].astype(F32) * dot(scal, spread_ref[1], NN), 0.0)
        whole = (exact_dot(b_ref[0].T, x_tail, NN), exact_dot(c_ref[0].T, g_grow, NN))
        for scan in range(2):
            for pair in range(heads // 2):
                row = (2 * pair + scan) * piece
                out_ref[:, row : row + piece] = whole[scan][:, pair * PAIR : (pair + 1) * PAIR].reshape(
                    pieces, piece, PAIR
                )

    @pl.when(at == work)
    def _():
        ratio = ratio_ref[...]
        rows = ratio.shape[1]
        first = lax.axis_index(("context", "tensor")) * rows
        place = lax.broadcasted_iota(jnp.int32, ratio.shape, 1) + first
        seq = lax.broadcasted_iota(jnp.int32, ratio.shape, 0)
        length = jnp.where(seq == 0, len_ref[0], len_ref[1])
        totals = jnp.sum(jnp.where(place < length, ratio, 0.0), axis=1, keepdims=True)
        tile_sc[2:4] = jnp.broadcast_to(totals, (2, 128))
        tile_sc[4:] = jnp.zeros((TILE - 4, 128), F32)
        out_ref[:, 0:TILE] = jnp.broadcast_to(tile_sc[...][None], (pieces, TILE, 128))


def chain_kernel(unit, heads, tile_ref, in_ref, spread_ref, out_ref, sums_ref, decay_sc):
    count = in_ref.shape[0]
    piece = NS // count
    parts = heads * HP // LANES
    at = pl.program_id(0) + unit
    part = lax.rem(at, parts)

    @pl.when(pl.program_id(0) == 0)
    def _():
        tiles = [tile_ref[src] for src in range(count)]
        sums_ref[...] = sum(tiles[1:], tiles[0])
        decay = jnp.concatenate(
            [tile[seq : seq + 1] for seq in range(2) for tile in tiles], axis=0
        )
        top, mid, low = [split.astype(F32) for split in split3(decay)]
        columns = top + pltpu.roll(mid, GAP, 1) + pltpu.roll(low, 2 * GAP, 1)
        wide = dot(columns.astype(BF16), spread_ref[0], NN)
        for seq in range(2):
            for pair in range(heads // 2):
                decay_sc[seq * (heads // 2) + pair] = wide[
                    seq * count : (seq + 1) * count, pair * PAIR : (pair + 1) * PAIR
                ]

    order = np.argsort(snake(count)).tolist()
    pairs = LANES // PAIR
    for pair in range(pairs):
        decay = decay_sc[lax.div(at, parts) * (heads // 2) + part * pairs + pair]
        rows = slice(2 * pair * piece, (2 * pair + 1) * piece)
        total = jnp.zeros((piece, PAIR), F32)
        for src in order:
            out_ref[src, rows] = total
            total = decay[src : src + 1] * total + in_ref[src, rows]
        rows = slice((2 * pair + 1) * piece, (2 * pair + 2) * piece)
        total = jnp.zeros((piece, PAIR), F32)
        for src in reversed(order):
            out_ref[src, rows] = total
            total = decay[src : src + 1] * total + in_ref[src, rows]


def intra_kernel(len_ref, x_ref, g_ref, b_ref, c_ref, dt_ref, bias_ref, alog_ref, gain_ref, spread_ref,
                 gather_ref, dx_ref, db_ref, dc_ref, diff_ref, col_ref, skip_ref, xv_ref, gg_ref, scal_ref, near_ref, aux_ref,
                 y_sc, d_sc, g_sc):
    heads = dt_ref.shape[1]
    seq, blk = pl.program_id(0), pl.program_id(1)
    raw = dt_ref[0] + column(bias_ref)
    step_all = softplus(raw)
    rate = -jnp.exp(column(alog_ref))
    cums = device_sums(step_all, rate, upper_ones())
    first = blk == 0
    cum = jnp.where(first, cums[0], cums[1])
    step = jnp.where(first, step_all[:, :QB], step_all[:, QB:])
    raw = jnp.where(first, raw[:, :QB], raw[:, QB:])
    cum_t = cum.T
    mid, over = cums[0][:, QB - 1 : QB], cums[1][:, QB - 1 : QB]
    slope = jax.nn.sigmoid(raw)
    aux_ref[0, 0] = slope / step
    aux_ref[0, 1] = slope * rate
    aux_ref[0, 2] = step * rate
    tail = jnp.exp(cum[:, QB - 1 : QB] - cum) * step
    grow = jnp.exp(cum)
    near_ref[0] = scale_columns(tail, grow)
    gain = jnp.broadcast_to(column(gain_ref), (heads, TILE))
    gain = dot(scale_columns(gain, gain), spread_ref[0], NN)[0:1]
    tail = jnp.exp(jnp.where(first, mid + over, over) - cum) * step
    grow = jnp.exp(cum + jnp.where(first, 0.0, mid))
    scal = scale_columns(tail, grow)
    scal_ref[0] = scal
    live = live_rows(token_base(pl.num_programs(1) * QB) + blk * QB, len_ref[seq], QB)
    x_full = x_ref[0].astype(F32)
    g_full = jnp.where(live, g_ref[0].astype(F32), 0.0)
    g_sc[...] = g_full.astype(BF16)
    skips = jnp.sum(x_full * g_full, axis=0, keepdims=True)
    skip_ref[0, 0] = lane_sums(jnp.broadcast_to(skips, (TILE, heads * HP)), gather_ref[0])
    xv_ref[0] = (x_full * dot(scal, spread_ref[0], NN)).astype(BF16)
    gg_ref[0] = (g_full * dot(scal, spread_ref[1], NN)).astype(BF16)
    gram = dot(c_ref[0], b_ref[0], NT)
    causal = (
        lax.broadcasted_iota(jnp.int32, (HALF, HALF), 0)
        >= lax.broadcasted_iota(jnp.int32, (HALF, HALF), 1)
    )
    low, high = slice(0, HALF), slice(HALF, QB)
    tiles = ((low, low), (high, low), (high, high))
    grams = [jnp.where(causal, gram[t, k], 0.0) if t is k else gram[t, k] for t, k in tiles]
    left = lax.broadcasted_iota(jnp.int32, (QB, PAIR), 1) < HP
    zero = jnp.zeros((QB, PAIR), BF16)
    dgrams = [jnp.zeros((HALF, HALF), F32) for _ in tiles]
    for pair in range(heads // 2):
        lanes = slice(pair * PAIR, (pair + 1) * PAIR)
        xx = x_ref[0, :, lanes]
        gg = g_sc[:, lanes]
        gs = [jnp.where(left, gg, zero), jnp.where(left, zero, gg)]
        xs = [jnp.where(left, xx, zero), jnp.where(left, zero, xx)]
        weights = []
        for one in range(2):
            head = 2 * pair + one
            mine = []
            dlow = dot(gs[one], xx[low], NT)
            dhigh = dot(gs[one][high], xx[high], NT)
            dparts = (dlow[low], dlow[high], dhigh)
            for which, (t, k) in enumerate(tiles):
                gap = cum_t[t, head : head + 1] - cum[head : head + 1, k]
                if t is k:
                    gap = jnp.minimum(gap, 0.0)
                decay = jnp.exp(gap) * step[head : head + 1, k]
                mine.append((grams[which] * decay).astype(BF16))
                dgrams[which] = dgrams[which] + dparts[which] * decay
            weights.append(mine)
        (a0, a1, a2), (b0, b1, b2) = weights
        y_sc[low, lanes] = dot(
            jnp.concatenate([a0, b0], axis=1), jnp.concatenate([xs[0][low], xs[1][low]], axis=0), NN
        )
        y_sc[high, lanes] = dot(
            jnp.concatenate([a1, a2, b1, b2], axis=1), jnp.concatenate(xs, axis=0), NN
        )
        d_sc[low, lanes] = dot(
            jnp.concatenate([a0, a1, b0, b1], axis=0), jnp.concatenate(gs, axis=0), TN
        )
        d_sc[high, lanes] = dot(
            jnp.concatenate([a2, b2], axis=0),
            jnp.concatenate([gs[0][high], gs[1][high]], axis=0), TN,
        )
    sums = lane_sums(g_full * y_sc[...], gather_ref[0])
    sums = (sums + lane_sums(x_full * d_sc[...], gather_ref[1])).T
    row, col = sums[:heads], sums[heads : 2 * heads]
    diff_ref[0] = row - col
    col_ref[0] = col
    dx_ref[0] = d_sc[...] + gain * g_full
    dgram = jnp.concatenate(
        [
            jnp.concatenate(
                [jnp.where(causal, dgrams[0], 0.0), jnp.zeros((HALF, HALF), F32)], axis=1
            ),
            jnp.concatenate([dgrams[1], jnp.where(causal, dgrams[2], 0.0)], axis=1),
        ],
        axis=0,
    ).astype(BF16)
    dc_ref[0] = dot(dgram, b_ref[0], NN)
    db_ref[0] = dot(dgram, c_ref[0], TN)


def cross_kernel(len_ref, x_ref, g_ref, b_ref, c_ref, near_ref, spread_ref, gather_ref,
                 diff_ref, col_ref, dxi_ref, dbi_ref, dci_ref,
                 dlog_ref, cols_ref, dx_ref, db_ref, dc_ref):
    heads = diff_ref.shape[1]
    seq = pl.program_id(0)
    toks = near_ref.shape[1]
    x_tail = x_ref[0].astype(F32) * dot(near_ref[0, :QB], spread_ref[0], NN)
    live = live_rows(token_base(toks) + QB, len_ref[seq], QB)
    g_grow = jnp.where(live, g_ref[0].astype(F32), 0.0) * dot(near_ref[0, QB:], spread_ref[1], NN)
    early, late = x_tail.astype(BF16), g_grow.astype(BF16)
    b_early, c_late = b_ref[0], c_ref[0]
    gram = dot(c_late, b_early, NT)
    top, low, _ = split3(gram)
    y = exact_dot(top, x_tail, NN) + dot(low, early, NN)
    back = exact_dot(top, g_grow, TN) + dot(low, late, TN)
    dgram = dot(late, early, NT).astype(BF16)
    dc_ref[0] = dci_ref[0] + dot(dgram, b_early, NN)
    db_ref[0] = dbi_ref[0] + dot(dgram, c_late, TN)
    dx_ref[0] = dxi_ref[0] + dot(near_ref[0, :QB], spread_ref[0], NN) * back
    row = lane_sums(g_grow * y, gather_ref[0]).T[:heads]
    col = lane_sums(x_tail * back, gather_ref[0]).T[:heads]
    ones = upper_ones()
    dlog_ref[0, :, :QB] = (
        running_sum(diff_ref[0, :, :QB], ones, NT) + running_sum(col, ones) - col
    )
    dlog_ref[0, :, QB:] = running_sum(diff_ref[0, :, QB:] + row, ones, NT)
    cols_ref[0, :, :QB] = col_ref[0, :, :QB] + col
    cols_ref[0, :, QB:] = col_ref[0, :, QB:]


def state_of(ends_ref, scan):
    piece = NS // ends_ref.shape[0]
    pairs = ends_ref.shape[1] // (2 * piece)
    return jnp.concatenate(
        [
            ends_ref[:, (2 * p + scan) * piece : (2 * p + scan + 1) * piece].reshape(NS, PAIR)
            for p in range(pairs)
        ],
        axis=1,
    )


def final_kernel(unit, heads, len_ref, gate_ref, x_ref, g_ref, b_ref, c_ref, ends_ref, scal_ref,
                 aux_ref, dlog_ref, cols_ref, skip_ref, spread_ref, gather_ref, *refs):
    ddt_ref, par_ref, part_ref, thru_ref, sum_sc, thru_sc, tile_sc = refs[-7:]
    before = refs[:-7]
    toks = x_ref.shape[1]
    parts = heads * HP // LANES
    at = pl.program_id(0) + unit
    seq, part = lax.div(at, parts), lax.rem(at, parts)
    gate = gate_ref[seq]

    @pl.when(pl.program_id(0) == 0)
    def _():
        tile_sc[...] = before[0][0] if before else jnp.zeros_like(tile_sc)
        if before:
            sum_sc[...] = before[1][...]
            thru_sc[...] = before[2][...]

    @pl.when(part == 0)
    def _():
        sum_sc[...] = jnp.zeros_like(sum_sc)
        thru_sc[...] = jnp.zeros_like(thru_sc)

    enter, leave = state_of(ends_ref, 0), state_of(ends_ref, 1)
    live = live_rows(token_base(toks), len_ref[seq], toks)
    grow = dot(scal_ref[0], spread_ref[1], NN)
    g_grow = jnp.where(live, g_ref[0].astype(F32) * grow, 0.0)
    y = exact_dot(c_ref[0], enter, NN)
    tail = dot(scal_ref[0], spread_ref[0], NN)
    u = tail * exact_dot(b_ref[0], leave, NN)
    sum_sc[...] += lane_sums(g_grow * y, gather_ref[0]) + lane_sums(
        x_ref[0].astype(F32) * u, gather_ref[1]
    )
    product = grow[toks - 1 : toks] * jnp.sum(enter * leave, axis=0, keepdims=True)
    thru_sc[...] += lane_sums(jnp.broadcast_to(product, (TILE, LANES)), gather_ref[0])

    @pl.when(part == parts - 1)
    def _():
        ones = upper_ones()
        halves = [slice(blk * QB, (blk + 1) * QB) for blk in range(2)]
        sums = [sum_sc[rows].T for rows in halves]
        both = jnp.concatenate([half[:heads] for half in sums], axis=0)
        cols = jnp.concatenate([half[heads : 2 * heads] for half in sums], axis=0)
        later = running_sum(both, ones, NT)
        earlier = running_sum(cols, ones)
        thru = thru_sc[...].T[:heads, 0:1]
        rest = (
            later[heads:, 0:1] + thru,
            earlier[:heads, QB - 1 : QB] + thru,
        )
        gb = jnp.zeros((heads, 1), F32)
        ga = jnp.zeros((heads, 1), F32)
        for blk, rows in enumerate(halves):
            mine = slice(blk * heads, (blk + 1) * heads)
            dlog = dlog_ref[0, :, rows] + later[mine] + earlier[mine] - cols[mine] + rest[blk]
            col = cols_ref[0, :, rows] + cols[mine]
            ddt = gate * (aux_ref[0, 0, :, rows] * col + aux_ref[0, 1, :, rows] * dlog)
            ddt_ref[0, :, rows] = ddt
            gb = gb + jnp.sum(ddt, axis=1, keepdims=True)
            ga = ga + gate * jnp.sum(aux_ref[0, 2, :, rows] * dlog, axis=1, keepdims=True)
        skips = gate * (skip_ref[0, 0] + skip_ref[0, 1])
        rows = [flat(ga, 128), flat(gb, 128), skips[0:1]]
        tile_sc[...] += jnp.concatenate(rows + [jnp.zeros((TILE - 3, 128), F32)], axis=0)

    @pl.when(pl.program_id(0) == pl.num_programs(0) - 1)
    def _():
        par_ref[...] = jnp.broadcast_to(tile_sc[...][None], par_ref.shape)
        part_ref[...] = sum_sc[...]
        thru_ref[...] = thru_sc[...]


def groups_kernel(seq, gate_ref, b_ref, scal_ref, xv_ref, gg_ref, dxi_ref, dbi_ref, dci_ref,
                  spread_ref, *refs):
    dx_ref, db_ref, dc_ref, db_sc, dc_sc = refs[-5:]
    ends = refs[:2] if seq else refs[:1]
    part = pl.program_id(0)
    gate = gate_ref[seq]

    @pl.when(part == 0)
    def _():
        db_sc[...] = dbi_ref[0]
        dc_sc[...] = dci_ref[0]

    def add(ends_ref):
        enter = state_of(ends_ref, 0).astype(BF16)
        leave = state_of(ends_ref, 1).astype(BF16)
        db_sc[...] += dot(xv_ref[0], leave, NT)
        dc_sc[...] += dot(gg_ref[0], enter, NT)
        u = dot(scal_ref[0], spread_ref[0], NN) * dot(b_ref[0], leave, NN)
        dx_ref[0] = (gate * (dxi_ref[0] + u)).astype(BF16)

    if seq:
        pl.when(part == 0)(lambda: add(ends[0]))
        pl.when(part == 1)(lambda: add(ends[1]))
    else:
        add(ends[0])

    @pl.when(part == pl.num_programs(0) - 1)
    def _():
        db_ref[0] = (gate * db_sc[...]).astype(BF16)
        dc_ref[0] = (gate * dc_sc[...]).astype(BF16)


def snake(count):
    return [
        COLS * y + (x if y % 2 == 0 else COLS - 1 - x)
        for y in range(count // COLS)
        for x in range(COLS)
    ]


def exchange(value):
    order = snake(lax.axis_size("context"))
    return lax.all_to_all(value, "context", 0, 0, axis_index_groups=[order])


def sum_tensor(value):
    count = lax.axis_size("tensor")
    if count == 1:
        return value
    value = value + lax.ppermute(value, "tensor", [(i, i ^ 1) for i in range(count)])
    parts = [
        lax.ppermute(value, "tensor", [(i, (i + 2 * turn) % count) for i in range(count)])
        for turn in range(1, count // 2)
    ]
    return sum(parts, value)


def on_device(
    seq_inputs, b_proj, c_proj, dt_raw, dt_bias, a_log, d_skip, out_grad, log_ratio, lengths
):
    seqs, toks, width = seq_inputs.shape
    heads = dt_bias.shape[0]
    count = lax.axis_size("context")
    parts = width // LANES
    units = seqs * parts
    head_units = units - 1
    chunk = 2 * (LANES // PAIR) * (NS // count)
    spread_ones = jnp.asarray(spreads(heads), BF16)
    gather_ones = jnp.asarray(gathers(heads), BF16)
    bias_row, alog_row, gain_row = dt_bias[None], a_log[None], d_skip[None]
    smem = pl.BlockSpec(memory_space=pltpu.SMEM)
    anywhere = pl.BlockSpec(memory_space=pl.ANY)
    params = pltpu.CompilerParams(vmem_limit_bytes=VMEM)
    whole = lambda *shape: pl.BlockSpec(shape, lambda *at: (0,) * len(shape))
    small = [whole(1, heads), whole(1, heads)]

    of_either = lambda *shape: pl.BlockSpec(
        (1,) + shape, lambda i: (jnp.minimum(i, seqs - 1),) + (0,) * len(shape)
    )
    local = pl.pallas_call(
        states_kernel,
        grid=(seqs + 1,),
        in_specs=[
            smem, of_either(toks, width), of_either(toks, width), of_either(toks, NS),
            of_either(toks, NS), whole(*dt_raw.shape), *small, whole(*log_ratio.shape),
            whole(2, 128, width),
        ],
        out_specs=pl.BlockSpec((count, parts * chunk, PAIR), lambda i: (0, i, 0)),
        out_shape=jax.ShapeDtypeStruct((count, units * chunk + TILE, PAIR), F32),
        scratch_shapes=[pltpu.VMEM((seqs, toks, 128), BF16), pltpu.VMEM((TILE, 128), F32)],
        compiler_params=params,
        name="states",
    )(lengths, seq_inputs, out_grad, b_proj, c_proj, dt_raw, bias_row, alog_row, log_ratio,
      spread_ones)

    owned = exchange(local)

    def chained(unit, number):
        return pl.pallas_call(
            lambda *refs: chain_kernel(unit, heads, *refs),
            grid=(number,),
            in_specs=[
                pl.BlockSpec((count, TILE, PAIR), lambda i: (0, units * chunk // TILE, 0)),
                pl.BlockSpec((count, chunk, PAIR), lambda i: (0, i + unit, 0)),
                whole(2, 128, width),
            ],
            out_specs=[pl.BlockSpec((count, chunk, PAIR), lambda i: (0, i, 0)), whole(TILE, 128)],
            out_shape=[
                jax.ShapeDtypeStruct((count, number * chunk, PAIR), F32),
                jax.ShapeDtypeStruct((TILE, 128), F32),
            ],
            scratch_shapes=[pltpu.VMEM((seqs * heads // 2, count, PAIR), F32)],
            compiler_params=params,
            name="chain",
        )(owned, owned, spread_ones)

    most, sums = chained(0, head_units)
    most, dt_raw = lax.optimization_barrier((most, dt_raw))
    most = exchange(most)

    tok_spec = lambda w: pl.BlockSpec((1, QB, w), lambda s, b: (s, b, 0))
    head_spec = pl.BlockSpec((1, heads, QB), lambda s, b: (s, 0, b))
    blocks = toks // QB
    dxi, dbi, dci, diff, col, skips, xv, gg, scal, near, aux = pl.pallas_call(
        intra_kernel,
        grid=(seqs, blocks),
        in_specs=[smem, tok_spec(width), tok_spec(width), tok_spec(NS), tok_spec(NS),
                  pl.BlockSpec((1, heads, toks), lambda s, b: (s, 0, 0)), *small, whole(1, heads),
                  whole(2, 128, width), whole(2, width, 128)],
        out_specs=[tok_spec(width), tok_spec(NS), tok_spec(NS), head_spec, head_spec,
                   pl.BlockSpec((1, 1, TILE, 128), lambda s, b: (s, b, 0, 0)),
                   tok_spec(width), tok_spec(width), tok_spec(128), tok_spec(128),
                   pl.BlockSpec((1, 3, heads, QB), lambda s, b: (s, 0, 0, b))],
        out_shape=[
            jax.ShapeDtypeStruct((seqs, toks, width), F32),
            jax.ShapeDtypeStruct((seqs, toks, NS), F32),
            jax.ShapeDtypeStruct((seqs, toks, NS), F32),
            jax.ShapeDtypeStruct((seqs, heads, toks), F32),
            jax.ShapeDtypeStruct((seqs, heads, toks), F32),
            jax.ShapeDtypeStruct((seqs, blocks, TILE, 128), F32),
            jax.ShapeDtypeStruct((seqs, toks, width), BF16),
            jax.ShapeDtypeStruct((seqs, toks, width), BF16),
            jax.ShapeDtypeStruct((seqs, toks, 128), BF16),
            jax.ShapeDtypeStruct((seqs, toks, 128), BF16),
            jax.ShapeDtypeStruct((seqs, 3, heads, toks), F32),
        ],
        scratch_shapes=[
            pltpu.VMEM((QB, width), F32), pltpu.VMEM((QB, width), F32),
            pltpu.VMEM((QB, width), BF16),
        ],
        compiler_params=params,
        name="intra",
    )(lengths, seq_inputs, out_grad, b_proj, c_proj, dt_raw, bias_row, alog_row, gain_row,
      spread_ones, gather_ones)

    of_seq = lambda *shape: pl.BlockSpec((1,) + shape, lambda i: (i,) + (0,) * len(shape))
    early = lambda w: pl.BlockSpec((1, QB, w), lambda i: (i, 0, 0))
    late = lambda w: pl.BlockSpec((1, QB, w), lambda i: (i, 1, 0))
    dlog, cols, dxi, dbi, dci = pl.pallas_call(
        cross_kernel,
        grid=(seqs,),
        in_specs=[smem, early(width), late(width), early(NS), late(NS), of_seq(toks, 128),
                  whole(2, 128, width), whole(2, width, 128), of_seq(heads, toks),
                  of_seq(heads, toks), early(width), early(NS), late(NS)],
        out_specs=[of_seq(heads, toks), of_seq(heads, toks), early(width), early(NS), late(NS)],
        out_shape=[
            jax.ShapeDtypeStruct((seqs, heads, toks), F32),
            jax.ShapeDtypeStruct((seqs, heads, toks), F32),
            jax.ShapeDtypeStruct((seqs, toks, width), F32),
            jax.ShapeDtypeStruct((seqs, toks, NS), F32),
            jax.ShapeDtypeStruct((seqs, toks, NS), F32),
        ],
        input_output_aliases={10: 2, 11: 3, 12: 4},
        compiler_params=params,
        name="cross",
    )(lengths, seq_inputs, out_grad, b_proj, c_proj, near, spread_ones, gather_ones, diff, col,
      dxi, dbi, dci)

    least, _ = chained(head_units, units - head_units)
    totals = sum_tensor(sums[2:4])[:, 0]
    signs = jnp.where(jnp.arange(2, dtype=jnp.int32) == 0, -1.0, 1.0).astype(F32)
    margin = -jnp.sum(signs * totals)
    gate = signs * BETA * jax.nn.sigmoid(-BETA * margin)
    least, gate, dxi = lax.optimization_barrier((least, gate, dxi))
    least = exchange(least)

    def final(unit, number, back, *before):
        at_seq = lambda *shape: pl.BlockSpec(
            (1,) + shape, lambda i: ((i + unit) // parts,) + (0,) * len(shape)
        )
        laned = pl.BlockSpec(
            (1, toks, LANES), lambda i: ((i + unit) // parts, 0, (i + unit) % parts)
        )
        return pl.pallas_call(
            lambda *refs: final_kernel(unit, heads, *refs),
            grid=(number,),
            in_specs=[
                smem, smem, laned, laned, at_seq(toks, NS), at_seq(toks, NS),
                pl.BlockSpec((count, chunk, PAIR), lambda i: (0, i, 0)),
                at_seq(toks, 128), at_seq(3, heads, toks), at_seq(heads, toks),
                at_seq(heads, toks), at_seq(blocks, TILE, 128),
                pl.BlockSpec((2, 128, LANES), lambda i: (0, 0, (i + unit) % parts)),
                pl.BlockSpec((2, LANES, 128), lambda i: (0, (i + unit) % parts, 0)),
            ] + ([whole(1, TILE, 128), whole(toks, 128), whole(TILE, 128), anywhere] if before else []),
            out_specs=[at_seq(heads, toks), whole(count, TILE, 128), whole(toks, 128),
                       whole(TILE, 128)],
            out_shape=[
                jax.ShapeDtypeStruct((seqs, heads, toks), F32),
                jax.ShapeDtypeStruct((count, TILE, 128), F32),
                jax.ShapeDtypeStruct((toks, 128), F32),
                jax.ShapeDtypeStruct((TILE, 128), F32),
            ],
            scratch_shapes=[pltpu.VMEM((toks, 128), F32), pltpu.VMEM((TILE, 128), F32),
                            pltpu.VMEM((TILE, 128), F32)],
            input_output_aliases={17: 0} if before else {},
            compiler_params=params,
            name="final",
        )(lengths, gate, seq_inputs, out_grad, b_proj, c_proj, back, scal, aux, dlog, cols, skips,
          spread_ones, gather_ones, *before)

    def groups(seq, states, *before):
        of_seq = lambda *shape: pl.BlockSpec((1,) + shape, lambda p: (seq,) + (0,) * len(shape))
        laned = pl.BlockSpec((1, toks, LANES), lambda p: (seq, 0, p))
        if seq:
            last = pl.BlockSpec((count, chunk, PAIR), lambda p: (0, 0, 0))
            ends = [pl.BlockSpec((count, chunk, PAIR), lambda p: (0, head_units - 1, 0)), last]
        else:
            ends = [pl.BlockSpec((count, chunk, PAIR), lambda p: (0, p, 0))]
        return pl.pallas_call(
            lambda *refs: groups_kernel(seq, *refs),
            grid=(parts,),
            in_specs=[smem, of_seq(toks, NS), of_seq(toks, 128), laned, laned, laned,
                      of_seq(toks, NS), of_seq(toks, NS),
                      pl.BlockSpec((2, 128, LANES), lambda p: (0, 0, p))]
            + ends + [anywhere] * len(before),
            out_specs=[laned, of_seq(toks, NS), of_seq(toks, NS)],
            out_shape=[jax.ShapeDtypeStruct((seqs, toks, w), BF16) for w in (width, NS, NS)],
            scratch_shapes=[pltpu.VMEM((toks, NS), F32), pltpu.VMEM((toks, NS), F32)],
            input_output_aliases={9 + len(ends) + k: k for k in range(len(before))},
            compiler_params=params,
            name="groups",
        )(gate, b_proj, scal, xv, gg, dxi, dbi, dci, spread_ones, *states, *before)

    ddt, pars, some, thru = final(0, head_units, most)
    dx, db, dc = groups(0, (most,))
    least, dx, some = lax.optimization_barrier((least, dx, some))
    ddt, pars, _, _ = final(head_units, units - head_units, least, pars, some, thru, ddt)
    closing = exchange(pars)
    dx, db, dc = groups(1, (most, least), dx, db, dc)
    sums = jnp.sum(closing, axis=0)[:3, :heads]
    return dx, db, dc, ddt, sums[0], sums[1], sums[2]


def solution(mesh):
    return jax.shard_map(
        on_device,
        mesh=mesh,
        in_specs=(
            P(None, "context", "tensor"),
            P(None, "context", "tensor"),
            P(None, "context", "tensor"),
            P(None, "tensor", "context"),
            P("tensor"),
            P("tensor"),
            P("tensor"),
            P(None, "context", "tensor"),
            P(None, ("context", "tensor")),
            P(),
        ),
        out_specs=(
            P(None, "context", "tensor"),
            P(None, "context", "tensor"),
            P(None, "context", "tensor"),
            P(None, "tensor", "context"),
            P("tensor"),
            P("tensor"),
            P("tensor"),
        ),
        check_vma=False,
    )
```
